32 devices in a mesh: dp: 8 (over z, y), tensor: 4 (over x, core).
Axes of the slice: x: 2, y: 2, z: 4, core: 2. Of those that a mesh axis runs over, the one named last changes fastest.
Arguments:
- tokens: bfloat16 [24576, 2048], P(('dp', 'tensor')), may hold values from -6 to 6
- cotangent: bfloat16 [24576, 2048], P(('dp', 'tensor'))
- doc_lengths: int32 [8, 4], P('dp'), may hold values from 1 to 1536, 3072 in all within a row
- mix_in: float32 [3, 2048, 2048], P(None, 'dp', 'tensor')
- mix_out: float32 [2048, 2048], P('tensor', 'dp')
- ffn_in: float32 [2, 2048, 5632], P(None, 'dp', 'tensor')
- ffn_out: float32 [5632, 2048], P('tensor', 'dp')
- gains: float32 [2, 2048], replicated, may hold values from 0.5 to 1.5
- mix_in_m: float32 [3, 2048, 2048], P(None, 'dp', 'tensor'), may hold values from -20 to 20
- mix_out_m: float32 [2048, 2048], P('tensor', 'dp'), may hold values from -40 to 40
- ffn_in_m: float32 [2, 2048, 5632], P(None, 'dp', 'tensor'), may hold values from -56 to 56
- ffn_out_m: float32 [5632, 2048], P('tensor', 'dp'), may hold values from -64 to 64
- gains_m: float32 [2, 2048], replicated, may hold values from -112 to 112
- mix_in_v: float32 [3, 2048, 2048], P(None, 'dp', 'tensor'), may hold values from 0.98304 to 3.93216
- mix_out_v: float32 [2048, 2048], P('tensor', 'dp'), may hold values from 3.93216 to 15.72864
- ffn_in_v: float32 [2, 2048, 5632], P(None, 'dp', 'tensor'), may hold values from 6.144 to 24.576
- ffn_out_v: float32 [5632, 2048], P('tensor', 'dp'), may hold values from 8.84736 to 35.38944
- gains_v: float32 [2, 2048], replicated, may hold values from 24.576 to 98.304
Outputs:
- mixed: bfloat16 [24576, 2048], P(('dp', 'tensor'))
- input_grad: float32 [24576, 2048], P(('dp', 'tensor'))
- mix_in_next: float32 [3, 2048, 2048], P(None, 'dp', 'tensor')
- mix_out_next: float32 [2048, 2048], P('tensor', 'dp')
- ffn_in_next: float32 [2, 2048, 5632], P(None, 'dp', 'tensor')
- ffn_out_next: float32 [5632, 2048], P('tensor', 'dp')
- gains_next: float32 [2, 2048], replicated
- mix_in_m_next: float32 [3, 2048, 2048], P(None, 'dp', 'tensor')
- mix_out_m_next: float32 [2048, 2048], P('tensor', 'dp')
- ffn_in_m_next: float32 [2, 2048, 5632], P(None, 'dp', 'tensor')
- ffn_out_m_next: float32 [5632, 2048], P('tensor', 'dp')
- gains_m_next: float32 [2, 2048], replicated
- mix_in_v_next: float32 [3, 2048, 2048], P(None, 'dp', 'tensor')
- mix_out_v_next: float32 [2048, 2048], P('tensor', 'dp')
- ffn_in_v_next: float32 [2, 2048, 5632], P(None, 'dp', 'tensor')
- ffn_out_v_next: float32 [5632, 2048], P('tensor', 'dp')
- gains_v_next: float32 [2, 2048], replicated
- mix_in_copy: bfloat16 [3, 2048, 2048], P(None, 'dp', 'tensor')
- mix_out_copy: bfloat16 [2048, 2048], P('tensor', 'dp')
- ffn_in_copy: bfloat16 [2, 2048, 5632], P(None, 'dp', 'tensor')
- ffn_out_copy: bfloat16 [5632, 2048], P('tensor', 'dp')
- layer_norms: float32 [2, 9], replicated
The draws below stay inside these ranges and needn't reach their ends.
Inputs may be any that keep to these rules, and one draw needn't show every extreme that they name: `doc_lengths`: each row holds the lengths of one group's 4 sequences, which together fill its 3072 rows; in every row the longest is exactly 1536.
All inputs are finite; a program needn't handle non-finite values.
Results may differ from the reference program's by a relative error of at most 0.022.
Values may be sent and summed in bfloat16 or wider, within the bound.
No kernel may reach another device: no remote copies, remote signals or barrier semaphores. Data moves between devices by JAX's collectives and lax.ppermute only.
A program may use at most 384 MiB of HBM per device.

```python
import math
import jax
import jax.numpy as jnp
import numpy as np
from jax import lax

D = 2048
FF = 5632
ROWS_DP = 3072
DOCS = 4
STEP = 10
TOKENS = 24576
MOST_LEN = 1536
N_DP = 8


def rising(length, lowest):
    places = (jnp.arange(length, dtype=jnp.float32) + 0.5) / length
    return lowest + places


def draw_mix_in(key, part):
    key = jax.random.fold_in(key, 11)
    noise_base = jax.random.normal(key, (3, D, D), jnp.float32)
    lowest = 0.5
    return noise_base * D ** (-0.5) * rising(D, lowest)[None, :, None] * rising(D, lowest)[None, None, :]


def draw_mix_out(key, part):
    key = jax.random.fold_in(key, 12)
    noise_base = jax.random.normal(key, (D, D), jnp.float32)
    lowest = 0.5
    return noise_base * (2.0 * D ** (-0.5)) * rising(D, lowest)[:, None] * rising(D, lowest)[None, :]


def draw_ffn_in(key, part):
    key = jax.random.fold_in(key, 13)
    noise_base = jax.random.normal(key, (2, D, FF), jnp.float32)
    lowest = 0.5
    return noise_base * D ** (-0.5) * rising(D, lowest)[None, :, None] * rising(FF, lowest)[None, None, :]


def draw_ffn_out(key, part):
    key = jax.random.fold_in(key, 14)
    noise_base = jax.random.normal(key, (FF, D), jnp.float32)
    lowest = 0.5
    return noise_base * FF ** (-0.5) * rising(FF, lowest)[:, None] * rising(D, lowest)[None, :]


def draw_cotangent(key, part):
    key = jax.random.fold_in(key, 15)
    noise_base = jax.random.normal(key, (TOKENS, D), jnp.float32)
    lowest = 0.5
    groups = TOKENS // ROWS_DP
    row_ids = jnp.arange(TOKENS, dtype=jnp.int32)
    within = ((row_ids % ROWS_DP).astype(jnp.float32) + 0.5) / ROWS_DP
    across = ((row_ids // ROWS_DP).astype(jnp.float32) + 0.5) / groups
    row_scale = (lowest + within) * (lowest + across)
    return (noise_base * row_scale[:, None]).astype(jnp.bfloat16)


def block_scale(rng, shape, pieces, smallest, largest):
    level, own = 1.0, jax.random.fold_in(rng, 6)
    for position, shards_of in pieces:
        heights = jnp.exp(jax.random.uniform(jax.random.fold_in(own, position), (shards_of,), jnp.float32, smallest / len(pieces), largest / len(pieces)))
        level = level * jnp.repeat(heights, shape[position] // shards_of).reshape([-1 if axis == position else 1 for axis in range(len(shape))])
    return level


def split_up(number_of, total, reach, slope):
    loads = [(1 << 20) // math.isqrt(grade ** slope) + 1 for grade in range(2, number_of + 1)]
    spare, given = total - reach - (number_of - 1), [1] * (number_of - 1)
    while spare > 0:
        free = [i for i in range(number_of - 1) if given[i] < reach]
        mass, remaining = sum([loads[i] for i in free]), spare
        for i in free:
            extra = min(reach - given[i], max(1, remaining * loads[i] // mass), spare)
            given[i] = given[i] + extra
            spare = spare - extra
    return np.array([reach] + given)


def ragged(rng, amount, total, limit, lean):
    if amount == 2:
        one = jax.random.randint(rng, (), max(1, total - limit), min(limit, total - 1) + 1)
        return jnp.stack([one, total - one])
    sizes = jnp.asarray(split_up(amount, total, limit, lean), jnp.int32)
    twos = (amount - 1) // 2
    donor, taker = sizes[1:1 + 2 * twos:2], sizes[2:2 + 2 * twos:2]
    room = jnp.minimum(donor - 1, limit - taker)
    moved = jax.random.randint(jax.random.fold_in(rng, 1), (twos,), 0, 1 << 20) % (room + 1)
    sizes = sizes.at[1:1 + 2 * twos:2].set(donor - moved).at[2:2 + 2 * twos:2].set(taker + moved)
    return sizes[jax.random.permutation(jax.random.fold_in(rng, 2), amount)]


def normal_values(stream_key, extent, scale, limit, shards=(), held_as=jnp.bfloat16):
    factor_of = block_scale(stream_key, extent, shards, -0.22, 0.18) if shards else 1.0
    entries = jax.random.normal(stream_key, extent, jnp.float32) * scale * factor_of
    return jnp.minimum(jnp.maximum(entries, -limit), limit).astype(held_as)


def setup_inputs(seed: int = 0) -> dict:
    arg_keys = jax.random.split(jax.random.key(seed), 19)
    return {
        "tokens": normal_values(arg_keys[0], (TOKENS, D), 1.0, 6.0, ((0, 32),)),
        "cotangent": draw_cotangent(jax.random.fold_in(arg_keys[18], 71), 0),
        "doc_lengths": jax.vmap(lambda own: ragged(own, DOCS, ROWS_DP, MOST_LEN, 2))(jax.random.split(arg_keys[2], N_DP)).reshape((N_DP, DOCS)).astype(jnp.int32),
        "mix_in": draw_mix_in(jax.random.fold_in(arg_keys[18], 71), 0),
        "mix_out": draw_mix_out(jax.random.fold_in(arg_keys[18], 71), 0),
        "ffn_in": draw_ffn_in(jax.random.fold_in(arg_keys[18], 71), 0),
        "ffn_out": draw_ffn_out(jax.random.fold_in(arg_keys[18], 71), 0),
        "gains": jnp.clip(1.0 + 0.1 * jax.random.normal(arg_keys[7], (2, D), jnp.float32), 0.5, 1.5),
        "mix_in_m": normal_values(arg_keys[8], (3, D, D), (0.022 * TOKENS ** 0.5), 20.0, ((1, 8), (2, 4)), jnp.float32),
        "mix_out_m": normal_values(arg_keys[9], (D, D), (0.044 * TOKENS ** 0.5), 40.0, ((0, 4), (1, 8)), jnp.float32),
        "ffn_in_m": normal_values(arg_keys[10], (2, D, FF), (0.055 * TOKENS ** 0.5), 56.0, ((1, 8), (2, 4)), jnp.float32),
        "ffn_out_m": normal_values(arg_keys[11], (FF, D), (0.066 * TOKENS ** 0.5), 64.0, ((0, 4), (1, 8)), jnp.float32),
        "gains_m": normal_values(arg_keys[12], (2, D), (0.11 * TOKENS ** 0.5), 112.0, (), jnp.float32),
        "mix_in_v": jnp.clip(jnp.exp(math.log(3.93216) - 1.3862944 * jax.random.uniform(arg_keys[13], (3, D, D), jnp.float32) ** block_scale(arg_keys[13], (3, D, D), ((1, 8), (2, 4)), -0.2, 0.2)), 0.98304, 3.93216),
        "mix_out_v": jnp.clip(jnp.exp(math.log(15.72864) - 1.3862944 * jax.random.uniform(arg_keys[14], (D, D), jnp.float32) ** block_scale(arg_keys[14], (D, D), ((0, 4), (1, 8)), -0.2, 0.2)), 3.93216, 15.72864),
        "ffn_in_v": jnp.clip(jnp.exp(math.log(24.576) - 1.3862944 * jax.random.uniform(arg_keys[15], (2, D, FF), jnp.float32) ** block_scale(arg_keys[15], (2, D, FF), ((1, 8), (2, 4)), -0.2, 0.2)), 6.144, 24.576),
        "ffn_out_v": jnp.clip(jnp.exp(math.log(35.38944) - 1.3862944 * jax.random.uniform(arg_keys[16], (FF, D), jnp.float32) ** block_scale(arg_keys[16], (FF, D), ((0, 4), (1, 8)), -0.2, 0.2)), 8.84736, 35.38944),
        "gains_v": jnp.clip(jnp.exp(jax.random.uniform(arg_keys[17], (2, D), jnp.float32, math.log(24.576), math.log(98.304))), 24.576, 98.304),
    }


@jax.custom_vjp
def low(v):
    return lax.optimization_barrier(v.astype(jnp.bfloat16)).astype(jnp.float32)

@jax.custom_vjp
def low_back(v):
    return v

def low_keep(v):
    return (low(v), None)

def low_pass(kept, grad):
    return (grad,)

def back_keep(v):
    return (v, None)

def back_low(kept, grad):
    return (low(grad),)
low.defvjp(low_keep, low_pass)
low_back.defvjp(back_keep, back_low)
LOWER_BOUND = 0.8
RMS_EPSILON = 1e-06
BETA_ONE = 0.9
BETA_TWO = 0.999
ADAM_EPSILON = 1e-06
WEIGHT_DECAY = 0.01
LEARN_RATE = 0.5
NORM_EPSILON = 1e-12
HIGHEST = lax.Precision.HIGHEST

def normalize(values, gain):
    return values * lax.rsqrt(lax.optimization_barrier(jnp.mean(values * values, axis=-1, keepdims=True)) + RMS_EPSILON) * gain

def start_keep(lengths, rows):
    offsets = (jnp.cumsum(lengths) - lengths).astype(jnp.int32)
    places = jnp.arange(rows, dtype=jnp.int32)
    starts = jnp.any(places[:, None] == offsets[None, :], axis=1)
    return jnp.where(starts, 0.0, 1.0).astype(jnp.float32)[:, None]

def combine(earlier, later):
    return (earlier[0] * later[0], later[0] * earlier[1] + later[1])

def linear_scan(rates, driving):
    return lax.associative_scan(combine, (rates, driving), axis=0)[1]

def group_layer(inputs, lengths, mix_in, mix_out, ffn_in, ffn_out, gains):
    normed = low(normalize(inputs, gains[0]))
    pre_all = jnp.einsum('rd,kdc->krc', normed, mix_in, precision=HIGHEST)
    pre_input = low_back(pre_all[0])
    pre_forget = low_back(pre_all[1])
    pre_gate = low_back(pre_all[2])
    keeping = start_keep(lengths, inputs.shape[0])
    rates = keeping * (LOWER_BOUND + (1.0 - LOWER_BOUND) * jax.nn.sigmoid(pre_forget))
    states = linear_scan(rates, (1.0 - rates) * jax.nn.silu(pre_input))
    gated = low(states * jax.nn.silu(pre_gate))
    middle = inputs + low_back(jnp.dot(gated, mix_out, precision=HIGHEST))
    normed_two = low(normalize(middle, gains[1]))
    gate_proj = low_back(jnp.dot(normed_two, ffn_in[0], precision=HIGHEST))
    up_proj = low_back(jnp.dot(normed_two, ffn_in[1], precision=HIGHEST))
    hidden = low(jax.nn.silu(gate_proj) * up_proj)
    return middle + jnp.dot(hidden, ffn_out, precision=HIGHEST)

def adam_moments(grad, weight, first, second, decay_rate):
    first_next = BETA_ONE * first + (1.0 - BETA_ONE) * grad
    second_next = BETA_TWO * second + (1.0 - BETA_TWO) * grad * grad
    update = first_next / (1.0 - BETA_ONE ** STEP) / (jnp.sqrt(second_next / (1.0 - BETA_TWO ** STEP)) + ADAM_EPSILON) + decay_rate * weight
    return (first_next, second_next, update)

def reference(tokens, cotangent, doc_lengths, mix_in, mix_out, ffn_in, ffn_out, gains, mix_in_m, mix_out_m, ffn_in_m, ffn_out_m, gains_m, mix_in_v, mix_out_v, ffn_in_v, ffn_out_v, gains_v):
    inputs = tokens.astype(jnp.float32).reshape(-1, ROWS_DP, D)
    backs = cotangent.astype(jnp.float32).reshape(-1, ROWS_DP, D)
    working = tuple((matrix.astype(jnp.bfloat16).astype(jnp.float32) for matrix in (mix_in, mix_out, ffn_in, ffn_out)))
    checked = jax.checkpoint(group_layer)

    def forward(group_inputs, w_mix_in, w_mix_out, w_ffn_in, w_ffn_out, gain_rows):

        def one_group(paired):
            return checked(paired[0], paired[1], w_mix_in, w_mix_out, w_ffn_in, w_ffn_out, gain_rows)
        return lax.map(one_group, (group_inputs, doc_lengths))
    outputs, pullback = jax.vjp(forward, inputs, working[0], working[1], working[2], working[3], gains)
    d_inputs, g_mix_in, g_mix_out, g_ffn_in, g_ffn_out, g_gains = pullback(backs)
    mi_first, mi_second, mi_update = adam_moments(g_mix_in, mix_in, mix_in_m, mix_in_v, WEIGHT_DECAY)
    mo_first, mo_second, mo_update = adam_moments(g_mix_out, mix_out, mix_out_m, mix_out_v, WEIGHT_DECAY)
    fi_first, fi_second, fi_update = adam_moments(g_ffn_in, ffn_in, ffn_in_m, ffn_in_v, WEIGHT_DECAY)
    fo_first, fo_second, fo_update = adam_moments(g_ffn_out, ffn_out, ffn_out_m, ffn_out_v, WEIGHT_DECAY)
    gn_first, gn_second, gn_update = adam_moments(g_gains, gains, gains_m, gains_v, 0.0)
    weight_sq = jnp.concatenate([lax.optimization_barrier(jnp.sum(mix_in * mix_in, axis=(1, 2))), jnp.sum(mix_out * mix_out)[None], lax.optimization_barrier(jnp.sum(ffn_in * ffn_in, axis=(1, 2))), jnp.sum(ffn_out * ffn_out)[None], lax.optimization_barrier(jnp.sum(gains * gains, axis=1))])
    update_sq = jnp.concatenate([lax.optimization_barrier(jnp.sum(mi_update * mi_update, axis=(1, 2))), jnp.sum(mo_update * mo_update)[None], lax.optimization_barrier(jnp.sum(fi_update * fi_update, axis=(1, 2))), jnp.sum(fo_update * fo_update)[None], lax.optimization_barrier(jnp.sum(gn_update * gn_update, axis=1))])
    trust = jnp.sqrt(weight_sq) / jnp.sqrt(update_sq + NORM_EPSILON)
    mix_in_next = mix_in - LEARN_RATE * trust[0:3][:, None, None] * mi_update
    mix_out_next = mix_out - LEARN_RATE * trust[3] * mo_update
    ffn_in_next = ffn_in - LEARN_RATE * trust[4:6][:, None, None] * fi_update
    ffn_out_next = ffn_out - LEARN_RATE * trust[6] * fo_update
    gains_next = gains - LEARN_RATE * trust[7:9][:, None] * gn_update
    layer_norms = jnp.stack([jnp.sqrt(weight_sq), jnp.sqrt(update_sq)])
    mixed = outputs.reshape(-1, D).astype(jnp.bfloat16)
    input_grad = d_inputs.reshape(-1, D)
    return (mixed, input_grad, mix_in_next, mix_out_next, ffn_in_next, ffn_out_next, gains_next, mi_first, mo_first, fi_first, fo_first, gn_first, mi_second, mo_second, fi_second, fo_second, gn_second, mix_in_next.astype(jnp.bfloat16), mix_out_next.astype(jnp.bfloat16), ffn_in_next.astype(jnp.bfloat16), ffn_out_next.astype(jnp.bfloat16), layer_norms)
```

```python
import functools

import jax
import jax.numpy as jnp
from jax import lax
from jax.experimental import pallas as pl
from jax.experimental.pallas import tpu as pltpu
from jax.sharding import PartitionSpec as P

STEP = 10
LOWER_BOUND = 0.8
RMS_EPSILON = 1e-06
BETA_ONE = 0.9
BETA_TWO = 0.999
ADAM_EPSILON = 1e-06
WEIGHT_DECAY = 0.01
LEARN_RATE = 0.5
NORM_EPSILON = 1e-12
CHUNKS = 2
BF = jnp.bfloat16
F32 = jnp.float32
LANES = 128
SUB = 8


def exchange(value, axis, size, offset):
    return lax.ppermute(value, axis, [(i, i ^ offset) for i in range(size)])


def after(value, *others):
    return lax.optimization_barrier((value,) + others)[0]


def mm(a, b):
    return jnp.dot(a, b, preferred_element_type=F32)


def mm_nt(a, b):
    return lax.dot_general(a, b, (((1,), (1,)), ((), ())), preferred_element_type=F32)


def mm_tn(a, b):
    return lax.dot_general(a, b, (((0,), (0,)), ((), ())), preferred_element_type=F32)


def offset_of(place, n):
    return 2 * (place % (n // 2)) + place // (n // 2)


def place_of(offset, n):
    return (offset % 2) * (n // 2) + offset // 2


def gather_blocks(own, axis, size):
    far = [own] + [exchange(own, axis, size, 2 * m) for m in range(1, size // 2)]
    near = [exchange(block, axis, size, 1) for block in far]
    return far + near


def reduce_rows(part, size, rows):
    half = size // 2
    near = exchange(part(half, size).astype(BF), "tensor", size, 1)
    far = (part(1, half) + near[rows:].astype(F32)).astype(BF)
    arrived = [
        exchange(far[(m - 1) * rows : m * rows], "tensor", size, 2 * m) for m in range(1, half)
    ]
    total = part(0, 1) + near[:rows].astype(F32)
    for value in arrived:
        total = total + value.astype(F32)
    return total


def reduce_grad(high, low, size, axis):
    half = size // 2
    near = exchange(high, "dp", size, 1)
    both = low.astype(F32) + near.astype(F32)
    width = both.shape[axis] // half
    parts = [lax.slice_in_dim(both, m * width, (m + 1) * width, axis=axis) for m in range(half)]
    total = parts[0]
    for m in range(1, half):
        total = total + exchange(parts[m].astype(BF), "dp", size, 2 * m).astype(F32)
    return total


def place_columns(values, source, width):
    rows, columns = values.shape

    def kernel(_, src, dst):
        dst[...] = src[...]

    return pl.pallas_call(
        kernel,
        grid_spec=pltpu.PrefetchScalarGridSpec(
            num_scalar_prefetch=1,
            grid=(columns // width,),
            in_specs=[pl.BlockSpec((rows, width), lambda j, s: (0, s[j]))],
            out_specs=pl.BlockSpec((rows, width), lambda j, s: (0, j)),
        ),
        out_shape=jax.ShapeDtypeStruct(values.shape, values.dtype),
        compiler_params=pltpu.CompilerParams(vmem_limit_bytes=32 * 2**20),
        name="place_columns",
    )(source, values)


def sigmoid(v):
    return 0.5 * jnp.tanh(0.5 * v) + 0.5


def keep_of(row0, offsets):
    places = row0 + lax.broadcasted_iota(jnp.int32, (SUB, LANES), 0)
    start = places == offsets[0]
    for d in range(1, offsets.shape[0]):
        start = start | (places == offsets[d])
    return jnp.where(start, 0.0, 1.0).astype(F32)


def forward_kernel(order, offsets, pin, pforget, pgate, gated, before, carry):
    block = pl.program_id(0)
    rows, channels = pin.shape[1:]

    @pl.when(block == 0)
    def _():
        carry[...] = jnp.zeros_like(carry)

    row_id = lax.broadcasted_iota(jnp.int32, (SUB, LANES), 0)

    def step(i, _):
        base = pl.multiple_of(i * 2 * SUB, 2 * SUB)
        keeps = [keep_of(block * rows + base + g * SUB, offsets) for g in range(2)]
        for c in range(channels // LANES):
            lanes = pl.ds(c * LANES, LANES)
            state = carry[:, lanes]
            outs = []
            for g in range(2):
                at = (0, pl.ds(base + g * SUB, SUB), lanes)
                vin, vforget, vgate = pin[at], pforget[at], pgate[at]
                rate = keeps[g] * (LOWER_BOUND + (1.0 - LOWER_BOUND) * sigmoid(vforget))
                drive = (1.0 - rate) * (vin * sigmoid(vin))
                a, b = rate, drive
                for s in (1, 2, 4):
                    inside = row_id >= s
                    a_up = jnp.where(inside, pltpu.roll(a, s, 0), 1.0)
                    b_up = jnp.where(inside, pltpu.roll(b, s, 0), 0.0)
                    b = a * b_up + b
                    a = a * a_up
                whole = b + a * state
                before[at] = jnp.where(row_id == 0, state, pltpu.roll(whole, 1, 0))
                last_a = jnp.broadcast_to(a[SUB - 1 : SUB], (SUB, LANES))
                last_b = jnp.broadcast_to(b[SUB - 1 : SUB], (SUB, LANES))
                state = last_b + last_a * state
                outs.append(whole * (vgate * sigmoid(vgate)))
            carry[:, lanes] = state
            gated[0, pl.ds(base, 2 * SUB), lanes] = jnp.concatenate(outs, axis=0).astype(BF)
        return 0

    lax.fori_loop(0, rows // (2 * SUB), step, 0)


def backward_kernel(order, offsets, pin, pforget, pgate, before, dgated, dpre, carry):
    step_id = pl.program_id(0)
    block = pl.num_programs(0) - 1 - step_id
    rows, channels = pin.shape[1:]

    @pl.when(step_id == 0)
    def _():
        carry[...] = jnp.zeros_like(carry)

    row_id = lax.broadcasted_iota(jnp.int32, (SUB, LANES), 0)
    groups = rows // (2 * SUB)

    def step(i, _):
        base = pl.multiple_of((groups - 1 - i) * 2 * SUB, 2 * SUB)
        keeps = [keep_of(block * rows + base + g * SUB, offsets) for g in range(2)]
        for c in range(channels // LANES):
            lanes = pl.ds(c * LANES, LANES)
            flow = carry[:, lanes]
            outs = [None, None]
            for g in (1, 0):
                at = (0, pl.ds(base + g * SUB, SUB), lanes)
                vin, vforget, vgate = pin[at], pforget[at], pgate[at]
                keep, prev, dg = keeps[g], before[at], dgated[at].astype(F32)
                s_forget = sigmoid(vforget)
                rate = keep * (LOWER_BOUND + (1.0 - LOWER_BOUND) * s_forget)
                s_in = sigmoid(vin)
                act_in = vin * s_in
                rest = 1.0 - rate
                state = rate * prev + rest * act_in
                s_gate = sigmoid(vgate)
                x = dg * (vgate * s_gate)
                a, b = rate, rate * x
                for s in (1, 2, 4):
                    inside = row_id < SUB - s
                    a_down = jnp.where(inside, pltpu.roll(a, SUB - s, 0), 1.0)
                    b_down = jnp.where(inside, pltpu.roll(b, SUB - s, 0), 0.0)
                    b = a * b_down + b
                    a = a * a_down
                q = b + a * flow
                carried = x + jnp.where(row_id == SUB - 1, flow, pltpu.roll(q, SUB - 1, 0))
                first_a = jnp.broadcast_to(a[0:1], (SUB, LANES))
                first_b = jnp.broadcast_to(b[0:1], (SUB, LANES))
                flow = first_b + first_a * flow
                d_in = carried * rest * (s_in * (1.0 + vin * (1.0 - s_in)))
                d_forget = (
                    carried
                    * (prev - act_in)
                    * keep
                    * ((1.0 - LOWER_BOUND) * s_forget * (1.0 - s_forget))
                )
                d_gate = dg * state * (s_gate * (1.0 + vgate * (1.0 - s_gate)))
                outs[g] = (d_in, d_forget, d_gate)
            carry[:, lanes] = flow
            for k in range(3):
                dpre[0, pl.ds(base, 2 * SUB), pl.ds(k * channels + c * LANES, LANES)] = (
                    jnp.concatenate([outs[0][k], outs[1][k]], axis=0).astype(BF)
                )
        return 0

    lax.fori_loop(0, groups, step, 0)


def recurrence_call(kernel, order, offsets, operands, outs, name):
    blocks, rows, channels = operands[0].shape

    def spec(width):
        return pl.BlockSpec((1, rows, width), lambda a, o, f: (o[a], 0, 0))

    return pl.pallas_call(
        kernel,
        grid_spec=pltpu.PrefetchScalarGridSpec(
            num_scalar_prefetch=2,
            grid=(blocks,),
            in_specs=[spec(v.shape[2]) for v in operands],
            out_specs=[spec(v.shape[2]) for v in outs],
            scratch_shapes=[pltpu.VMEM((SUB, channels), F32)],
        ),
        out_shape=outs,
        compiler_params=pltpu.CompilerParams(vmem_limit_bytes=48 * 2**20),
        cost_estimate=pl.CostEstimate(
            flops=blocks * rows * channels * 100,
            bytes_accessed=blocks * rows * channels * 4 * 6,
            transcendentals=blocks * rows * channels * 3,
        ),
        name=name,
    )(order, offsets, *operands)


def unit(values):
    scaling = lax.rsqrt(jnp.mean(values * values, axis=-1, keepdims=True) + RMS_EPSILON)
    return values * scaling, scaling


def norm_backward(d_normed, unit_rows, scaling, gain):
    d_unit = d_normed * gain
    d_values = scaling * (d_unit - unit_rows * jnp.mean(d_unit * unit_rows, axis=-1, keepdims=True))
    return d_values, jnp.sum(d_normed * unit_rows, axis=0)


def adam_moments(grad, weight, first, second, decay_rate):
    first_next = BETA_ONE * first + (1.0 - BETA_ONE) * grad
    second_next = BETA_TWO * second + (1.0 - BETA_TWO) * grad * grad
    update = (
        first_next
        / (1.0 - BETA_ONE**STEP)
        / (jnp.sqrt(second_next / (1.0 - BETA_TWO**STEP)) + ADAM_EPSILON)
        + decay_rate * weight
    )
    return (first_next, second_next, update)


def total_over_mesh(values, n_dp, n_tensor):
    for axis, size in (("tensor", n_tensor), ("dp", n_dp)):
        offset = 1
        while offset < size:
            values = values + exchange(values, axis, size, offset)
            offset *= 2
    return values


def per_device(
    n_dp,
    n_tensor,
    tokens,
    cotangent,
    doc_lengths,
    mix_in,
    mix_out,
    ffn_in,
    ffn_out,
    gains,
    mix_in_m,
    mix_out_m,
    ffn_in_m,
    ffn_out_m,
    gains_m,
    mix_in_v,
    mix_out_v,
    ffn_in_v,
    ffn_out_v,
    gains_v,
):
    rows, width = tokens.shape
    depth = mix_in.shape[1]
    channels = mix_in.shape[2]
    hidden_units = ffn_in.shape[2]
    piece = rows // CHUNKS
    half_width = width // 2
    dp_id = lax.axis_index("dp")
    tensor_id = lax.axis_index("tensor")
    place_source = jnp.stack([dp_id ^ offset_of(p, n_dp) for p in range(n_dp)]).astype(jnp.int32)
    place_back = jnp.stack([place_of(a ^ dp_id, n_dp) for a in range(n_dp)]).astype(jnp.int32)
    order = jnp.stack([place_of(a ^ tensor_id, n_tensor) for a in range(n_tensor)]).astype(jnp.int32)
    offsets = (jnp.cumsum(doc_lengths[0]) - doc_lengths[0]).astype(jnp.int32)

    tokens_p = place_columns(tokens, place_source, depth)
    gains_p = place_columns(gains, place_source, depth)
    inputs = tokens_p.astype(F32)
    unit_one, scale_one = unit(inputs)
    normed_one = (unit_one * gains_p[0]).astype(BF)

    def gather_rows(own):
        return jnp.concatenate(gather_blocks(own, "tensor", n_tensor), axis=0)

    w_mix_in = [
        jnp.concatenate(gather_blocks(mix_in[k].astype(BF), "dp", n_dp), axis=0) for k in range(3)
    ]
    whole_one = gather_rows(normed_one)
    w_mix_out = jnp.concatenate(
        gather_blocks(after(mix_out.astype(BF), w_mix_in[2]), "dp", n_dp), axis=1
    )
    w_ffn_in = [
        jnp.concatenate(
            gather_blocks(after(ffn_in[k].astype(BF), w_mix_in[2]), "dp", n_dp), axis=0
        )
        for k in range(2)
    ]
    w_ffn_out = jnp.concatenate(
        gather_blocks(after(ffn_out.astype(BF), w_ffn_in[1]), "dp", n_dp), axis=1
    )
    cot_p = place_columns(cotangent, place_source, depth)
    cot_pieces = [
        gather_rows(after(cot_p[i * piece : (i + 1) * piece], whole_one)) for i in range(CHUNKS)
    ]

    pre = [mm(whole_one, w).reshape(n_tensor, rows, channels) for w in w_mix_in]
    blocked = (n_tensor, rows, channels)
    gated, before = recurrence_call(
        forward_kernel,
        order,
        offsets,
        pre,
        [jax.ShapeDtypeStruct(blocked, BF), jax.ShapeDtypeStruct(blocked, F32)],
        "recurrence_forward",
    )

    def piece_of(values, i):
        return values[:, i * piece : (i + 1) * piece]

    middle, unit_two, scale_two, whole_two = [], [], [], []
    for i in range(CHUNKS):
        gated_i = piece_of(gated, i)

        def part(lo, hi, gated_i=gated_i):
            return mm(gated_i[lo:hi].reshape(-1, channels), w_mix_out)

        middle_i = inputs[i * piece : (i + 1) * piece] + reduce_rows(part, n_tensor, piece)
        unit_i, scale_i = unit(middle_i)
        middle.append(middle_i)
        unit_two.append(unit_i)
        scale_two.append(scale_i)
        whole_two.append(gather_rows((unit_i * gains_p[1]).astype(BF)))

    hidden, d_gate, d_up, d_middle, gain_two, whole_d = [], [], [], [], 0.0, []
    for i in range(CHUNKS):
        gate = mm(whole_two[i], w_ffn_in[0])
        up = mm(whole_two[i], w_ffn_in[1])
        s_gate = jax.nn.sigmoid(gate)
        act = gate * s_gate
        hidden.append((act * up).astype(BF))
        d_hidden = mm_nt(cot_pieces[i], w_ffn_out)
        d_gate.append((d_hidden * up * (s_gate * (1.0 + gate * (1.0 - s_gate)))).astype(BF))
        d_up.append((d_hidden * act).astype(BF))

        def part(lo, hi, i=i):
            at = slice(lo * piece, hi * piece)
            return mm_nt(d_gate[i][at], w_ffn_in[0]) + mm_nt(d_up[i][at], w_ffn_in[1])

        d_normed = reduce_rows(part, n_tensor, piece)
        d_norm, gain_i = norm_backward(d_normed, unit_two[i], scale_two[i], gains_p[1])
        d_middle_i = cot_p[i * piece : (i + 1) * piece].astype(F32) + d_norm
        gain_two = gain_two + gain_i
        d_middle.append(d_middle_i)
        whole_d.append(gather_rows(d_middle_i.astype(BF)))
    mixed = []
    for i in range(CHUNKS):

        def part(lo, hi, i=i):
            return mm(hidden[i][lo * piece : hi * piece], w_ffn_out)

        mixed.append((middle[i] + reduce_rows(part, n_tensor, piece)).astype(BF))

    def grad_of(lefts, rights):
        total = mm_tn(lefts[0], rights[0])
        for left, right in zip(lefts[1:], rights[1:]):
            total = total + mm_tn(left, right)
        return total.astype(BF)

    g_ffn_out = grad_of(hidden, cot_pieces)
    g_ffn_out = reduce_grad(g_ffn_out[:, half_width:], g_ffn_out[:, :half_width], n_dp, 1)
    g_ffn_in = []
    for side in (d_gate, d_up):
        grad = grad_of(whole_two, side)
        g_ffn_in.append(reduce_grad(grad[half_width:], grad[:half_width], n_dp, 0))

    d_gated = [mm_nt(v, w_mix_out).reshape(n_tensor, piece, channels) for v in whole_d]
    d_gated = jnp.concatenate(d_gated, axis=1)
    (d_pre,) = recurrence_call(
        backward_kernel,
        order[::-1],
        offsets,
        pre + [before, d_gated],
        [jax.ShapeDtypeStruct((n_tensor, rows, 3 * channels), BF)],
        "recurrence_backward",
    )
    w_mix_all = jnp.concatenate(w_mix_in, axis=1)
    g_mix_out = grad_of([piece_of(gated, i).reshape(-1, channels) for i in range(CHUNKS)], whole_d)
    g_mix_out = reduce_grad(g_mix_out[:, half_width:], g_mix_out[:, :half_width], n_dp, 1)
    d_flat = d_pre.reshape(n_tensor * rows, 3 * channels)
    g_mix_in = []
    for k in range(3):
        grad = mm_tn(whole_one, d_flat[:, k * channels : (k + 1) * channels]).astype(BF)
        g_mix_in.append(reduce_grad(grad[half_width:], grad[:half_width], n_dp, 0))
    input_grad, gain_one = [], 0.0
    for i in range(CHUNKS):
        d_i = piece_of(d_pre, i)

        def part(lo, hi, d_i=d_i):
            return mm_nt(d_i[lo:hi].reshape(-1, 3 * channels), w_mix_all)

        at = slice(i * piece, (i + 1) * piece)
        d_norm, gain_i = norm_backward(
            reduce_rows(part, n_tensor, piece), unit_one[at], scale_one[at], gains_p[0]
        )
        gain_one = gain_one + gain_i
        input_grad.append(d_middle[i] + d_norm)

    mixed = place_columns(jnp.concatenate(mixed, axis=0), place_back, depth)
    input_grad = place_columns(jnp.concatenate(input_grad, axis=0), place_back, depth)
    gain_grads = place_columns(jnp.stack([gain_one, gain_two]), place_back, depth)

    weights = [mix_in[0], mix_in[1], mix_in[2], mix_out, ffn_in[0], ffn_in[1], ffn_out]
    firsts = [mix_in_m[0], mix_in_m[1], mix_in_m[2], mix_out_m, ffn_in_m[0], ffn_in_m[1], ffn_out_m]
    seconds = [mix_in_v[0], mix_in_v[1], mix_in_v[2], mix_out_v, ffn_in_v[0], ffn_in_v[1], ffn_out_v]
    grads = g_mix_in + [g_mix_out] + g_ffn_in + [g_ffn_out]
    moments = [
        adam_moments(g, w, m, v, WEIGHT_DECAY)
        for g, w, m, v in zip(grads, weights, firsts, seconds)
    ]
    squares = jnp.stack(
        [jnp.sum(w * w) for w in weights] + [jnp.sum(u * u) for _, _, u in moments]
    )
    packed = jnp.concatenate([gain_grads.reshape(-1), jnp.pad(squares, (0, SUB * LANES - 14))])
    packed = total_over_mesh(packed.reshape(-1, LANES), n_dp, n_tensor).reshape(-1)
    gain_grads = packed[: 2 * width].reshape(2, width)
    squares = packed[2 * width : 2 * width + 14].reshape(2, 7)
    gn_first, gn_second, gn_update = adam_moments(gain_grads, gains, gains_m, gains_v, 0.0)
    weight_sq = jnp.concatenate([squares[0], jnp.sum(gains * gains, axis=1)])
    update_sq = jnp.concatenate([squares[1], jnp.sum(gn_update * gn_update, axis=1)])
    trust = jnp.sqrt(weight_sq) / jnp.sqrt(update_sq + NORM_EPSILON)
    nexts = [w - LEARN_RATE * trust[i] * moments[i][2] for i, w in enumerate(weights)]
    gains_next = gains - LEARN_RATE * trust[7:9][:, None] * gn_update
    layer_norms = jnp.stack([jnp.sqrt(weight_sq), jnp.sqrt(update_sq)])

    def grouped(values):
        return (jnp.stack(values[0:3]), values[3], jnp.stack(values[4:6]), values[6])

    return (
        (mixed, input_grad)
        + grouped(nexts)
        + (gains_next,)
        + grouped([m for m, _, _ in moments])
        + (gn_first,)
        + grouped([v for _, v, _ in moments])
        + (gn_second,)
        + grouped([n.astype(BF) for n in nexts])
        + (layer_norms,)
    )


def solution(mesh):
    rows = P(("dp", "tensor"), None)
    inner = P(None, "dp", "tensor")
    outer = P("tensor", "dp")
    matrices = (inner, outer, inner, outer)
    in_specs = (rows, rows, P("dp", None)) + (matrices + (P(),)) * 3
    out_specs = (rows, rows) + (matrices + (P(),)) * 3 + matrices + (P(),)
    body = functools.partial(per_device, mesh.shape["dp"], mesh.shape["tensor"])
    return jax.shard_map(
        body, mesh=mesh, in_specs=in_specs, out_specs=out_specs, check_vma=False
    )
```

```python
import functools

import jax
import jax.numpy as jnp
from jax import lax
from jax.experimental import pallas as pl
from jax.experimental.pallas import tpu as pltpu
from jax.sharding import PartitionSpec as P

STEP = 10
LOWER_BOUND = 0.8
RMS_EPSILON = 1e-06
BETA_ONE = 0.9
BETA_TWO = 0.999
ADAM_EPSILON = 1e-06
WEIGHT_DECAY = 0.01
LEARN_RATE = 0.5
NORM_EPSILON = 1e-12
CHUNKS = 2
BF = jnp.bfloat16
F32 = jnp.float32
LANES = 128
SUB = 8


def likely_flops(flops):
    return int(1.6 * flops) + 4_000_000_000


def exchange(value, axis, size, offset):
    return lax.ppermute(value, axis, [(i, i ^ offset) for i in range(size)])


def after(value, *others):
    return lax.optimization_barrier((value,) + others)[0]


def mm(a, b):
    return jnp.dot(a, b, preferred_element_type=F32)


def mm_nt(a, b):
    return lax.dot_general(a, b, (((1,), (1,)), ((), ())), preferred_element_type=F32)


def mm_tn(a, b):
    return lax.dot_general(a, b, (((0,), (0,)), ((), ())), preferred_element_type=F32)


class Sequence:
    def __init__(self):
        self.last = None

    def run(self, call, *operands):
        if self.last is not None:
            operands = (after(operands[0], self.last),) + operands[1:]
        result = call(*operands)
        self.last = jax.tree.leaves(result)[0]
        return result

    def pin(self, *values):
        out = lax.optimization_barrier(values + (self.last,))
        self.last = out[0]
        return out[:-1]


def join(axis):
    return lambda *blocks: jnp.concatenate(blocks, axis=axis)


def halving(n):
    offsets, offset = [], 1
    while offset < n:
        offsets.append(offset)
        offset *= 2
    return offsets


def offsets_by_place(exchanges):
    offsets = [0]
    for offset in reversed(exchanges):
        offsets = offsets + [o ^ offset for o in offsets]
    return offsets


def owners(index, exchanges):
    return jnp.stack([index ^ o for o in offsets_by_place(exchanges)]).astype(jnp.int32)


def spread(blocks, owner):
    rows, columns = blocks[0].shape
    whole = jnp.zeros((rows * len(blocks), columns), blocks[0].dtype)
    for p, block in enumerate(blocks):
        whole = lax.dynamic_update_slice(whole, block, (owner[p] * rows, 0))
    return whole


class SummedGrad:
    def __init__(self, sequence, halves, size, exchanges):
        self.sequence, self.size, self.exchanges = sequence, size, exchanges
        self.send(*halves)

    def send(self, sent, kept):
        self.kept = kept
        self.coming = exchange(sent, "dp", self.size, self.exchanges[0])
        self.exchanges = self.exchanges[1:]

    def step(self):
        def added(a, b):
            total = (a.astype(F32) + b.astype(F32)).astype(BF)
            half = total.shape[0] // 2
            return total[half:], total[:half]

        self.send(*self.sequence.run(added, self.kept, self.coming))

    def steps(self):
        while self.exchanges:
            self.step()


class Gathered:
    def __init__(self, own, size):
        self.size, self.held = size, [own]
        offset = size // 2
        while offset > 1:
            self.held = self.held + [exchange(part, "tensor", size, offset) for part in self.held]
            offset //= 2
        self.near = [exchange(own, "tensor", size, 1)]

    def relay(self, *done):
        self.near += [exchange(after(part, *done), "tensor", self.size, 1) for part in self.held[1:]]

    def parts(self):
        return self.held + self.near


class SummedRows:
    def __init__(self, sequence, operand, weight, size, rows):
        self.sequence, self.weight, self.size, self.rows = sequence, weight, size, rows
        self.operand = operand

    def high(self):
        half = self.size // 2 * self.rows
        if isinstance(self.operand, tuple):
            self.operand, upper = self.operand
            call = lambda v, w: mm_nt(v, w).astype(BF)
        else:
            upper = self.operand
            call = lambda v, w: mm_nt(v[half:], w).astype(BF)
        sent = self.sequence.run(call, upper, self.weight)
        self.near = exchange(sent, "tensor", self.size, 1)

    def rest(self):
        size, rows, offset, places = self.size, self.rows, 2, self.size // 4
        far, self.kept = self.sequence.run(
            lambda v, w, n: near_added(v, w, n, places * rows), self.operand, self.weight, self.near
        )
        self.coming = exchange(far, "tensor", size, offset)
        while places > 1:
            total = self.kept + self.coming.astype(F32)
            offset, places = 2 * offset, places // 2
            self.kept = total[: places * rows]
            self.coming = exchange(total[places * rows :].astype(BF), "tensor", size, offset)


def near_added(operand, weight, near, tile):
    width = weight.shape[0]

    def kernel(v, w, n, far, kept):
        step = pl.program_id(0)
        total = mm_nt(v[...], w[...]) + n[...].astype(F32)

        @pl.when(step == 0)
        def _():
            far[...] = total.astype(BF)

        @pl.when(step == 1)
        def _():
            kept[...] = total

    def rowed(v):
        return pl.BlockSpec((tile, v.shape[1]), lambda i: (1 - i, 0))

    fixed = pl.BlockSpec((tile, width), lambda i: (0, 0))
    return pl.pallas_call(
        kernel,
        grid=(2,),
        in_specs=[
            rowed(operand),
            pl.BlockSpec(weight.shape, lambda i: (0, 0), pipeline_mode=pl.Buffered(1)),
            rowed(near),
        ],
        out_specs=[fixed, fixed],
        out_shape=[jax.ShapeDtypeStruct((tile, width), BF), jax.ShapeDtypeStruct((tile, width), F32)],
        compiler_params=pltpu.CompilerParams(vmem_limit_bytes=56 * 2**20),
        cost_estimate=pl.CostEstimate(
            flops=likely_flops(4 * tile * weight.size), bytes_accessed=2 * weight.size, transcendentals=0
        ),
        name="near_added",
    )(operand, weight, near)


def sigmoid(v):
    return 0.5 * jnp.tanh(0.5 * v) + 0.5


def gate_up_kernel(x, w, hidden, slope, act):
    units = hidden.shape[1]
    for n in range(0, units, 256):
        at = slice(n, min(n + 256, units))
        up_at = slice(units + n, units + min(n + 256, units))
        gate = jnp.dot(x[...], w[:, at], preferred_element_type=F32)
        up = jnp.dot(x[...], w[:, up_at], preferred_element_type=F32)
        s = sigmoid(gate)
        a = gate * s
        hidden[:, at] = (a * up).astype(BF)
        act[:, at] = a.astype(BF)
        slope[:, at] = (up * (s * (1.0 + gate * (1.0 - s)))).astype(BF)


def gate_up_back_kernel(c, w, slope, act, out):
    units = slope.shape[1]
    for n in range(0, units, 256):
        at = slice(n, min(n + 256, units))
        up_at = slice(units + n, units + min(n + 256, units))
        d = jnp.dot(c[...], w[:, at], preferred_element_type=F32)
        out[:, at] = (d * slope[:, at].astype(F32)).astype(BF)
        out[:, up_at] = (d * act[:, at].astype(F32)).astype(BF)


def pre_kernel(x, w, out):
    out[...] = jnp.dot(x[...], w[...], preferred_element_type=F32)


def row_tiles(kernel, parts, weight, others, outs, flops, name):
    count = len(parts)
    tile, depth = parts[0].shape

    def body(*refs):
        sources, w, rest = refs[:count], refs[count], refs[count + 1 : -2]
        buffer, arrived = refs[-2:]
        step = pl.program_id(0)

        def copy(p):
            return pltpu.make_async_copy(sources[p], buffer.at[p % 2], arrived.at[p % 2])

        @pl.when(step == 0)
        def _():
            copy(0).start()

        for p in range(count):

            @pl.when(step == p)
            def _(p=p):
                if p + 1 < count:
                    copy(p + 1).start()
                copy(p).wait()

        kernel(buffer.at[lax.rem(step, 2)], w, *rest)

    def spec(v):
        return pl.BlockSpec((tile, v.shape[1]), lambda i: (i, 0))

    return pl.pallas_call(
        body,
        grid=(count,),
        in_specs=[pl.BlockSpec(memory_space=pl.ANY)] * count
        + [pl.BlockSpec(weight.shape, lambda i: (0, 0), pipeline_mode=pl.Buffered(1))]
        + [spec(v) for v in others],
        out_specs=[spec(v) for v in outs],
        out_shape=outs,
        scratch_shapes=[pltpu.VMEM((2, tile, depth), BF), pltpu.SemaphoreType.DMA((2,))],
        compiler_params=pltpu.CompilerParams(vmem_limit_bytes=56 * 2**20),
        cost_estimate=pl.CostEstimate(
            flops=likely_flops(flops), bytes_accessed=weight.size * 4, transcendentals=0
        ),
        name=name,
    )(*parts, weight, *others)


def grad_kernel(lefts, rights, moving, wide, name, fixed=(0, 1), owner=None):
    part, parts = fixed
    mover, other = (lefts, rights) if moving == "left" else (rights, lefts)
    rows = sum(v.shape[0] for v in mover)
    steps = mover[0].shape[1] // wide
    held = other[0].shape[1] // parts
    shape = (wide, held) if moving == "left" else (held, wide)
    half = steps // 2
    count, others = len(mover), len(other)

    def body(owners_ref, sources, write):
        movers, fixers = sources[:count], sources[count : count + others]
        moved, kept, arrived, ready = sources[-4:]
        step = pl.program_id(0)

        def copies(at, slot):
            column = at if owners_ref is None else owners_ref[lax.rem(at + half, steps)]
            columns = pl.ds(pl.multiple_of(column * wide, wide), wide)
            made, row = [], 0
            for p, source in enumerate(movers):
                size = source.shape[0]
                made.append(
                    pltpu.make_async_copy(
                        source.at[:, columns],
                        moved.at[slot, pl.ds(row, size), :],
                        arrived.at[slot, p],
                    )
                )
                row += size
            return made

        def fixed_copies():
            made, row = [], 0
            for p, source in enumerate(fixers):
                size = source.shape[0]
                made.append(
                    pltpu.make_async_copy(
                        source.at[:, pl.ds(part * held, held)],
                        kept.at[pl.ds(row, size), :],
                        ready.at[p],
                    )
                )
                row += size
            return made

        @pl.when(step == 0)
        def _():
            for copy in copies(0, 0) + fixed_copies():
                copy.start()

        slot = lax.rem(step, 2)

        @pl.when(step + 1 < steps)
        def _():
            for copy in copies(step + 1, 1 - slot):
                copy.start()

        for copy in copies(step, slot):
            copy.wait()

        @pl.when(step == 0)
        def _():
            for copy in fixed_copies():
                copy.wait()

        pair = (moved[slot], kept[...]) if moving == "left" else (kept[...], moved[slot])
        total = lax.dot_general(
            *pair, (((0,), (0,)), ((), ())), preferred_element_type=F32
        ).astype(BF)
        write(step, total)

    settings = dict(
        compiler_params=pltpu.CompilerParams(vmem_limit_bytes=56 * 2**20),
        cost_estimate=pl.CostEstimate(
            flops=likely_flops(2 * steps * shape[0] * shape[1] * rows),
            bytes_accessed=2 * steps * shape[0] * shape[1],
            transcendentals=0,
        ),
        name=name,
    )
    in_specs = [pl.BlockSpec(memory_space=pl.ANY)] * (count + others)
    scratch = [
        pltpu.VMEM((2, rows, wide), BF),
        pltpu.VMEM((rows, held), BF),
        pltpu.SemaphoreType.DMA((2, count)),
        pltpu.SemaphoreType.DMA((others,)),
    ]
    if owner is None:

        def kernel(*refs):
            out = refs[count + others]

            def write(step, total):
                out[...] = total

            body(None, refs[: count + others] + refs[-4:], write)

        whole = (shape[0] * steps, shape[1]) if moving == "left" else (shape[0], shape[1] * steps)
        place = (lambda p: (p, 0)) if moving == "left" else (lambda p: (0, p))
        return pl.pallas_call(
            kernel,
            grid=(steps,),
            in_specs=in_specs,
            out_specs=pl.BlockSpec(shape, place),
            out_shape=jax.ShapeDtypeStruct(whole, BF),
            scratch_shapes=scratch,
            **settings,
        )(*mover, *other)

    def kernel_by_place(owners_ref, *refs):
        sent, kept = refs[count + others : count + others + 2]

        def write(step, total):
            @pl.when(step < half)
            def _():
                sent[0] = total

            @pl.when(step >= half)
            def _():
                kept[0] = total

        body(owners_ref, refs[: count + others] + refs[-4:], write)

    return pl.pallas_call(
        kernel_by_place,
        grid_spec=pltpu.PrefetchScalarGridSpec(
            num_scalar_prefetch=1,
            grid=(steps,),
            in_specs=in_specs,
            out_specs=[
                pl.BlockSpec((1,) + shape, lambda p, o: (jnp.minimum(p, half - 1), 0, 0)),
                pl.BlockSpec((1,) + shape, lambda p, o: (jnp.maximum(p - half, 0), 0, 0)),
            ],
            scratch_shapes=scratch,
        ),
        out_shape=[jax.ShapeDtypeStruct((half,) + shape, BF)] * 2,
        **settings,
    )(owner, *mover, *other)


def keep_of(row0, offsets):
    places = row0 + lax.broadcasted_iota(jnp.int32, (SUB, LANES), 0)
    start = places == offsets[0]
    for d in range(1, offsets.shape[0]):
        start = start | (places == offsets[d])
    return jnp.where(start, 0.0, 1.0).astype(F32)


def forward_kernel(order, offsets, pre, before, *rest):
    gated, carry = rest[:-1], rest[-1]
    block = pl.program_id(0)
    rows = pre.shape[1]
    channels = before.shape[2]
    piece = rows // len(gated)

    @pl.when(block == 0)
    def _():
        carry[...] = jnp.zeros_like(carry)

    row_id = lax.broadcasted_iota(jnp.int32, (SUB, LANES), 0)

    def step(i, _, p):
        local = pl.multiple_of(i * 2 * SUB, 2 * SUB)
        base = pl.multiple_of(p * piece + i * 2 * SUB, 2 * SUB)
        keeps = [keep_of(block * rows + base + g * SUB, offsets) for g in range(2)]
        for c in range(channels // LANES):
            lanes = pl.ds(c * LANES, LANES)
            state = carry[:, lanes]
            outs = []
            for g in range(2):
                here = pl.ds(base + g * SUB, SUB)
                vin, vforget, vgate = (
                    pre[0, here, pl.ds(k * channels + c * LANES, LANES)] for k in range(3)
                )
                rate = keeps[g] * (LOWER_BOUND + (1.0 - LOWER_BOUND) * sigmoid(vforget))
                drive = (1.0 - rate) * (vin * sigmoid(vin))
                a, b = rate, drive
                for s in (1, 2, 4):
                    inside = row_id >= s
                    a_up = jnp.where(inside, pltpu.roll(a, s, 0), 1.0)
                    b_up = jnp.where(inside, pltpu.roll(b, s, 0), 0.0)
                    b = a * b_up + b
                    a = a * a_up
                whole = b + a * state
                before[0, here, lanes] = jnp.where(row_id == 0, state, pltpu.roll(whole, 1, 0))
                last_a = jnp.broadcast_to(a[SUB - 1 : SUB], (SUB, LANES))
                last_b = jnp.broadcast_to(b[SUB - 1 : SUB], (SUB, LANES))
                state = last_b + last_a * state
                outs.append(whole * (vgate * sigmoid(vgate)))
            carry[:, lanes] = state
            gated[p][0, pl.ds(local, 2 * SUB), lanes] = jnp.concatenate(outs, axis=0).astype(BF)
        return 0

    for p in range(len(gated)):
        lax.fori_loop(0, piece // (2 * SUB), functools.partial(step, p=p), 0)


def backward_kernel(order, offsets, pre, before, *rest):
    pieces = (len(rest) - 2) // 2
    dgated, dpieces, dpre, carry = rest[:pieces], rest[pieces : 2 * pieces], rest[-2], rest[-1]
    step_id = pl.program_id(0)
    block = pl.num_programs(0) - 1 - step_id
    rows = pre.shape[1]
    channels = before.shape[2]
    piece = rows // pieces
    groups = piece // (2 * SUB)

    @pl.when(step_id == 0)
    def _():
        carry[...] = jnp.zeros_like(carry)

    row_id = lax.broadcasted_iota(jnp.int32, (SUB, LANES), 0)

    def step(i, _, p):
        local = pl.multiple_of((groups - 1 - i) * 2 * SUB, 2 * SUB)
        base = pl.multiple_of(p * piece + (groups - 1 - i) * 2 * SUB, 2 * SUB)
        keeps = [keep_of(block * rows + base + g * SUB, offsets) for g in range(2)]
        for c in range(channels // LANES):
            lanes = pl.ds(c * LANES, LANES)
            flow = carry[:, lanes]
            outs = [None, None]
            for g in (1, 0):
                here = pl.ds(base + g * SUB, SUB)
                vin, vforget, vgate = (
                    pre[0, here, pl.ds(k * channels + c * LANES, LANES)] for k in range(3)
                )
                keep, prev = keeps[g], before[0, here, lanes]
                dg = dgated[p][0, pl.ds(local + g * SUB, SUB), lanes]
                s_forget = sigmoid(vforget)
                rate = keep * (LOWER_BOUND + (1.0 - LOWER_BOUND) * s_forget)
                s_in = sigmoid(vin)
                act_in = vin * s_in
                rest_in = 1.0 - rate
                state = rate * prev + rest_in * act_in
                s_gate = sigmoid(vgate)
                x = dg * (vgate * s_gate)
                a, b = rate, rate * x
                for s in (1, 2, 4):
                    inside = row_id < SUB - s
                    a_down = jnp.where(inside, pltpu.roll(a, SUB - s, 0), 1.0)
                    b_down = jnp.where(inside, pltpu.roll(b, SUB - s, 0), 0.0)
                    b = a * b_down + b
                    a = a * a_down
                q = b + a * flow
                carried = x + jnp.where(row_id == SUB - 1, flow, pltpu.roll(q, SUB - 1, 0))
                first_a = jnp.broadcast_to(a[0:1], (SUB, LANES))
                first_b = jnp.broadcast_to(b[0:1], (SUB, LANES))
                flow = first_b + first_a * flow
                d_in = carried * rest_in * (s_in * (1.0 + vin * (1.0 - s_in)))
                d_forget = (
                    carried
                    * (prev - act_in)
                    * keep
                    * ((1.0 - LOWER_BOUND) * s_forget * (1.0 - s_forget))
                )
                d_gate = dg * state * (s_gate * (1.0 + vgate * (1.0 - s_gate)))
                outs[g] = (d_in, d_forget, d_gate)
            carry[:, lanes] = flow
            for k in range(3):
                value = jnp.concatenate([outs[0][k], outs[1][k]], axis=0).astype(BF)
                at = pl.ds(k * channels + c * LANES, LANES)
                dpre[0, pl.ds(base, 2 * SUB), at] = value
                dpieces[p][0, pl.ds(local, 2 * SUB), at] = value
        return 0

    for p in reversed(range(pieces)):
        lax.fori_loop(0, groups, functools.partial(step, p=p), 0)


def recurrence_call(kernel, order, offsets, operands, outs, channels, name):
    blocks, rows = operands[0].shape[:2]

    def spec(v):
        return pl.BlockSpec((1,) + v.shape[1:], lambda a, o, f: (o[a], 0, 0))

    return pl.pallas_call(
        kernel,
        grid_spec=pltpu.PrefetchScalarGridSpec(
            num_scalar_prefetch=2,
            grid=(blocks,),
            in_specs=[spec(v) for v in operands],
            out_specs=[spec(v) for v in outs],
            scratch_shapes=[pltpu.VMEM((SUB, channels), F32)],
        ),
        out_shape=outs,
        compiler_params=pltpu.CompilerParams(vmem_limit_bytes=48 * 2**20),
        cost_estimate=pl.CostEstimate(
            flops=blocks * rows * channels * 15000,
            bytes_accessed=blocks * rows * channels * 4 * 6,
            transcendentals=blocks * rows * channels * 3,
        ),
        name=name,
    )(order, offsets, *operands)


def unit(values):
    scaling = lax.rsqrt(jnp.mean(values * values, axis=-1, keepdims=True) + RMS_EPSILON)
    return values * scaling, scaling


def norm_backward(d_normed, unit_rows, scaling, gain):
    d_unit = d_normed * gain
    d_values = scaling * (d_unit - unit_rows * jnp.mean(d_unit * unit_rows, axis=-1, keepdims=True))
    return d_values, jnp.sum(d_normed * unit_rows, axis=0)


def adam_moments(grad, weight, first, second, decay_rate):
    first_next = BETA_ONE * first + (1.0 - BETA_ONE) * grad
    second_next = BETA_TWO * second + (1.0 - BETA_TWO) * grad * grad
    update = (
        first_next
        / (1.0 - BETA_ONE**STEP)
        / (jnp.sqrt(second_next / (1.0 - BETA_TWO**STEP)) + ADAM_EPSILON)
        + decay_rate * weight
    )
    return (first_next, second_next, update)


def total_over_mesh(values, n_dp, n_tensor):
    for axis, size in (("tensor", n_tensor), ("dp", n_dp)):
        offset = 1
        while offset < size:
            values = values + exchange(values, axis, size, offset)
            offset *= 2
    return values


def per_device(
    n_dp,
    n_tensor,
    tokens,
    cotangent,
    doc_lengths,
    mix_in,
    mix_out,
    ffn_in,
    ffn_out,
    gains,
    mix_in_m,
    mix_out_m,
    ffn_in_m,
    ffn_out_m,
    gains_m,
    mix_in_v,
    mix_out_v,
    ffn_in_v,
    ffn_out_v,
    gains_v,
):
    rows, width = tokens.shape
    depth = mix_in.shape[1]
    channels = mix_in.shape[2]
    hidden_units = ffn_in.shape[2]
    units = -(-hidden_units // LANES) * LANES
    piece = rows // CHUNKS
    pieces = range(CHUNKS)
    dp_id = lax.axis_index("dp")
    tensor_id = lax.axis_index("tensor")
    near_first = halving(n_dp)
    owner = owners(dp_id, near_first)
    z_first = near_first[1:2] + near_first[:1] + near_first[2:]
    owner_z = owners(dp_id, z_first)
    row_places = offsets_by_place(halving(n_tensor))
    place_of = jnp.array([row_places.index(o) for o in range(n_tensor)], jnp.int32)
    order = place_of[jnp.arange(n_tensor) ^ tensor_id]
    offsets = (jnp.cumsum(doc_lengths[0]) - doc_lengths[0]).astype(jnp.int32)
    sequence = Sequence()
    run = sequence.run

    def cut(i):
        return slice(i * piece, (i + 1) * piece)

    def padded(v):
        return jnp.pad(v, ((0, 0), (0, units - hidden_units)))

    weights = [mix_in[0], mix_in[1], mix_in[2], mix_out, ffn_in[0], ffn_in[1], ffn_out]

    own_mix_in = jnp.concatenate([mix_in[k] for k in range(3)], axis=1).astype(BF)
    halves, scales_one = [], []
    for i in range(2):
        half = tokens[i * (rows // 2) : (i + 1) * (rows // 2)]
        unit_i, scale_i = unit(after(half, own_mix_in).astype(F32))
        halves.append((unit_i * gains[0]).astype(BF))
        scales_one.append(scale_i)
    scale_one = jnp.concatenate(scales_one, axis=0)
    far_offsets = offsets_by_place(near_first)[1 : n_dp // 2]
    early = sorted(far_offsets, key=lambda o: (o & near_first[1] == 0, o))
    early, late = early[: len(early) // 2 + 1], early[len(early) // 2 + 1 :]
    all_offsets = [0] + far_offsets
    owner_far = [dp_id ^ j for j in all_offsets]
    owner_near = [dp_id ^ j ^ 1 for j in all_offsets]

    def distant(half):
        held, offset = [half], n_tensor // 2
        while offset > 1:
            held = held + [exchange(part, "tensor", n_tensor, offset) for part in held]
            offset //= 2
        return held

    far = {j: exchange(own_mix_in, "dp", n_dp, j) for j in early}
    near = {0: exchange(own_mix_in, "dp", n_dp, 1)}
    far_a = distant(halves[0])
    first = lax.optimization_barrier((far_a, near, far))
    far_a, near, far = first
    own_ffn_in = jnp.concatenate([padded(ffn_in[k].astype(BF)) for k in range(2)], axis=1)
    far.update({j: exchange(after(own_mix_in, far_a[0]), "dp", n_dp, j) for j in late})
    near.update({j: exchange(far[j], "dp", n_dp, 1) for j in early})
    own_b = after(halves[1], far_a[0])
    far_b = distant(own_b)
    weight_sq = jnp.stack([jnp.sum(w * w) for w in [after(weights[0], far_a[0])] + weights[1:]])
    second = lax.optimization_barrier((far_a, far_b, near, far, weight_sq, own_ffn_in))
    far_a, far_b, near, far, weight_sq, own_ffn_in = second
    near.update({j: exchange(far[j], "dp", n_dp, 1) for j in late})
    near_a = [exchange(part, "tensor", n_tensor, 1) for part in far_a]
    near_b = [exchange(part, "tensor", n_tensor, 1) for part in far_b]
    known = [(dp_id, after(own_mix_in, far_a[0]))] + [(dp_id ^ j, far[j]) for j in far_offsets]
    known += [(dp_id ^ j ^ 1, near[j]) for j in [0] + early]
    w_mix_in = jnp.zeros((width, 3 * channels), BF)
    for place, block in known:
        w_mix_in = lax.dynamic_update_slice(w_mix_in, block, (place * depth, 0))
    own_mix_out = after(mix_out.astype(BF).T, *near_a, *near_b)
    far_mo = [own_mix_out] + [exchange(own_mix_out, "dp", n_dp, j) for j in far_offsets]
    third = lax.optimization_barrier(
        (near_a, near_b, w_mix_in, own_ffn_in, [near[j] for j in late], far_mo)
    )
    near_a, near_b, w_mix_in, own_ffn_in, last, far_mo = third
    w_ffn_in = lax.all_gather(own_ffn_in, "dp", axis=0, tiled=True)
    w_ffn_out = lax.all_gather(padded(ffn_out.astype(BF).T), "dp", axis=0, tiled=True)
    cots = [Gathered(after(cotangent[cut(0)], near_b[0]), n_tensor)]
    for j, block in zip(late, last):
        w_mix_in = lax.dynamic_update_slice(w_mix_in, block, ((dp_id ^ j ^ 1) * depth, 0))
    sequence.last = near_b[0]
    whole_one = [v for pair in zip(far_a + near_a, far_b + near_b) for v in pair]
    near_mo = [exchange(block, "dp", n_dp, 1) for block in far_mo]
    (pre,) = run(
        lambda w, *parts: row_tiles(
            pre_kernel,
            parts,
            w,
            [],
            [jax.ShapeDtypeStruct((n_tensor * rows, 3 * channels), F32)],
            2 * n_tensor * rows * width * 3 * channels,
            "pre",
        ),
        w_mix_in,
        *whole_one,
    )
    pre = pre.reshape(n_tensor, rows, 3 * channels)
    scanned = recurrence_call(
        forward_kernel,
        order,
        offsets,
        [after(pre, sequence.last)],
        [jax.ShapeDtypeStruct((n_tensor, rows, channels), F32)]
        + [jax.ShapeDtypeStruct((n_tensor, piece, channels), BF)] * CHUNKS,
        channels,
        "recurrence_forward",
    )
    before, gated = scanned[0], scanned[1:]
    sequence.last = before

    w_mix_out = run(
        lambda *blocks: spread(blocks, owner_far + owner_near), far_mo[0], *far_mo[1:], *near_mo
    )

    sums = [
        SummedRows(sequence, gated[i].reshape(-1, channels), w_mix_out, n_tensor, piece) for i in pieces
    ]
    (cots[0].held[1],) = sequence.pin(cots[0].held[1])
    for i in pieces:
        sums[i].high()
    for i in pieces:
        sums[i].rest()
    comings = sequence.pin(*[v.coming for v in sums])

    def middle_of(kept, coming, own):
        middle = own.astype(F32) + kept + coming.astype(F32)
        unit_rows, scaling = unit(middle)
        return (unit_rows * gains[1]).astype(BF), middle, scaling

    middle, scale_two, whole_two = [], [], []
    for i in pieces:
        normed_i, middle_i, scale_i = run(middle_of, sums[i].kept, comings[i], tokens[cut(i)])
        middle.append(middle_i)
        scale_two.append(scale_i)
        if i > 0:
            normed_i = after(normed_i, whole_two[i - 1].held[1])
        whole_two.append(Gathered(normed_i, n_tensor))
    hidden, slope, act = [], [], []
    many = n_tensor * piece
    flops = 2 * many * width * units
    whole_two[0].relay()
    one = jax.ShapeDtypeStruct((many // 2, units), BF)
    for i in pieces:
        if i > 0:
            whole_two[i].relay(sequence.last)
        halves = [
            run(
                lambda w, *parts: row_tiles(
                    gate_up_kernel, parts, w, [], [one] * 3, flops, "gate_up"
                ),
                w_ffn_in,
                *parts,
            )
            for parts in (whole_two[i].held, whole_two[i].near)
        ]
        if i > 0:
            cots[i].relay(sequence.last)
        elif CHUNKS > 1:
            cots[0].relay(sequence.last)
            cots.append(
                Gathered(after(cotangent[cut(1)], whole_two[1].held[1], sequence.last), n_tensor)
            )
        hidden.append((halves[0][0], halves[1][0]))
        slope.append((halves[0][1], halves[1][1]))
        act.append((halves[0][2], halves[1][2]))

    def listed(chunks):
        return [part for gathered in chunks for part in gathered.parts()]

    def grad(lefts, rights, *settings, **more):
        def call(*values):
            return grad_kernel(values[: len(lefts)], values[len(lefts) :], *settings, **more)

        return run(call, *lefts, *rights)

    def flat(pairs):
        return [v for pair in pairs for v in pair]

    grad_fo = grad(flat(hidden), listed(cots), "right", min(256, depth), "grad_out")
    grad_fo = lax.psum_scatter(grad_fo, "dp", scatter_dimension=1, tiled=True)

    def gate_up_back(i, half):
        (d,) = run(
            lambda w, v, a, *parts: row_tiles(
                gate_up_back_kernel,
                parts,
                w,
                [v, a],
                [jax.ShapeDtypeStruct((many // 2, 2 * units), BF)],
                flops // 2,
                "gate_up_back",
            ),
            w_ffn_out,
            slope[i][half],
            act[i][half],
            *(cots[i].near if half else cots[i].held),
        )
        return d

    sums = [SummedRows(sequence, None, w_ffn_in, n_tensor, piece) for i in pieces]
    downs = [SummedRows(sequence, h, w_ffn_out, n_tensor, piece) for h in hidden]
    upper = []
    for i in pieces:
        upper.append(gate_up_back(i, 1))
        sums[i].operand = (None, upper[i])
        sums[i].high()
    d_two = []
    for i in pieces:
        lower = gate_up_back(i, 0)
        d_two.append((lower, upper[i]))
        sums[i].operand = lower
        sums[i].rest()
    for i in pieces:
        downs[i].high()
    (grad_fo,) = sequence.pin(grad_fo)
    grad_fi = grad(listed(whole_two), flat(d_two), "left", min(256, depth), "grad_in")
    grad_fi = lax.psum_scatter(grad_fi, "dp", scatter_dimension=0, tiled=True)
    comings = sequence.pin(*[v.coming for v in sums])

    def middle_back(kept, coming, mid, scaling, cot):
        unit_rows = mid * scaling
        d_norm, gain = norm_backward(kept + coming.astype(F32), unit_rows, scaling, gains[1])
        d_mid = cot.astype(F32) + d_norm
        return d_mid.astype(BF), d_mid, gain

    d_middle, gain_two, lows, whole_d = [], 0.0, [], []
    for i in pieces:
        low, d_mid, gain_i = run(
            middle_back, sums[i].kept, comings[i], middle[i], scale_two[i], cotangent[cut(i)]
        )
        d_middle.append(d_mid)
        gain_two = gain_two + gain_i
        lows.append(low)
    whole_d.append(Gathered(lows[0], n_tensor))
    for i in pieces:
        downs[i].rest()
    for i in range(1, CHUNKS):
        whole_d.append(
            Gathered(after(lows[i], whole_d[i - 1].held[1], sequence.last), n_tensor)
        )
    for gathered in whole_d:
        gathered.relay(sequence.last)

    d_gated = []
    for i in pieces:
        (d_i,) = run(
            lambda w, *parts: row_tiles(
                pre_kernel,
                parts,
                w,
                [],
                [jax.ShapeDtypeStruct((many, channels), F32)],
                2 * many * width * channels,
                "d_gated",
            ),
            w_mix_out,
            *whole_d[i].parts(),
        )
        d_gated.append(d_i.reshape(n_tensor, piece, channels))
    scanned = recurrence_call(
        backward_kernel,
        order[::-1],
        offsets,
        [pre, before, *d_gated[:-1], after(d_gated[-1], sequence.last)],
        [jax.ShapeDtypeStruct((n_tensor, piece, 3 * channels), BF)] * CHUNKS
        + [jax.ShapeDtypeStruct((n_tensor, rows, 3 * channels), BF)],
        channels,
        "recurrence_backward",
    )
    d_pieces, d_pre = scanned[:-1], scanned[-1]
    sequence.last = d_pre
    d_flat = d_pre.reshape(n_tensor * rows, 3 * channels)
    sums_one = [
        SummedRows(sequence, d.reshape(-1, 3 * channels), w_mix_in, n_tensor, piece) for d in d_pieces
    ]
    grad_mi = []

    def grad_mix_in(k):
        halves = grad(
            whole_one, [d_flat], "left", depth, "grad_mix_in", fixed=(k, 3), owner=owner
        )
        grad_mi.append(SummedGrad(sequence, halves, n_dp, near_first))

    def grad_mix_out():
        halves = grad(
            [g.reshape(-1, channels) for g in gated],
            listed(whole_d),
            "right",
            depth,
            "grad_mix_out",
            owner=owner,
        )
        return SummedGrad(sequence, halves, n_dp, near_first)

    moments = [None] * 7

    def lamb(at, grad):
        tall, wide = weights[at].shape

        def call(kept, *coming):
            if coming:
                total = kept[0].astype(F32) + coming[0][0].astype(F32)
            else:
                total = kept.astype(F32)
            first, second, update = adam_moments(
                total[:tall, :wide], weights[at], firsts[at], seconds[at], WEIGHT_DECAY
            )
            return update, first, second, jnp.sum(update * update)

        if isinstance(grad, SummedGrad):
            grad.steps()
            update, first, second, square = run(call, grad.kept, grad.coming)
        else:
            update, first, second, square = run(call, grad)
        moments[at] = (first, second, update, square)

    firsts = [mix_in_m[0], mix_in_m[1], mix_in_m[2], mix_out_m, ffn_in_m[0], ffn_in_m[1], ffn_out_m]
    seconds = [mix_in_v[0], mix_in_v[1], mix_in_v[2], mix_out_v, ffn_in_v[0], ffn_in_v[1], ffn_out_v]
    grad_mix_in(0)
    for i in pieces:
        sums_one[i].high()
    grad_mix_in(1)
    sums_one[0].rest()
    grad_mi[0].step()
    grad_mix_in(2)
    for i in range(1, CHUNKS):
        sums_one[i].rest()
    grad_mi[1].step()
    grad_mi[0].step()
    grad_mo = grad_mix_out()
    mixed = run(
        lambda *parts: jnp.concatenate(
            [
                m + k + c.astype(F32)
                for m, k, c in zip(parts[:CHUNKS], parts[CHUNKS : 2 * CHUNKS], parts[2 * CHUNKS :])
            ],
            axis=0,
        ).astype(BF),
        *middle,
        *[v.kept for v in downs],
        *[v.coming for v in downs],
    )
    lamb(6, grad_fo)
    grad_mi[1].step()

    def input_back(kept, coming, own, scaling, d_mid):
        unit_rows = own.astype(F32) * scaling
        d_norm, gain = norm_backward(kept + coming.astype(F32), unit_rows, scaling, gains[0])
        return d_mid + d_norm, gain

    input_grad, gain_one = [], 0.0
    for i in pieces:
        at = cut(i)
        grad_i, gain_i = run(
            input_back, sums_one[i].kept, sums_one[i].coming, tokens[at], scale_one[at], d_middle[i]
        )
        gain_one = gain_one + gain_i
        input_grad.append(grad_i)
        if i == 0:
            lamb(0, grad_mi[0])
            grad_mo.step()
            grad_mi[2].step()
    input_grad = jnp.concatenate(input_grad, axis=0)
    gain_grads = jnp.stack([gain_one, gain_two])
    grad_mo.step()
    lamb(1, grad_mi[1])
    lamb(4, grad_fi[:, :units])
    lamb(5, grad_fi[:, units:])
    lamb(2, grad_mi[2])
    lamb(3, grad_mo)
    squares = jnp.concatenate([weight_sq, jnp.stack([m[3] for m in moments])])
    packed = jnp.concatenate([gain_grads.reshape(-1), jnp.pad(squares, (0, SUB * LANES - 14))])
    packed = total_over_mesh(packed.reshape(-1, LANES), n_dp, n_tensor).reshape(-1)
    gain_grads = packed[: 2 * width].reshape(2, width)
    squares = packed[2 * width : 2 * width + 14].reshape(2, 7)
    gn_first, gn_second, gn_update = adam_moments(gain_grads, gains, gains_m, gains_v, 0.0)
    weight_sq = jnp.concatenate([squares[0], jnp.sum(gains * gains, axis=1)])
    update_sq = jnp.concatenate([squares[1], jnp.sum(gn_update * gn_update, axis=1)])
    trust = jnp.sqrt(weight_sq) / jnp.sqrt(update_sq + NORM_EPSILON)
    nexts = [w - LEARN_RATE * trust[i] * moments[i][2] for i, w in enumerate(weights)]
    gains_next = gains - LEARN_RATE * trust[7:9][:, None] * gn_update
    layer_norms = jnp.stack([jnp.sqrt(weight_sq), jnp.sqrt(update_sq)])

    def grouped(values):
        return (jnp.stack(values[0:3]), values[3], jnp.stack(values[4:6]), values[6])

    return (
        (mixed, input_grad)
        + grouped(nexts)
        + (gains_next,)
        + grouped([m[0] for m in moments])
        + (gn_first,)
        + grouped([m[1] for m in moments])
        + (gn_second,)
        + grouped([n.astype(BF) for n in nexts])
        + (layer_norms,)
    )


def solution(mesh):
    rows = P(("dp", "tensor"), None)
    inner = P(None, "dp", "tensor")
    outer = P("tensor", "dp")
    matrices = (inner, outer, inner, outer)
    in_specs = (rows, rows, P("dp", None)) + (matrices + (P(),)) * 3
    out_specs = (rows, rows) + (matrices + (P(),)) * 3 + matrices + (P(),)
    body = functools.partial(per_device, mesh.shape["dp"], mesh.shape["tensor"])
    return jax.shard_map(
        body, mesh=mesh, in_specs=in_specs, out_specs=out_specs, check_vma=False
    )
```

```python
import functools

import jax
import jax.numpy as jnp
from jax import lax
from jax.experimental import pallas as pl
from jax.experimental.pallas import tpu as pltpu
from jax.sharding import PartitionSpec as P

STEP = 10
LOWER_BOUND = 0.8
RMS_EPSILON = 1e-06
BETA_ONE = 0.9
BETA_TWO = 0.999
ADAM_EPSILON = 1e-06
WEIGHT_DECAY = 0.01
LEARN_RATE = 0.5
NORM_EPSILON = 1e-12
CHUNKS = 2
BF = jnp.bfloat16
F32 = jnp.float32
LANES = 128
SUB = 8


def likely_flops(flops):
    return int(1.6 * flops) + 4_000_000_000


def exchange(value, axis, size, offset):
    return lax.ppermute(value, axis, [(i, i ^ offset) for i in range(size)])


def after(value, *others):
    return lax.optimization_barrier((value,) + others)[0]


def mm(a, b):
    return jnp.dot(a, b, preferred_element_type=F32)


def mm_nt(a, b):
    return lax.dot_general(a, b, (((1,), (1,)), ((), ())), preferred_element_type=F32)


def mm_tn(a, b):
    return lax.dot_general(a, b, (((0,), (0,)), ((), ())), preferred_element_type=F32)


class Sequence:
    def __init__(self):
        self.last = None
        self.held = {}

    def run(self, call, *operands):
        if self.last is not None:
            operands = (after(operands[0], self.last),) + operands[1:]
        result = call(*operands)
        self.last = jax.tree.leaves(result)[0]
        return result

    def close(self, **named):
        names = list(named)
        out = lax.optimization_barrier(tuple(named[n] for n in names) + (self.last,))
        self.last = jax.tree.leaves(out[0])[0]
        self.held.update(zip(names, out[:-1]))

    def __getattr__(self, name):
        return self.__dict__["held"][name]


def halving(n):
    offsets, offset = [], 1
    while offset < n:
        offsets.append(offset)
        offset *= 2
    return offsets


def offsets_by_place(exchanges):
    offsets = [0]
    for offset in reversed(exchanges):
        offsets = offsets + [o ^ offset for o in offsets]
    return offsets


def owners(index, exchanges):
    return jnp.stack([index ^ o for o in offsets_by_place(exchanges)]).astype(jnp.int32)


def spread(blocks, owner):
    rows, columns = blocks[0].shape
    whole = jnp.zeros((rows * len(blocks), columns), blocks[0].dtype)
    for p, block in enumerate(blocks):
        whole = lax.dynamic_update_slice(whole, block, (owner[p] * rows, 0))
    return whole


def halves_added(kept, coming):
    total = (kept.astype(F32) + coming.astype(F32)).astype(BF)
    half = total.shape[0] // 2
    return total[half:], total[:half]


def near_added(operand, weight, near):
    rows, depth = operand.shape[0] // 2, operand.shape[1]
    width = weight.shape[0]
    tile = rows // 2
    outs = [jax.ShapeDtypeStruct((tile, width), BF), jax.ShapeDtypeStruct((tile, width), F32)]
    settings = dict(
        out_shape=outs,
        compiler_params=pltpu.CompilerParams(vmem_limit_bytes=56 * 2**20),
        cost_estimate=pl.CostEstimate(
            flops=likely_flops(2 * rows * weight.size), bytes_accessed=2 * weight.size, transcendentals=0
        ),
        name="near_added",
    )
    if depth >= width:
        wide = min(256, width)

        def by_columns(v, w, added, far, kept):
            total = mm_nt(v[...], w[...])
            far[...] = (total[tile:] + added[tile:, :].astype(F32)).astype(BF)
            kept[...] = total[:tile] + added[:tile, :].astype(F32)

        def columns(height):
            return pl.BlockSpec((height, wide), lambda j: (0, j))

        return pl.pallas_call(
            by_columns,
            grid=(width // wide,),
            in_specs=[
                pl.BlockSpec((rows, depth), lambda j: (0, 0), pipeline_mode=pl.Buffered(1)),
                pl.BlockSpec((wide, depth), lambda j: (j, 0)),
                columns(rows),
            ],
            out_specs=[columns(tile)] * 2,
            **settings,
        )(operand, weight, near)

    def by_rows(v, w, n, far, kept):
        step = pl.program_id(0)
        total = mm_nt(v[...], w[...]) + n[...].astype(F32)

        @pl.when(step == 0)
        def _():
            far[...] = total.astype(BF)

        @pl.when(step == 1)
        def _():
            kept[...] = total

    def rowed(v):
        return pl.BlockSpec((tile, v.shape[1]), lambda i: (1 - i, 0))

    fixed = pl.BlockSpec((tile, width), lambda i: (0, 0))
    return pl.pallas_call(
        by_rows,
        grid=(2,),
        in_specs=[
            rowed(operand),
            pl.BlockSpec(weight.shape, lambda i: (0, 0), pipeline_mode=pl.Buffered(1)),
            rowed(near),
        ],
        out_specs=[fixed, fixed],
        **settings,
    )(operand, weight, near)


def sigmoid(v):
    return 0.5 * jnp.tanh(0.5 * v) + 0.5


def gate_up_kernel(x, w, hidden, slope, act):
    units = hidden.shape[1]
    for n in range(0, units, 256):
        at = slice(n, min(n + 256, units))
        up_at = slice(units + n, units + min(n + 256, units))
        gate = jnp.dot(x[...], w[:, at], preferred_element_type=F32)
        up = jnp.dot(x[...], w[:, up_at], preferred_element_type=F32)
        s = sigmoid(gate)
        a = gate * s
        hidden[:, at] = (a * up).astype(BF)
        act[:, at] = a.astype(BF)
        slope[:, at] = (up * (s * (1.0 + gate * (1.0 - s)))).astype(BF)


def gate_up_back_kernel(c, w, slope, act, out):
    units = slope.shape[1]
    for n in range(0, units, 256):
        at = slice(n, min(n + 256, units))
        up_at = slice(units + n, units + min(n + 256, units))
        d = jnp.dot(c[...], w[:, at], preferred_element_type=F32)
        out[:, at] = (d * slope[:, at].astype(F32)).astype(BF)
        out[:, up_at] = (d * act[:, at].astype(F32)).astype(BF)


def pre_kernel(x, w, out):
    out[...] = jnp.dot(x[...], w[...], preferred_element_type=F32)


def row_tiles(kernel, parts, weight, others, outs, flops, name):
    count = len(parts)
    tile, depth = parts[0].shape

    def body(*refs):
        sources, w, rest = refs[:count], refs[count], refs[count + 1 : -2]
        buffer, arrived = refs[-2:]
        step = pl.program_id(0)

        def copy(p):
            return pltpu.make_async_copy(sources[p], buffer.at[p % 2], arrived.at[p % 2])

        @pl.when(step == 0)
        def _():
            copy(0).start()

        for p in range(count):

            @pl.when(step == p)
            def _(p=p):
                if p + 1 < count:
                    copy(p + 1).start()
                copy(p).wait()

        kernel(buffer.at[lax.rem(step, 2)], w, *rest)

    def spec(v):
        return pl.BlockSpec((tile, v.shape[1]), lambda i: (i, 0))

    return pl.pallas_call(
        body,
        grid=(count,),
        in_specs=[pl.BlockSpec(memory_space=pl.ANY)] * count
        + [pl.BlockSpec(weight.shape, lambda i: (0, 0), pipeline_mode=pl.Buffered(1))]
        + [spec(v) for v in others],
        out_specs=[spec(v) for v in outs],
        out_shape=outs,
        scratch_shapes=[pltpu.VMEM((2, tile, depth), BF), pltpu.SemaphoreType.DMA((2,))],
        compiler_params=pltpu.CompilerParams(vmem_limit_bytes=56 * 2**20),
        cost_estimate=pl.CostEstimate(
            flops=likely_flops(flops), bytes_accessed=weight.size * 4, transcendentals=0
        ),
        name=name,
    )(*parts, weight, *others)


def grad_kernel(lefts, rights, moving, wide, name, fixed=(0, 1), owner=None):
    part, parts = fixed
    part, span = part if isinstance(part, tuple) else (part, 1)
    mover, other = (lefts, rights) if moving == "left" else (rights, lefts)
    rows = sum(v.shape[0] for v in mover)
    steps = mover[0].shape[1] // wide
    held = other[0].shape[1] // parts * span
    begin = other[0].shape[1] // parts * part
    shape = (wide, held) if moving == "left" else (held, wide)
    half = steps // 2
    count, others = len(mover), len(other)

    def body(owners_ref, sources, write):
        movers, fixers = sources[:count], sources[count : count + others]
        moved, kept, arrived, ready = sources[-4:]
        step = pl.program_id(0)

        def copies(at, slot):
            column = at if owners_ref is None else owners_ref[lax.rem(at + half, steps)]
            columns = pl.ds(pl.multiple_of(column * wide, wide), wide)
            made, row = [], 0
            for p, source in enumerate(movers):
                size = source.shape[0]
                made.append(
                    pltpu.make_async_copy(
                        source.at[:, columns],
                        moved.at[slot, pl.ds(row, size), :],
                        arrived.at[slot, p],
                    )
                )
                row += size
            return made

        def fixed_copies():
            made, row = [], 0
            for p, source in enumerate(fixers):
                size = source.shape[0]
                made.append(
                    pltpu.make_async_copy(
                        source.at[:, pl.ds(begin, held)],
                        kept.at[pl.ds(row, size), :],
                        ready.at[p],
                    )
                )
                row += size
            return made

        @pl.when(step == 0)
        def _():
            for copy in copies(0, 0) + fixed_copies():
                copy.start()

        slot = lax.rem(step, 2)

        @pl.when(step + 1 < steps)
        def _():
            for copy in copies(step + 1, 1 - slot):
                copy.start()

        for copy in copies(step, slot):
            copy.wait()

        @pl.when(step == 0)
        def _():
            for copy in fixed_copies():
                copy.wait()

        pair = (moved[slot], kept[...]) if moving == "left" else (kept[...], moved[slot])
        total = lax.dot_general(
            *pair, (((0,), (0,)), ((), ())), preferred_element_type=F32
        ).astype(BF)
        write(step, total)

    settings = dict(
        compiler_params=pltpu.CompilerParams(vmem_limit_bytes=56 * 2**20),
        cost_estimate=pl.CostEstimate(
            flops=likely_flops(2 * steps * shape[0] * shape[1] * rows),
            bytes_accessed=2 * steps * shape[0] * shape[1],
            transcendentals=0,
        ),
        name=name,
    )
    in_specs = [pl.BlockSpec(memory_space=pl.ANY)] * (count + others)
    scratch = [
        pltpu.VMEM((2, rows, wide), BF),
        pltpu.VMEM((rows, held), BF),
        pltpu.SemaphoreType.DMA((2, count)),
        pltpu.SemaphoreType.DMA((others,)),
    ]
    if owner is None:

        def kernel(*refs):
            out = refs[count + others]

            def write(step, total):
                out[...] = total

            body(None, refs[: count + others] + refs[-4:], write)

        whole = (shape[0] * steps, shape[1]) if moving == "left" else (shape[0], shape[1] * steps)
        place = (lambda p: (p, 0)) if moving == "left" else (lambda p: (0, p))
        return pl.pallas_call(
            kernel,
            grid=(steps,),
            in_specs=in_specs,
            out_specs=pl.BlockSpec(shape, place),
            out_shape=jax.ShapeDtypeStruct(whole, BF),
            scratch_shapes=scratch,
            **settings,
        )(*mover, *other)

    def kernel_by_place(owners_ref, *refs):
        sent, kept = refs[count + others : count + others + 2]

        def write(step, total):
            @pl.when(step < half)
            def _():
                sent[0] = total

            @pl.when(step >= half)
            def _():
                kept[0] = total

        body(owners_ref, refs[: count + others] + refs[-4:], write)

    return pl.pallas_call(
        kernel_by_place,
        grid_spec=pltpu.PrefetchScalarGridSpec(
            num_scalar_prefetch=1,
            grid=(steps,),
            in_specs=in_specs,
            out_specs=[
                pl.BlockSpec((1,) + shape, lambda p, o: (jnp.minimum(p, half - 1), 0, 0)),
                pl.BlockSpec((1,) + shape, lambda p, o: (jnp.maximum(p - half, 0), 0, 0)),
            ],
            scratch_shapes=scratch,
        ),
        out_shape=[jax.ShapeDtypeStruct((half,) + shape, BF)] * 2,
        **settings,
    )(owner, *mover, *other)


def keep_of(row0, offsets):
    places = row0 + lax.broadcasted_iota(jnp.int32, (SUB, LANES), 0)
    start = places == offsets[0]
    for d in range(1, offsets.shape[0]):
        start = start | (places == offsets[d])
    return jnp.where(start, 0.0, 1.0).astype(F32)


def forward_kernel(order, offsets, pre, before, *rest):
    gated, carry = rest[:-1], rest[-1]
    block = pl.program_id(0)
    rows = pre.shape[1]
    channels = before.shape[2]
    piece = rows // len(gated)

    @pl.when(block == 0)
    def _():
        carry[...] = jnp.zeros_like(carry)

    row_id = lax.broadcasted_iota(jnp.int32, (SUB, LANES), 0)

    def step(i, _, p):
        local = pl.multiple_of(i * 2 * SUB, 2 * SUB)
        base = pl.multiple_of(p * piece + i * 2 * SUB, 2 * SUB)
        keeps = [keep_of(block * rows + base + g * SUB, offsets) for g in range(2)]
        for c in range(channels // LANES):
            lanes = pl.ds(c * LANES, LANES)
            state = carry[:, lanes]
            outs = []
            for g in range(2):
                here = pl.ds(base + g * SUB, SUB)
                vin, vforget, vgate = (
                    pre[0, here, pl.ds(k * channels + c * LANES, LANES)] for k in range(3)
                )
                rate = keeps[g] * (LOWER_BOUND + (1.0 - LOWER_BOUND) * sigmoid(vforget))
                drive = (1.0 - rate) * (vin * sigmoid(vin))
                a, b = rate, drive
                for s in (1, 2, 4):
                    inside = row_id >= s
                    a_up = jnp.where(inside, pltpu.roll(a, s, 0), 1.0)
                    b_up = jnp.where(inside, pltpu.roll(b, s, 0), 0.0)
                    b = a * b_up + b
                    a = a * a_up
                whole = b + a * state
                before[0, here, lanes] = jnp.where(row_id == 0, state, pltpu.roll(whole, 1, 0))
                last_a = jnp.broadcast_to(a[SUB - 1 : SUB], (SUB, LANES))
                last_b = jnp.broadcast_to(b[SUB - 1 : SUB], (SUB, LANES))
                state = last_b + last_a * state
                outs.append(whole * (vgate * sigmoid(vgate)))
            carry[:, lanes] = state
            gated[p][0, pl.ds(local, 2 * SUB), lanes] = jnp.concatenate(outs, axis=0).astype(BF)
        return 0

    for p in range(len(gated)):
        lax.fori_loop(0, piece // (2 * SUB), functools.partial(step, p=p), 0)


def backward_kernel(order, offsets, pre, before, *rest):
    pieces = (len(rest) - 1) // 2
    dgated, dpieces, carry = rest[:pieces], rest[pieces : 2 * pieces], rest[-1]
    step_id = pl.program_id(0)
    block = pl.num_programs(0) - 1 - step_id
    rows = pre.shape[1]
    channels = before.shape[2]
    piece = rows // pieces
    groups = piece // (2 * SUB)

    @pl.when(step_id == 0)
    def _():
        carry[...] = jnp.zeros_like(carry)

    row_id = lax.broadcasted_iota(jnp.int32, (SUB, LANES), 0)

    def step(i, _, p):
        local = pl.multiple_of((groups - 1 - i) * 2 * SUB, 2 * SUB)
        base = pl.multiple_of(p * piece + (groups - 1 - i) * 2 * SUB, 2 * SUB)
        keeps = [keep_of(block * rows + base + g * SUB, offsets) for g in range(2)]
        for c in range(channels // LANES):
            lanes = pl.ds(c * LANES, LANES)
            flow = carry[:, lanes]
            outs = [None, None]
            for g in (1, 0):
                here = pl.ds(base + g * SUB, SUB)
                vin, vforget, vgate = (
                    pre[0, here, pl.ds(k * channels + c * LANES, LANES)] for k in range(3)
                )
                keep, prev = keeps[g], before[0, here, lanes]
                dg = dgated[p][0, pl.ds(local + g * SUB, SUB), lanes]
                s_forget = sigmoid(vforget)
                rate = keep * (LOWER_BOUND + (1.0 - LOWER_BOUND) * s_forget)
                s_in = sigmoid(vin)
                act_in = vin * s_in
                rest_in = 1.0 - rate
                state = rate * prev + rest_in * act_in
                s_gate = sigmoid(vgate)
                x = dg * (vgate * s_gate)
                a, b = rate, rate * x
                for s in (1, 2, 4):
                    inside = row_id < SUB - s
                    a_down = jnp.where(inside, pltpu.roll(a, SUB - s, 0), 1.0)
                    b_down = jnp.where(inside, pltpu.roll(b, SUB - s, 0), 0.0)
                    b = a * b_down + b
                    a = a * a_down
                q = b + a * flow
                carried = x + jnp.where(row_id == SUB - 1, flow, pltpu.roll(q, SUB - 1, 0))
                first_a = jnp.broadcast_to(a[0:1], (SUB, LANES))
                first_b = jnp.broadcast_to(b[0:1], (SUB, LANES))
                flow = first_b + first_a * flow
                d_in = carried * rest_in * (s_in * (1.0 + vin * (1.0 - s_in)))
                d_forget = (
                    carried
                    * (prev - act_in)
                    * keep
                    * ((1.0 - LOWER_BOUND) * s_forget * (1.0 - s_forget))
                )
                d_gate = dg * state * (s_gate * (1.0 + vgate * (1.0 - s_gate)))
                outs[g] = (d_in, d_forget, d_gate)
            carry[:, lanes] = flow
            for k in range(3):
                value = jnp.concatenate([outs[0][k], outs[1][k]], axis=0).astype(BF)
                at = pl.ds(k * channels + c * LANES, LANES)
                dpieces[p][0, pl.ds(local, 2 * SUB), at] = value
        return 0

    for p in reversed(range(pieces)):
        lax.fori_loop(0, groups, functools.partial(step, p=p), 0)


def recurrence_call(kernel, order, offsets, operands, outs, channels, name):
    blocks, rows = operands[0].shape[:2]

    def spec(v):
        return pl.BlockSpec((1,) + v.shape[1:], lambda a, o, f: (o[a], 0, 0))

    return pl.pallas_call(
        kernel,
        grid_spec=pltpu.PrefetchScalarGridSpec(
            num_scalar_prefetch=2,
            grid=(blocks,),
            in_specs=[spec(v) for v in operands],
            out_specs=[spec(v) for v in outs],
            scratch_shapes=[pltpu.VMEM((SUB, channels), F32)],
        ),
        out_shape=outs,
        compiler_params=pltpu.CompilerParams(vmem_limit_bytes=48 * 2**20),
        cost_estimate=pl.CostEstimate(
            flops=blocks * rows * channels * 15000,
            bytes_accessed=blocks * rows * channels * 4 * 6,
            transcendentals=blocks * rows * channels * 3,
        ),
        name=name,
    )(order, offsets, *operands)


def unit(values):
    scaling = lax.rsqrt(jnp.mean(values * values, axis=-1, keepdims=True) + RMS_EPSILON)
    return values * scaling, scaling


def norm_backward(d_normed, unit_rows, scaling, gain):
    d_unit = d_normed * gain
    d_values = scaling * (d_unit - unit_rows * jnp.mean(d_unit * unit_rows, axis=-1, keepdims=True))
    return d_values, jnp.sum(d_normed * unit_rows, axis=0)


def adam_moments(grad, weight, first, second, decay_rate):
    first_next = BETA_ONE * first + (1.0 - BETA_ONE) * grad
    second_next = BETA_TWO * second + (1.0 - BETA_TWO) * grad * grad
    update = (
        first_next
        / (1.0 - BETA_ONE**STEP)
        / (jnp.sqrt(second_next / (1.0 - BETA_TWO**STEP)) + ADAM_EPSILON)
        + decay_rate * weight
    )
    return (first_next, second_next, update)


def total_over_mesh(values, n_dp, n_tensor):
    for axis, size, offsets in (
        ("tensor", n_tensor, (1, 2)),
        ("tensor", n_tensor, (4, 8)),
        ("dp", n_dp, (1,)),
        ("dp", n_dp, (2, 4)),
        ("dp", n_dp, (8,)),
    ):
        offsets = [o for o in offsets if o < size]
        if len(offsets) == 2:
            one, two = offsets
            parts = [exchange(values, axis, size, o) for o in (one, two, one + two)]
            values = (values + parts[0]) + (parts[1] + parts[2])
        elif offsets:
            values = values + exchange(values, axis, size, offsets[0])
    return values


def new_weights(steps, weights, updates):
    tiles = weights[3].shape[0] // 176
    counts = [v.shape[0] if v.ndim == 3 else 0 for v in weights]

    def kernel(factor, *refs):
        olds, changes, news, copies = refs[:4], refs[4:11], refs[11:15], refs[15:]
        n = 0
        for old, new, copy, count in zip(olds, news, copies, counts):
            for k in range(max(count, 1)):
                at = (k,) if count else Ellipsis
                value = old[at] - factor[n] * changes[n][...]
                new[at] = value
                copy[at] = value.astype(BF)
                n += 1

    def spec(v):
        if v.ndim == 3:
            return pl.BlockSpec((v.shape[0], v.shape[1] // tiles, v.shape[2]), lambda i, f: (0, i, 0))
        return pl.BlockSpec((v.shape[0] // tiles, v.shape[1]), lambda i, f: (i, 0))

    outs = pl.pallas_call(
        kernel,
        grid_spec=pltpu.PrefetchScalarGridSpec(
            num_scalar_prefetch=1,
            grid=(tiles,),
            in_specs=[spec(v) for v in weights] + [spec(v) for v in updates],
            out_specs=[spec(v) for v in weights] * 2,
        ),
        out_shape=[jax.ShapeDtypeStruct(v.shape, F32) for v in weights]
        + [jax.ShapeDtypeStruct(v.shape, BF) for v in weights],
        compiler_params=pltpu.CompilerParams(vmem_limit_bytes=60 * 2**20),
        name="new_weights",
    )(steps, *weights, *updates)
    return outs[:4], outs[4:]


def per_device(
    n_dp,
    n_tensor,
    tokens,
    cotangent,
    doc_lengths,
    mix_in,
    mix_out,
    ffn_in,
    ffn_out,
    gains,
    mix_in_m,
    mix_out_m,
    ffn_in_m,
    ffn_out_m,
    gains_m,
    mix_in_v,
    mix_out_v,
    ffn_in_v,
    ffn_out_v,
    gains_v,
):
    rows, width = tokens.shape
    depth = mix_in.shape[1]
    channels = mix_in.shape[2]
    hidden_units = ffn_in.shape[2]
    units = -(-hidden_units // LANES) * LANES
    piece = rows // CHUNKS
    pieces = range(CHUNKS)
    dp_id = lax.axis_index("dp")
    tensor_id = lax.axis_index("tensor")
    near_first = halving(n_dp)
    owner = owners(dp_id, near_first)
    row_places = offsets_by_place(halving(n_tensor))
    place_of = jnp.array([row_places.index(o) for o in range(n_tensor)], jnp.int32)
    order = place_of[jnp.arange(n_tensor) ^ tensor_id]
    offsets = (jnp.cumsum(doc_lengths[0]) - doc_lengths[0]).astype(jnp.int32)
    q = Sequence()
    run = q.run

    def cut(i):
        return slice(i * piece, (i + 1) * piece)

    def padded(v):
        return jnp.pad(v, ((0, 0), (0, units - hidden_units)))

    weights = [mix_in[0], mix_in[1], mix_in[2], mix_out, ffn_in[0], ffn_in[1], ffn_out]

    own_mix_in = jnp.concatenate([mix_in[k] for k in range(3)], axis=1).astype(BF)
    halves, scales_one = [], []
    for i in range(2):
        half = tokens[i * (rows // 2) : (i + 1) * (rows // 2)]
        unit_i, scale_i = unit(after(half, own_mix_in).astype(F32))
        halves.append((unit_i * gains[0]).astype(BF))
        scales_one.append(scale_i)
    scale_one = jnp.concatenate(scales_one, axis=0)
    far_offsets = offsets_by_place(near_first)[1 : n_dp // 2]
    early = sorted(far_offsets, key=lambda o: (o & near_first[1] == 0, o))
    early, late = early[: len(early) // 2 + 1], early[len(early) // 2 + 1 :]
    all_offsets = [0] + far_offsets
    owner_far = [dp_id ^ j for j in all_offsets]
    owner_near = [dp_id ^ j ^ 1 for j in all_offsets]

    def distant(half):
        held, offset = [half], n_tensor // 2
        while offset > 1:
            held = held + [exchange(part, "tensor", n_tensor, offset) for part in held]
            offset //= 2
        return held

    far = {j: exchange(own_mix_in, "dp", n_dp, j) for j in early}
    near = {0: exchange(own_mix_in, "dp", n_dp, 1)}
    far_a = distant(halves[0])
    first = lax.optimization_barrier((far_a, near, far, own_mix_in, halves[1]))
    far_a, near, far, own_mix_in, own_b = first
    own_ffn_in = jnp.concatenate([padded(ffn_in[k].astype(BF)) for k in range(2)], axis=1)
    far.update({j: exchange(own_mix_in, "dp", n_dp, j) for j in late})
    near.update({j: exchange(far[j], "dp", n_dp, 1) for j in early})
    far_b = distant(own_b)
    near_a = [exchange(far_a[0], "tensor", n_tensor, 1)]
    near_b = [exchange(after(own_b, near_a[0]), "tensor", n_tensor, 1)]
    second = lax.optimization_barrier(
        (far_a, far_b, near, far, own_ffn_in, near_a, near_b, mix_out.astype(BF).T, own_mix_in)
    )
    far_a, far_b, near, far, own_ffn_in, near_a, near_b, own_mix_out, own_mix_in = second
    near.update({j: exchange(far[j], "dp", n_dp, 1) for j in late})
    near_a += [exchange(part, "tensor", n_tensor, 1) for part in far_a[1:]]
    near_b += [exchange(after(part, near_a[-1]), "tensor", n_tensor, 1) for part in far_b[1:]]
    known = [(dp_id, own_mix_in)] + [(dp_id ^ j, far[j]) for j in far_offsets]
    known += [(dp_id ^ j ^ 1, near[j]) for j in [0] + early]
    w_mix_in = jnp.zeros((width, 3 * channels), BF)
    for place, block in known:
        w_mix_in = lax.dynamic_update_slice(w_mix_in, block, (place * depth, 0))
    far_mo = [own_mix_out] + [exchange(own_mix_out, "dp", n_dp, j) for j in far_offsets]
    third = lax.optimization_barrier(
        (near_a, near_b, w_mix_in, own_ffn_in, [near[j] for j in late], far_mo, cotangent)
    )
    near_a, near_b, w_mix_in, own_ffn_in, last, far_mo, cot_all = third
    q.last = near_b[0]

    def far_rows(own):
        return distant(own)[1:]

    def to_core(parts):
        return [exchange(part, "tensor", n_tensor, 1) for part in parts]

    def to_far(rows_sent):
        return exchange(rows_sent, "tensor", n_tensor, 2)

    def landed(kept, coming):
        places, offset = n_tensor // 4, 2
        while places > 1:
            total = kept + coming.astype(F32)
            offset, places = 2 * offset, places // 2
            kept = total[: places * piece]
            coming = exchange(total[places * piece :].astype(BF), "tensor", n_tensor, offset)
        return kept, coming

    def upper(operand, weight):
        half = operand.shape[0] // 2
        return run(lambda v, w: mm_nt(v[half:], w).astype(BF), operand, weight)

    def lower(operand, weight, near):
        return run(near_added, operand, weight, near)

    def add_halves(kept, coming):
        return run(halves_added, kept, coming)

    w_ffn_in = lax.all_gather(own_ffn_in, "dp", axis=0, tiled=True)
    cot_own = [cot_all[cut(i)] for i in pieces]
    cot_far = far_rows(cot_own[0])
    near_mo = exchange(jnp.concatenate(far_mo, axis=0), "dp", n_dp, 1)
    for j, block in zip(late, last):
        w_mix_in = lax.dynamic_update_slice(w_mix_in, block, ((dp_id ^ j ^ 1) * depth, 0))
    whole_one = [v for pair in zip(far_a + near_a, far_b + near_b) for v in pair]
    (pre,) = run(
        lambda w, *parts: row_tiles(
            pre_kernel,
            parts,
            w,
            [],
            [jax.ShapeDtypeStruct((n_tensor * rows, 3 * channels), F32)],
            2 * n_tensor * rows * width * 3 * channels,
            "pre",
        ),
        w_mix_in,
        *whole_one,
    )
    q.close(pre=pre.reshape(n_tensor, rows, 3 * channels), cot0=cot_far, cot_own1=cot_own[1])

    cot_far = far_rows(q.cot_own1)
    cot0_near = to_core([cot_own[0]] + q.cot0)
    scanned = recurrence_call(
        forward_kernel,
        order,
        offsets,
        [q.pre],
        [jax.ShapeDtypeStruct((n_tensor, rows, channels), F32)]
        + [jax.ShapeDtypeStruct((n_tensor, piece, channels), BF)] * CHUNKS,
        channels,
        "recurrence_forward",
    )
    q.last = scanned[0]
    mo_blocks = far_mo + [near_mo[p * depth : (p + 1) * depth] for p in range(len(far_mo))]
    w_mix_out = run(lambda *blocks: spread(blocks, owner_far + owner_near), *mo_blocks)
    gated = [v.reshape(-1, channels) for v in scanned[1:]]
    q.close(
        up0=upper(gated[0], w_mix_out),
        w_mo=w_mix_out,
        gated=gated,
        before=scanned[0],
        cot0_near=cot0_near,
    )
    cot_parts = [[cot_own[0]] + q.cot0 + q.cot0_near]

    (near0,) = to_core([q.up0])
    q.close(up1=upper(q.gated[1], q.w_mo), near0=near0)

    (near1,) = to_core([q.up1])
    far0, kept0 = lower(q.gated[0], q.w_mo, q.near0)
    q.close(far0=far0, kept0=kept0, near1=near1, cot1=cot_far)

    coming0 = to_far(q.far0)
    cot1_near = to_core([cot_own[1]] + q.cot1)
    far1, kept1 = lower(q.gated[1], q.w_mo, q.near1)
    q.close(far1=far1, kept1=kept1, coming0=coming0, cot1_near=cot1_near)
    cot_parts.append([cot_own[1]] + q.cot1 + q.cot1_near)

    coming1 = to_far(q.far1)

    def middle_of(kept, coming, own):
        middle = own.astype(F32) + kept + coming.astype(F32)
        unit_rows, scaling = unit(middle)
        return (unit_rows * gains[1]).astype(BF), middle, scaling

    normed0, middle0, scale0 = run(middle_of, *landed(q.kept0, q.coming0), tokens[cut(0)])
    q.close(coming1=coming1, normed0=normed0, middle0=middle0, scale0=scale0, w_ffn_in=w_ffn_in)
    w_ffn_out = lax.all_gather(
        after(padded(ffn_out.astype(BF).T), q.w_ffn_in), "dp", axis=0, tiled=True
    )
    normed_far = far_rows(q.normed0)
    normed1, middle1, scale1 = run(middle_of, *landed(q.kept1, q.coming1), tokens[cut(1)])
    weight_sq = run(lambda *ws: jnp.stack([jnp.sum(w * w) for w in ws]), *weights)
    q.close(
        normed1=normed1, middle1=middle1, scale1=scale1, normed0_far=normed_far, weight_sq=weight_sq
    )
    weight_sq = q.weight_sq
    middle, scale_two = [q.middle0, q.middle1], [q.scale0, q.scale1]

    many = n_tensor * piece
    flops = 2 * many * width * units
    one = jax.ShapeDtypeStruct((many, units), BF)

    def gate_up(parts):
        return run(
            lambda w, *parts: row_tiles(
                gate_up_kernel, parts, w, [], [one] * 3, 2 * flops, "gate_up"
            ),
            q.w_ffn_in,
            *parts,
        )

    normed_far = far_rows(q.normed1)
    normed0 = [q.normed0] + q.normed0_far
    whole_two = normed0 + to_core(normed0)
    out0 = gate_up(whole_two)
    q.close(out0=out0, normed1_far=normed_far)
    normed1 = [q.normed1] + q.normed1_far
    parts1 = normed1 + to_core(normed1)
    out1 = gate_up(parts1)
    whole_two = whole_two + parts1
    hidden = [q.out0[0], out1[0]]

    def grad(lefts, rights, *settings, **more):
        def call(*values):
            return grad_kernel(values[: len(lefts)], values[len(lefts) :], *settings, **more)

        return run(call, *lefts, *rights)

    wide = min(256, depth)
    grad_fo = grad(hidden, cot_parts[0] + cot_parts[1], "right", wide, "grad_out")
    q.close(grad_fo=grad_fo, out1=out1)
    hidden = [q.out0[0], q.out1[0]]

    def gate_up_back(i):
        out = (q.out0, q.out1)[i]
        (d,) = run(
            lambda w, v, a, *parts: row_tiles(
                gate_up_back_kernel,
                parts,
                w,
                [v, a],
                [jax.ShapeDtypeStruct((many, 2 * units), BF)],
                flops,
                "gate_up_back",
            ),
            w_ffn_out,
            out[1],
            out[2],
            *cot_parts[i],
        )
        return d

    d0 = gate_up_back(0)
    q.close(up0=upper(d0, q.w_ffn_in), d0=d0, grad_fo=q.grad_fo)

    sum_fo = lax.psum_scatter(q.grad_fo, "dp", scatter_dimension=1, tiled=True)
    (near0,) = to_core([q.up0])
    d1 = gate_up_back(1)
    up1 = upper(d1, q.w_ffn_in)
    far0, kept0 = lower(q.d0, q.w_ffn_in, near0)
    q.close(far0=far0, kept0=kept0, up1=up1, d1=d1, w_ffn_out=w_ffn_out)

    coming0 = to_far(q.far0)
    (near1,) = to_core([q.up1])
    down0 = upper(hidden[0], q.w_ffn_out)
    down1 = upper(hidden[1], q.w_ffn_out)
    far1, kept1 = lower(q.d1, q.w_ffn_in, near1)
    q.close(far1=far1, kept1=kept1, coming0=coming0, down0=down0, down1=down1)

    def middle_back(kept, coming, mid, scaling, cot):
        unit_rows = mid * scaling
        d_norm, gain = norm_backward(kept + coming.astype(F32), unit_rows, scaling, gains[1])
        d_mid = cot.astype(F32) + d_norm
        return d_mid.astype(BF), d_mid, gain

    def grad_in(part):
        return grad(whole_two, [q.d0, q.d1], "left", wide, "grad_in", fixed=(part, 2))

    def sum_in(value):
        return lax.psum_scatter(value, "dp", scatter_dimension=0, tiled=True)

    coming1 = to_far(q.far1)
    down_near = to_core([q.down0, q.down1])
    back0 = run(
        middle_back, *landed(q.kept0, q.coming0), middle[0], scale_two[0], cotangent[cut(0)]
    )
    grad_fg = grad_in(0)
    q.close(
        coming1=coming1, back0=back0, grad_fg=grad_fg, down_near=down_near, sum_fo=sum_fo
    )

    low_far = far_rows(q.back0[0])
    sum_fg = sum_in(q.grad_fg)
    back1 = run(
        middle_back, *landed(q.kept1, q.coming1), middle[1], scale_two[1], cotangent[cut(1)]
    )
    grad_fu = grad_in(1)
    q.close(back1=back1, grad_fu=grad_fu, low0_far=low_far)

    def d_gated_of(parts):
        (d,) = run(
            lambda w, *parts: row_tiles(
                pre_kernel,
                parts,
                w,
                [],
                [jax.ShapeDtypeStruct((many, channels), F32)],
                2 * many * width * channels,
                "d_gated",
            ),
            q.w_mo,
            *parts,
        )
        return d.reshape(n_tensor, piece, channels)

    low_far = far_rows(q.back1[0])
    low0 = [q.back0[0]] + q.low0_far
    whole_d0 = low0 + to_core(low0)
    low1_near = to_core([q.back1[0]])
    down_far0, down_kept0 = lower(hidden[0], q.w_ffn_out, q.down_near[0])
    down_far1, down_kept1 = lower(hidden[1], q.w_ffn_out, q.down_near[1])
    d_gated0 = d_gated_of(whole_d0)
    q.close(
        d_gated0=d_gated0,
        low1_far=low_far,
        low1_near=low1_near,
        whole_d0=whole_d0,
        down_far=[down_far0, down_far1],
        down_kept=[down_kept0, down_kept1],
    )

    down_coming0 = to_far(q.down_far[0])
    whole_d1 = [q.back1[0]] + q.low1_far + q.low1_near + to_core(q.low1_far)
    d_gated1 = d_gated_of(whole_d1)
    scanned = recurrence_call(
        backward_kernel,
        order[::-1],
        offsets,
        [q.pre, q.before, q.d_gated0, d_gated1],
        [jax.ShapeDtypeStruct((n_tensor, piece, 3 * channels), BF)] * CHUNKS,
        channels,
        "recurrence_backward",
    )
    q.last = scanned[-1]
    q.close(scanned=scanned, whole_d1=whole_d1, down_coming0=down_coming0, sum_fg=sum_fg)
    d_pieces = [v.reshape(-1, 3 * channels) for v in q.scanned]
    whole_one = far_a + near_a + far_b + near_b

    def grad_mix_in(k):
        return grad(
            whole_one, d_pieces, "left", depth, "grad_mix_in", fixed=(k, 3), owner=owner
        )

    def over_y(halves):
        return exchange(halves[0], "dp", n_dp, 1)

    def over_z(halves, offset):
        return exchange(halves[0], "dp", n_dp, offset)

    def finished(kept, coming, offset):
        while kept.shape[0] > 1:
            sent, kept = halves_added(kept, coming)
            offset *= 2
            coming = exchange(sent, "dp", n_dp, offset)
        return kept, coming

    sum_fu = sum_in(q.grad_fu)
    down_coming1 = to_far(q.down_far[1])
    grad0 = grad_mix_in(0)
    q.close(grad0=grad0)

    y0 = over_y(q.grad0)
    up0 = upper(d_pieces[0], w_mix_in)
    grad1 = grad_mix_in(1)
    q.close(grad1=grad1, up0=up0, y0=y0, down_coming1=down_coming1)

    half0 = add_halves(q.grad0[1], q.y0)
    y1 = over_y(q.grad1)
    z0 = over_z(half0, 2)
    (near0,) = to_core([q.up0])
    up1 = upper(d_pieces[1], w_mix_in)
    grad2 = grad_mix_in(2)
    q.close(grad2=grad2, up1=up1, y1=y1, z0=z0, kept_y0=half0[1], near0=near0)

    y2 = over_y(q.grad2)
    half1 = add_halves(q.grad1[1], q.y1)
    z1 = over_z(half1, 2)
    half0 = add_halves(q.kept_y0, q.z0)
    w0 = over_z(half0, 4)
    (near1,) = to_core([q.up1])
    far0, kept0 = lower(d_pieces[0], w_mix_in, q.near0)
    q.close(far0=far0, kept0=kept0, kept_y1=half1[1], kept_z0=half0[1])

    coming0 = to_far(q.far0)
    grad3 = grad(
        q.gated, q.whole_d0 + q.whole_d1, "right", depth, "grad_mix_out", owner=owner
    )
    far1, kept1 = lower(d_pieces[1], w_mix_in, near1)
    q.close(
        far1=far1, kept1=kept1, coming0=coming0, grad3=grad3, y2=y2, z1=z1, w0=w0
    )

    firsts = [mix_in_m[0], mix_in_m[1], mix_in_m[2], mix_out_m, ffn_in_m[0], ffn_in_m[1], ffn_out_m]
    seconds = [mix_in_v[0], mix_in_v[1], mix_in_v[2], mix_out_v, ffn_in_v[0], ffn_in_v[1], ffn_out_v]
    moments = [None] * 7

    def lamb(at, kept, coming=None):
        tall, wide = weights[at].shape
        if coming is not None:
            kept, coming = finished(kept, coming, 4)

        def call(kept, *coming):
            if coming:
                total = kept[0].astype(F32) + coming[0][0].astype(F32)
            else:
                total = kept.astype(F32)
            first, second, update = adam_moments(
                total[:tall, :wide], weights[at], firsts[at], seconds[at], WEIGHT_DECAY
            )
            return update, first, second, jnp.sum(update * update)

        update, first, second, square = run(call, kept, *([] if coming is None else [coming]))
        moments[at] = (first, second, update, square)

    def input_back(kept, coming, own, scaling, d_mid):
        unit_rows = own.astype(F32) * scaling
        d_norm, gain = norm_backward(kept + coming.astype(F32), unit_rows, scaling, gains[0])
        return d_mid + d_norm, gain

    coming1 = to_far(q.far1)
    half2 = add_halves(q.grad2[1], q.y2)
    y3 = over_y(q.grad3)
    z2 = over_z(half2, 2)
    half1 = add_halves(q.kept_y1, q.z1)
    w1 = over_z(half1, 4)
    input_grad0, gain_one0 = run(
        input_back,
        *landed(q.kept0, q.coming0),
        tokens[cut(0)],
        scale_one[cut(0)],
        q.back0[1],
    )
    lamb(0, q.kept_z0, q.w0)
    lamb(6, q.sum_fo)
    mixed = run(
        lambda *parts: jnp.concatenate(
            [
                m + k + c.astype(F32)
                for m, k, c in zip(parts[:CHUNKS], parts[CHUNKS : 2 * CHUNKS], parts[2 * CHUNKS :])
            ],
            axis=0,
        ).astype(BF),
        *middle,
        *[
            v
            for pair in zip(
                *[
                    landed(k, c)
                    for k, c in zip(q.down_kept, [q.down_coming0, q.down_coming1])
                ]
            )
            for v in pair
        ],
    )
    q.close(
        coming1=coming1,
        y3=y3,
        z2=z2,
        kept_y2=half2[1],
        w1=w1,
        kept_z1=half1[1],
        sum_fu=sum_fu,
    )

    half3 = add_halves(q.grad3[1], q.y3)
    z3 = over_z(half3, 2)
    half2 = add_halves(q.kept_y2, q.z2)
    w2 = over_z(half2, 4)
    input_grad1, gain_one1 = run(
        input_back,
        *landed(q.kept1, q.coming1),
        tokens[cut(1)],
        scale_one[cut(1)],
        q.back1[1],
    )
    lamb(1, q.kept_z1, q.w1)
    q.close(z3=z3, kept_y3=half3[1], w2=w2, kept_z2=half2[1])

    half3 = add_halves(q.kept_y3, q.z3)
    w3 = over_z(half3, 4)
    lamb(4, q.sum_fg)
    lamb(5, q.sum_fu)
    lamb(2, q.kept_z2, q.w2)
    lamb(3, half3[1], w3)
    input_grad = jnp.concatenate([input_grad0, input_grad1], axis=0)
    gain_grads = jnp.stack([gain_one0 + gain_one1, q.back0[2] + q.back1[2]])
    squares = jnp.concatenate([weight_sq, jnp.stack([m[3] for m in moments])])
    packed = jnp.concatenate([gain_grads.reshape(-1), jnp.pad(squares, (0, SUB * LANES - 14))])
    packed = total_over_mesh(packed.reshape(-1, LANES), n_dp, n_tensor).reshape(-1)
    gain_grads = packed[: 2 * width].reshape(2, width)
    squares = packed[2 * width : 2 * width + 14].reshape(2, 7)
    gn_first, gn_second, gn_update = adam_moments(gain_grads, gains, gains_m, gains_v, 0.0)
    weight_sq = jnp.concatenate([squares[0], jnp.sum(gains * gains, axis=1)])
    update_sq = jnp.concatenate([squares[1], jnp.sum(gn_update * gn_update, axis=1)])
    trust = jnp.sqrt(weight_sq) / jnp.sqrt(update_sq + NORM_EPSILON)
    nexts, copies = new_weights(
        LEARN_RATE * trust[0:7], (mix_in, mix_out, ffn_in, ffn_out), [m[2] for m in moments]
    )
    gains_next = gains - LEARN_RATE * trust[7:9][:, None] * gn_update
    layer_norms = jnp.stack([jnp.sqrt(weight_sq), jnp.sqrt(update_sq)])

    def grouped(values):
        return (jnp.stack(values[0:3]), values[3], jnp.stack(values[4:6]), values[6])

    return (
        (mixed, input_grad)
        + tuple(nexts)
        + (gains_next,)
        + grouped([m[0] for m in moments])
        + (gn_first,)
        + grouped([m[1] for m in moments])
        + (gn_second,)
        + tuple(copies)
        + (layer_norms,)
    )


def solution(mesh):
    rows = P(("dp", "tensor"), None)
    inner = P(None, "dp", "tensor")
    outer = P("tensor", "dp")
    matrices = (inner, outer, inner, outer)
    in_specs = (rows, rows, P("dp", None)) + (matrices + (P(),)) * 3
    out_specs = (rows, rows) + (matrices + (P(),)) * 3 + matrices + (P(),)
    body = functools.partial(per_device, mesh.shape["dp"], mesh.shape["tensor"])
    return jax.shard_map(
        body, mesh=mesh, in_specs=in_specs, out_specs=out_specs, check_vma=False
    )
```

```python
import functools

import jax
import jax.numpy as jnp
from jax import lax
from jax.experimental import pallas as pl
from jax.experimental.pallas import tpu as pltpu
from jax.sharding import PartitionSpec as P

STEP = 10
LOWER_BOUND = 0.8
RMS_EPSILON = 1e-06
BETA_ONE = 0.9
BETA_TWO = 0.999
ADAM_EPSILON = 1e-06
WEIGHT_DECAY = 0.01
LEARN_RATE = 0.5
NORM_EPSILON = 1e-12
CHUNKS = 2
BF = jnp.bfloat16
F32 = jnp.float32
LANES = 128
SUB = 8


def likely_flops(flops):
    return int(1.6 * flops) + 4_000_000_000


def exchange(value, axis, size, offset):
    return lax.ppermute(value, axis, [(i, i ^ offset) for i in range(size)])


def after(value, *others):
    return lax.optimization_barrier((value,) + others)[0]


def mm(a, b):
    return jnp.dot(a, b, preferred_element_type=F32)


def mm_nt(a, b):
    return lax.dot_general(a, b, (((1,), (1,)), ((), ())), preferred_element_type=F32)


def mm_tn(a, b):
    return lax.dot_general(a, b, (((0,), (0,)), ((), ())), preferred_element_type=F32)


class Sequence:
    def __init__(self):
        self.last = None
        self.held = {}

    def run(self, call, *operands):
        if self.last is not None:
            operands = (after(operands[0], self.last),) + operands[1:]
        result = call(*operands)
        self.last = jax.tree.leaves(result)[0]
        return result

    def close(self, **named):
        names = list(named)
        out = lax.optimization_barrier(tuple(named[n] for n in names) + (self.last,))
        self.last = jax.tree.leaves(out[0])[0]
        self.held.update(zip(names, out[:-1]))

    def __getattr__(self, name):
        return self.__dict__["held"][name]


def halving(n):
    offsets, offset = [], 1
    while offset < n:
        offsets.append(offset)
        offset *= 2
    return offsets


def offsets_by_place(exchanges):
    offsets = [0]
    for offset in reversed(exchanges):
        offsets = offsets + [o ^ offset for o in offsets]
    return offsets


def owners(index, exchanges):
    return jnp.stack([index ^ o for o in offsets_by_place(exchanges)]).astype(jnp.int32)


def spread(blocks, owner):
    rows, columns = blocks[0].shape
    whole = jnp.zeros((rows * len(blocks), columns), blocks[0].dtype)
    for p, block in enumerate(blocks):
        whole = lax.dynamic_update_slice(whole, block, (owner[p] * rows, 0))
    return whole


def halves_added(kept, coming):
    total = (kept.astype(F32) + coming.astype(F32)).astype(BF)
    half = total.shape[0] // 2
    return total[half:], total[:half]


def near_added(operand, weight, near):
    rows, depth = operand.shape[0] // 2, operand.shape[1]
    width = weight.shape[0]
    tile = rows // 2
    outs = [jax.ShapeDtypeStruct((tile, width), BF), jax.ShapeDtypeStruct((tile, width), F32)]
    settings = dict(
        out_shape=outs,
        compiler_params=pltpu.CompilerParams(vmem_limit_bytes=56 * 2**20),
        cost_estimate=pl.CostEstimate(
            flops=likely_flops(2 * rows * weight.size), bytes_accessed=2 * weight.size, transcendentals=0
        ),
        name="near_added",
    )
    if depth >= width:
        wide = min(256, width)

        def by_columns(v, w, added, far, kept):
            total = mm_nt(v[...], w[...])
            far[...] = (total[tile:] + added[tile:, :].astype(F32)).astype(BF)
            kept[...] = total[:tile] + added[:tile, :].astype(F32)

        def columns(height):
            return pl.BlockSpec((height, wide), lambda j: (0, j))

        return pl.pallas_call(
            by_columns,
            grid=(width // wide,),
            in_specs=[
                pl.BlockSpec((rows, depth), lambda j: (0, 0), pipeline_mode=pl.Buffered(1)),
                pl.BlockSpec((wide, depth), lambda j: (j, 0)),
                columns(rows),
            ],
            out_specs=[columns(tile)] * 2,
            **settings,
        )(operand, weight, near)

    def by_rows(v, w, n, far, kept):
        step = pl.program_id(0)
        total = mm_nt(v[...], w[...]) + n[...].astype(F32)

        @pl.when(step == 0)
        def _():
            far[...] = total.astype(BF)

        @pl.when(step == 1)
        def _():
            kept[...] = total

    def rowed(v):
        return pl.BlockSpec((tile, v.shape[1]), lambda i: (1 - i, 0))

    fixed = pl.BlockSpec((tile, width), lambda i: (0, 0))
    return pl.pallas_call(
        by_rows,
        grid=(2,),
        in_specs=[
            rowed(operand),
            pl.BlockSpec(weight.shape, lambda i: (0, 0), pipeline_mode=pl.Buffered(1)),
            rowed(near),
        ],
        out_specs=[fixed, fixed],
        **settings,
    )(operand, weight, near)


def sigmoid(v):
    return 0.5 * jnp.tanh(0.5 * v) + 0.5


def gate_up_kernel(x, w, hidden, slope, act):
    units = hidden.shape[1]
    for n in range(0, units, 256):
        at = slice(n, min(n + 256, units))
        up_at = slice(units + n, units + min(n + 256, units))
        gate = jnp.dot(x[...], w[:, at], preferred_element_type=F32)
        up = jnp.dot(x[...], w[:, up_at], preferred_element_type=F32)
        s = sigmoid(gate)
        a = gate * s
        hidden[:, at] = (a * up).astype(BF)
        act[:, at] = a.astype(BF)
        slope[:, at] = (up * (s * (1.0 + gate * (1.0 - s)))).astype(BF)


def gate_up_back_kernel(c, w, slope, act, out):
    units = slope.shape[1]
    for n in range(0, units, 256):
        at = slice(n, min(n + 256, units))
        up_at = slice(units + n, units + min(n + 256, units))
        d = jnp.dot(c[...], w[:, at], preferred_element_type=F32)
        out[:, at] = (d * slope[:, at].astype(F32)).astype(BF)
        out[:, up_at] = (d * act[:, at].astype(F32)).astype(BF)


def d_gated_kernel(x, w, out):
    out[...] = jnp.dot(x[...], w[...], preferred_element_type=F32).astype(BF)


def pre_kernel(x, w, rate, act_in, act_gate, slope_in, slope_gate):
    channels = rate.shape[1]

    def silu(v):
        s = sigmoid(v)
        a = v * s
        return a, s + a * (1.0 - s)

    def product(k):
        return jnp.dot(
            x[...], w[:, k * channels : (k + 1) * channels], preferred_element_type=F32
        )

    act, slope = silu(product(0))
    act_in[...] = act
    slope_in[...] = slope.astype(BF)
    rate[...] = LOWER_BOUND + (1.0 - LOWER_BOUND) * sigmoid(product(1))
    act, slope = silu(product(2))
    act_gate[...] = act.astype(BF)
    slope_gate[...] = slope.astype(BF)


def row_tiles(kernel, parts, weight, others, outs, flops, name):
    count = len(parts)
    tile, depth = parts[0].shape

    def body(*refs):
        sources, w, rest = refs[:count], refs[count], refs[count + 1 : -2]
        buffer, arrived = refs[-2:]
        step = pl.program_id(0)

        def copy(p):
            return pltpu.make_async_copy(sources[p], buffer.at[p % 2], arrived.at[p % 2])

        @pl.when(step == 0)
        def _():
            copy(0).start()

        for p in range(count):

            @pl.when(step == p)
            def _(p=p):
                if p + 1 < count:
                    copy(p + 1).start()
                copy(p).wait()

        kernel(buffer.at[lax.rem(step, 2)], w, *rest)

    def spec(v):
        return pl.BlockSpec((tile, v.shape[1]), lambda i: (i, 0))

    return pl.pallas_call(
        body,
        grid=(count,),
        in_specs=[pl.BlockSpec(memory_space=pl.ANY)] * count
        + [pl.BlockSpec(weight.shape, lambda i: (0, 0), pipeline_mode=pl.Buffered(1))]
        + [spec(v) for v in others],
        out_specs=[spec(v) for v in outs],
        out_shape=outs,
        scratch_shapes=[pltpu.VMEM((2, tile, depth), BF), pltpu.SemaphoreType.DMA((2,))],
        compiler_params=pltpu.CompilerParams(vmem_limit_bytes=56 * 2**20),
        cost_estimate=pl.CostEstimate(
            flops=likely_flops(flops), bytes_accessed=weight.size * 4, transcendentals=0
        ),
        name=name,
    )(*parts, weight, *others)


def grad_kernel(lefts, rights, moving, wide, name, fixed=(0, 1), owner=None):
    part, parts = fixed
    part, span = part if isinstance(part, tuple) else (part, 1)
    mover, other = (lefts, rights) if moving == "left" else (rights, lefts)
    rows = sum(v.shape[0] for v in mover)
    steps = mover[0].shape[1] // wide
    held = other[0].shape[1] // parts * span
    begin = other[0].shape[1] // parts * part
    shape = (wide, held) if moving == "left" else (held, wide)
    half = steps // 2
    count, others = len(mover), len(other)

    def body(owners_ref, sources, write):
        movers, fixers = sources[:count], sources[count : count + others]
        moved, kept, arrived, ready = sources[-4:]
        step = pl.program_id(0)

        def copies(at, slot):
            column = at if owners_ref is None else owners_ref[lax.rem(at + half, steps)]
            columns = pl.ds(pl.multiple_of(column * wide, wide), wide)
            made, row = [], 0
            for p, source in enumerate(movers):
                size = source.shape[0]
                made.append(
                    pltpu.make_async_copy(
                        source.at[:, columns],
                        moved.at[slot, pl.ds(row, size), :],
                        arrived.at[slot, p],
                    )
                )
                row += size
            return made

        def fixed_copies():
            made, row = [], 0
            for p, source in enumerate(fixers):
                size = source.shape[0]
                made.append(
                    pltpu.make_async_copy(
                        source.at[:, pl.ds(begin, held)],
                        kept.at[pl.ds(row, size), :],
                        ready.at[p],
                    )
                )
                row += size
            return made

        @pl.when(step == 0)
        def _():
            for copy in copies(0, 0) + fixed_copies():
                copy.start()

        slot = lax.rem(step, 2)

        @pl.when(step + 1 < steps)
        def _():
            for copy in copies(step + 1, 1 - slot):
                copy.start()

        for copy in copies(step, slot):
            copy.wait()

        @pl.when(step == 0)
        def _():
            for copy in fixed_copies():
                copy.wait()

        pair = (moved[slot], kept[...]) if moving == "left" else (kept[...], moved[slot])
        total = lax.dot_general(
            *pair, (((0,), (0,)), ((), ())), preferred_element_type=F32
        ).astype(BF)
        write(step, total)

    settings = dict(
        compiler_params=pltpu.CompilerParams(vmem_limit_bytes=56 * 2**20),
        cost_estimate=pl.CostEstimate(
            flops=likely_flops(2 * steps * shape[0] * shape[1] * rows),
            bytes_accessed=2 * steps * shape[0] * shape[1],
            transcendentals=0,
        ),
        name=name,
    )
    in_specs = [pl.BlockSpec(memory_space=pl.ANY)] * (count + others)
    scratch = [
        pltpu.VMEM((2, rows, wide), BF),
        pltpu.VMEM((rows, held), BF),
        pltpu.SemaphoreType.DMA((2, count)),
        pltpu.SemaphoreType.DMA((others,)),
    ]
    if owner is None:

        def kernel(*refs):
            out = refs[count + others]

            def write(step, total):
                out[...] = total

            body(None, refs[: count + others] + refs[-4:], write)

        whole = (shape[0] * steps, shape[1]) if moving == "left" else (shape[0], shape[1] * steps)
        place = (lambda p: (p, 0)) if moving == "left" else (lambda p: (0, p))
        return pl.pallas_call(
            kernel,
            grid=(steps,),
            in_specs=in_specs,
            out_specs=pl.BlockSpec(shape, place),
            out_shape=jax.ShapeDtypeStruct(whole, BF),
            scratch_shapes=scratch,
            **settings,
        )(*mover, *other)

    def kernel_by_place(owners_ref, *refs):
        sent, kept = refs[count + others : count + others + 2]

        def write(step, total):
            @pl.when(step < half)
            def _():
                sent[0] = total

            @pl.when(step >= half)
            def _():
                kept[0] = total

        body(owners_ref, refs[: count + others] + refs[-4:], write)

    return pl.pallas_call(
        kernel_by_place,
        grid_spec=pltpu.PrefetchScalarGridSpec(
            num_scalar_prefetch=1,
            grid=(steps,),
            in_specs=in_specs,
            out_specs=[
                pl.BlockSpec((1,) + shape, lambda p, o: (jnp.minimum(p, half - 1), 0, 0)),
                pl.BlockSpec((1,) + shape, lambda p, o: (jnp.maximum(p - half, 0), 0, 0)),
            ],
            scratch_shapes=scratch,
        ),
        out_shape=[jax.ShapeDtypeStruct((half,) + shape, BF)] * 2,
        **settings,
    )(owner, *mover, *other)


def keep_of(row0, offsets):
    places = row0 + lax.broadcasted_iota(jnp.int32, (SUB, LANES), 0)
    start = places == offsets[0]
    for d in range(1, offsets.shape[0]):
        start = start | (places == offsets[d])
    return jnp.where(start, 0.0, 1.0).astype(F32)


def forward_kernel(order, offsets, free, act_in, act_gate, before, *rest):
    gated, carry = rest[:-1], rest[-1]
    block = pl.program_id(0)
    rows, channels = free.shape[1:]
    piece = rows // len(gated)

    @pl.when(block == 0)
    def _():
        carry[...] = jnp.zeros_like(carry)

    row_id = lax.broadcasted_iota(jnp.int32, (SUB, LANES), 0)

    def step(i, _, p):
        local = pl.multiple_of(i * 2 * SUB, 2 * SUB)
        base = pl.multiple_of(p * piece + i * 2 * SUB, 2 * SUB)
        keeps = [keep_of(block * rows + base + g * SUB, offsets) for g in range(2)]
        for c in range(channels // LANES):
            lanes = pl.ds(c * LANES, LANES)
            state = carry[:, lanes]
            gates = act_gate[0, pl.ds(base, 2 * SUB), lanes].astype(F32)
            outs = []
            for g in range(2):
                here = pl.ds(base + g * SUB, SUB)
                rate = keeps[g] * free[0, here, lanes]
                a, b = rate, (1.0 - rate) * act_in[0, here, lanes]
                for s in (1, 2, 4):
                    inside = row_id >= s
                    a_up = jnp.where(inside, pltpu.roll(a, s, 0), 1.0)
                    b_up = jnp.where(inside, pltpu.roll(b, s, 0), 0.0)
                    b = a * b_up + b
                    a = a * a_up
                whole = b + a * state
                before[0, here, lanes] = jnp.where(row_id == 0, state, pltpu.roll(whole, 1, 0))
                last_a = jnp.broadcast_to(a[SUB - 1 : SUB], (SUB, LANES))
                last_b = jnp.broadcast_to(b[SUB - 1 : SUB], (SUB, LANES))
                state = last_b + last_a * state
                outs.append(whole * gates[g * SUB : (g + 1) * SUB])
            carry[:, lanes] = state
            gated[p][0, pl.ds(local, 2 * SUB), lanes] = jnp.concatenate(outs, axis=0).astype(BF)
        return 0

    for p in range(len(gated)):
        lax.fori_loop(0, piece // (2 * SUB), functools.partial(step, p=p), 0)


def backward_kernel(
    order, offsets, free, act_in, act_gate, slope_in, slope_gate, before, *rest
):
    pieces = (len(rest) - 1) // 2
    dgated, dpieces, carry = rest[:pieces], rest[pieces : 2 * pieces], rest[-1]
    step_id = pl.program_id(0)
    block = pl.num_programs(0) - 1 - step_id
    rows, channels = free.shape[1:]
    piece = rows // pieces
    groups = piece // (2 * SUB)

    @pl.when(step_id == 0)
    def _():
        carry[...] = jnp.zeros_like(carry)

    row_id = lax.broadcasted_iota(jnp.int32, (SUB, LANES), 0)

    def step(i, _, p):
        local = pl.multiple_of((groups - 1 - i) * 2 * SUB, 2 * SUB)
        base = pl.multiple_of(p * piece + (groups - 1 - i) * 2 * SUB, 2 * SUB)
        keeps = [keep_of(block * rows + base + g * SUB, offsets) for g in range(2)]
        for c in range(channels // LANES):
            lanes = pl.ds(c * LANES, LANES)
            both = pl.ds(base, 2 * SUB)
            flow = carry[:, lanes]
            halves = [
                v.astype(F32)
                for v in (
                    act_gate[0, both, lanes],
                    slope_in[0, both, lanes],
                    slope_gate[0, both, lanes],
                    dgated[p][0, pl.ds(local, 2 * SUB), lanes],
                )
            ]
            outs = [None, None]
            for g in (1, 0):
                here = pl.ds(base + g * SUB, SUB)
                gate, in_slope, gate_slope, dg = [v[g * SUB : (g + 1) * SUB] for v in halves]
                open_rate, act, prev = free[0, here, lanes], act_in[0, here, lanes], before[0, here, lanes]
                keep = keeps[g]
                rate = keep * open_rate
                rest_in = 1.0 - rate
                state = rate * prev + rest_in * act
                x = dg * gate
                a, b = rate, rate * x
                for s in (1, 2, 4):
                    inside = row_id < SUB - s
                    a_down = jnp.where(inside, pltpu.roll(a, SUB - s, 0), 1.0)
                    b_down = jnp.where(inside, pltpu.roll(b, SUB - s, 0), 0.0)
                    b = a * b_down + b
                    a = a * a_down
                q = b + a * flow
                carried = x + jnp.where(row_id == SUB - 1, flow, pltpu.roll(q, SUB - 1, 0))
                first_a = jnp.broadcast_to(a[0:1], (SUB, LANES))
                first_b = jnp.broadcast_to(b[0:1], (SUB, LANES))
                flow = first_b + first_a * flow
                d_in = carried * rest_in * in_slope
                d_forget = (
                    carried
                    * (prev - act)
                    * keep
                    * ((open_rate - LOWER_BOUND) * (1.0 - open_rate) * (1.0 / (1.0 - LOWER_BOUND)))
                )
                d_gate = dg * state * gate_slope
                outs[g] = (d_in, d_forget, d_gate)
            carry[:, lanes] = flow
            for k in range(3):
                value = jnp.concatenate([outs[0][k], outs[1][k]], axis=0).astype(BF)
                at = pl.ds(k * channels + c * LANES, LANES)
                dpieces[p][0, pl.ds(local, 2 * SUB), at] = value
        return 0

    for p in reversed(range(pieces)):
        lax.fori_loop(0, groups, functools.partial(step, p=p), 0)


def recurrence_call(kernel, order, offsets, operands, outs, channels, name):
    blocks, rows = operands[0].shape[:2]

    def spec(v):
        return pl.BlockSpec((1,) + v.shape[1:], lambda a, o, f: (o[a], 0, 0))

    return pl.pallas_call(
        kernel,
        grid_spec=pltpu.PrefetchScalarGridSpec(
            num_scalar_prefetch=2,
            grid=(blocks,),
            in_specs=[spec(v) for v in operands],
            out_specs=[spec(v) for v in outs],
            scratch_shapes=[pltpu.VMEM((SUB, channels), F32)],
        ),
        out_shape=outs,
        compiler_params=pltpu.CompilerParams(vmem_limit_bytes=48 * 2**20),
        cost_estimate=pl.CostEstimate(
            flops=blocks * rows * channels * 15000,
            bytes_accessed=blocks * rows * channels * 4 * 6,
            transcendentals=blocks * rows * channels * 3,
        ),
        name=name,
    )(order, offsets, *operands)


def unit(values):
    scaling = lax.rsqrt(jnp.mean(values * values, axis=-1, keepdims=True) + RMS_EPSILON)
    return values * scaling, scaling


def norm_backward(d_normed, unit_rows, scaling, gain):
    d_unit = d_normed * gain
    d_values = scaling * (d_unit - unit_rows * jnp.mean(d_unit * unit_rows, axis=-1, keepdims=True))
    return d_values, jnp.sum(d_normed * unit_rows, axis=0)


def adam_moments(grad, weight, first, second, decay_rate):
    first_next = BETA_ONE * first + (1.0 - BETA_ONE) * grad
    second_next = BETA_TWO * second + (1.0 - BETA_TWO) * grad * grad
    update = (
        first_next
        / (1.0 - BETA_ONE**STEP)
        / (jnp.sqrt(second_next / (1.0 - BETA_TWO**STEP)) + ADAM_EPSILON)
        + decay_rate * weight
    )
    return (first_next, second_next, update)


def total_over_mesh(values, n_dp, n_tensor):
    for axis, size, offsets in (
        ("tensor", n_tensor, (1, 2)),
        ("tensor", n_tensor, (4, 8)),
        ("dp", n_dp, (1,)),
        ("dp", n_dp, (2, 4)),
        ("dp", n_dp, (8,)),
    ):
        offsets = [o for o in offsets if o < size]
        if len(offsets) == 2:
            one, two = offsets
            parts = [exchange(values, axis, size, o) for o in (one, two, one + two)]
            values = (values + parts[0]) + (parts[1] + parts[2])
        elif offsets:
            values = values + exchange(values, axis, size, offsets[0])
    return values


def new_weights(steps, weights, updates):
    tiles = weights[3].shape[0] // 352
    counts = [v.shape[0] if v.ndim == 3 else 0 for v in weights]

    def kernel(factor, *refs):
        olds, changes, news, copies = refs[:4], refs[4:11], refs[11:15], refs[15:]
        n = 0
        for old, new, copy, count in zip(olds, news, copies, counts):
            for k in range(max(count, 1)):
                at = (k,) if count else Ellipsis
                value = old[at] - factor[n] * changes[n][...]
                new[at] = value
                copy[at] = value.astype(BF)
                n += 1

    def spec(v):
        if v.ndim == 3:
            return pl.BlockSpec((v.shape[0], v.shape[1] // tiles, v.shape[2]), lambda i, f: (0, i, 0))
        return pl.BlockSpec((v.shape[0] // tiles, v.shape[1]), lambda i, f: (i, 0))

    outs = pl.pallas_call(
        kernel,
        grid_spec=pltpu.PrefetchScalarGridSpec(
            num_scalar_prefetch=1,
            grid=(tiles,),
            in_specs=[spec(v) for v in weights] + [spec(v) for v in updates],
            out_specs=[spec(v) for v in weights] * 2,
        ),
        out_shape=[jax.ShapeDtypeStruct(v.shape, F32) for v in weights]
        + [jax.ShapeDtypeStruct(v.shape, BF) for v in weights],
        compiler_params=pltpu.CompilerParams(vmem_limit_bytes=60 * 2**20),
        name="new_weights",
    )(steps, *weights, *updates)
    return outs[:4], outs[4:]


def per_device(
    n_dp,
    n_tensor,
    tokens,
    cotangent,
    doc_lengths,
    mix_in,
    mix_out,
    ffn_in,
    ffn_out,
    gains,
    mix_in_m,
    mix_out_m,
    ffn_in_m,
    ffn_out_m,
    gains_m,
    mix_in_v,
    mix_out_v,
    ffn_in_v,
    ffn_out_v,
    gains_v,
):
    rows, width = tokens.shape
    depth = mix_in.shape[1]
    channels = mix_in.shape[2]
    hidden_units = ffn_in.shape[2]
    units = -(-hidden_units // LANES) * LANES
    piece = rows // CHUNKS
    pieces = range(CHUNKS)
    dp_id = lax.axis_index("dp")
    tensor_id = lax.axis_index("tensor")
    near_first = halving(n_dp)
    owner = owners(dp_id, near_first)
    row_places = offsets_by_place(halving(n_tensor))
    place_of = jnp.array([row_places.index(o) for o in range(n_tensor)], jnp.int32)
    order = place_of[jnp.arange(n_tensor) ^ tensor_id]
    offsets = (jnp.cumsum(doc_lengths[0]) - doc_lengths[0]).astype(jnp.int32)
    q = Sequence()
    run = q.run

    def cut(i):
        return slice(i * piece, (i + 1) * piece)

    def padded(v):
        return jnp.pad(v, ((0, 0), (0, units - hidden_units)))

    weights = [mix_in[0], mix_in[1], mix_in[2], mix_out, ffn_in[0], ffn_in[1], ffn_out]

    own_mix_in = jnp.concatenate([mix_in[k] for k in range(3)], axis=1).astype(BF)
    halves, scales_one = [], []
    for i in range(2):
        half = tokens[i * (rows // 2) : (i + 1) * (rows // 2)]
        unit_i, scale_i = unit(after(half, own_mix_in).astype(F32))
        halves.append((unit_i * gains[0]).astype(BF))
        scales_one.append(scale_i)
    scale_one = jnp.concatenate(scales_one, axis=0)
    far_offsets = offsets_by_place(near_first)[1 : n_dp // 2]
    early = sorted(far_offsets, key=lambda o: (o & near_first[1] == 0, o))
    early, late = early[: len(early) // 2 + 1], early[len(early) // 2 + 1 :]
    all_offsets = [0] + far_offsets
    owner_far = [dp_id ^ j for j in all_offsets]
    owner_near = [dp_id ^ j ^ 1 for j in all_offsets]

    def distant(half):
        held, offset = [half], n_tensor // 2
        while offset > 1:
            held = held + [exchange(part, "tensor", n_tensor, offset) for part in held]
            offset //= 2
        return held

    far = {j: exchange(own_mix_in, "dp", n_dp, j) for j in early}
    near = {0: exchange(own_mix_in, "dp", n_dp, 1)}
    far_a = distant(halves[0])
    first = lax.optimization_barrier((far_a, near, far, own_mix_in, halves[1]))
    far_a, near, far, own_mix_in, own_b = first
    own_ffn_in = jnp.concatenate([padded(ffn_in[k].astype(BF)) for k in range(2)], axis=1)
    far.update({j: exchange(own_mix_in, "dp", n_dp, j) for j in late})
    near.update({j: exchange(far[j], "dp", n_dp, 1) for j in early})
    far_b = distant(own_b)
    near_a = [exchange(far_a[0], "tensor", n_tensor, 1)]
    near_b = [exchange(after(own_b, near_a[0]), "tensor", n_tensor, 1)]
    second = lax.optimization_barrier(
        (far_a, far_b, near, far, own_ffn_in, near_a, near_b, mix_out.astype(BF).T, own_mix_in)
    )
    far_a, far_b, near, far, own_ffn_in, near_a, near_b, own_mix_out, own_mix_in = second
    near.update({j: exchange(far[j], "dp", n_dp, 1) for j in late})
    near_a += [exchange(part, "tensor", n_tensor, 1) for part in far_a[1:]]
    near_b += [exchange(after(part, near_a[-1]), "tensor", n_tensor, 1) for part in far_b[1:]]
    known = [(dp_id, own_mix_in)] + [(dp_id ^ j, far[j]) for j in far_offsets]
    known += [(dp_id ^ j ^ 1, near[j]) for j in [0] + early]
    w_mix_in = jnp.zeros((width, 3 * channels), BF)
    for place, block in known:
        w_mix_in = lax.dynamic_update_slice(w_mix_in, block, (place * depth, 0))
    far_mo = [own_mix_out] + [exchange(own_mix_out, "dp", n_dp, j) for j in far_offsets]
    third = lax.optimization_barrier(
        (near_a, near_b, w_mix_in, own_ffn_in, [near[j] for j in late], far_mo, cotangent)
    )
    near_a, near_b, w_mix_in, own_ffn_in, last, far_mo, cot_all = third
    q.last = near_b[0]

    def far_rows(own):
        return distant(own)[1:]

    def to_core(parts):
        return [exchange(part, "tensor", n_tensor, 1) for part in parts]

    def to_far(rows_sent):
        return exchange(rows_sent, "tensor", n_tensor, 2)

    def landed(kept, coming):
        places, offset = n_tensor // 4, 2
        while places > 1:
            total = kept + coming.astype(F32)
            offset, places = 2 * offset, places // 2
            kept = total[: places * piece]
            coming = exchange(total[places * piece :].astype(BF), "tensor", n_tensor, offset)
        return kept, coming

    def upper(operand, weight):
        half = operand.shape[0] // 2
        return run(lambda v, w: mm_nt(v[half:], w).astype(BF), operand, weight)

    def lower(operand, weight, near):
        return run(near_added, operand, weight, near)

    def add_halves(kept, coming):
        return run(halves_added, kept, coming)

    w_ffn_in = lax.all_gather(own_ffn_in, "dp", axis=0, tiled=True)
    cot_own = [cot_all[cut(i)] for i in pieces]
    cot_far = far_rows(cot_own[0])
    near_mo = exchange(jnp.concatenate(far_mo, axis=0), "dp", n_dp, 1)
    for j, block in zip(late, last):
        w_mix_in = lax.dynamic_update_slice(w_mix_in, block, ((dp_id ^ j ^ 1) * depth, 0))
    whole_one = [v for pair in zip(far_a + near_a, far_b + near_b) for v in pair]
    tall = n_tensor * rows
    pre = run(
        lambda w, *parts: row_tiles(
            pre_kernel,
            parts,
            w,
            [],
            [jax.ShapeDtypeStruct((tall, channels), t) for t in (F32, F32, BF, BF, BF)],
            2 * tall * width * 3 * channels,
            "pre",
        ),
        w_mix_in,
        *whole_one,
    )
    q.close(pre=[v.reshape(n_tensor, rows, channels) for v in pre], cot0=cot_far)

    cot0_near = to_core([cot_own[0]] + q.cot0)
    scanned = recurrence_call(
        forward_kernel,
        order,
        offsets,
        q.pre[:3],
        [jax.ShapeDtypeStruct((n_tensor, rows, channels), F32)]
        + [jax.ShapeDtypeStruct((n_tensor, piece, channels), BF)] * CHUNKS,
        channels,
        "recurrence_forward",
    )
    q.last = scanned[0]
    mo_blocks = far_mo + [near_mo[p * depth : (p + 1) * depth] for p in range(len(far_mo))]
    w_mix_out = run(lambda *blocks: spread(blocks, owner_far + owner_near), *mo_blocks)
    gated = [v.reshape(-1, channels) for v in scanned[1:]]
    q.close(
        up0=upper(gated[0], w_mix_out),
        w_mo=w_mix_out,
        gated=gated,
        before=scanned[0],
        cot0_near=cot0_near,
    )
    cot_parts = [[cot_own[0]] + q.cot0 + q.cot0_near]

    (near0,) = to_core([q.up0])
    q.close(up1=upper(q.gated[1], q.w_mo), near0=near0)

    (near1,) = to_core([q.up1])
    far0, kept0 = lower(q.gated[0], q.w_mo, q.near0)
    q.close(far0=far0, kept0=kept0, near1=near1)

    coming0 = to_far(q.far0)
    far1, kept1 = lower(q.gated[1], q.w_mo, q.near1)
    q.close(far1=far1, kept1=kept1, coming0=coming0)

    coming1 = to_far(q.far1)

    def middle_of(kept, coming, own):
        middle = own.astype(F32) + kept + coming.astype(F32)
        unit_rows, scaling = unit(middle)
        return (unit_rows * gains[1]).astype(BF), middle, scaling

    normed0, middle0, scale0 = run(middle_of, *landed(q.kept0, q.coming0), tokens[cut(0)])
    q.close(coming1=coming1, normed0=normed0, middle0=middle0, scale0=scale0)
    normed_far = far_rows(q.normed0)
    normed_near = to_core([q.normed0])
    normed1, middle1, scale1 = run(middle_of, *landed(q.kept1, q.coming1), tokens[cut(1)])
    weight_sq = run(lambda *ws: jnp.stack([jnp.sum(w * w) for w in ws]), *weights)
    q.close(w_ffn_in=w_ffn_in, weight_sq=weight_sq)
    w_ffn_out = lax.all_gather(
        after(padded(ffn_out.astype(BF).T), q.w_ffn_in), "dp", axis=0, tiled=True
    )
    q.close(
        normed1=normed1, middle1=middle1, scale1=scale1, normed0_far=normed_far, normed0_near=normed_near
    )
    weight_sq = q.weight_sq
    middle, scale_two = [q.middle0, q.middle1], [q.scale0, q.scale1]

    many = n_tensor * piece
    flops = 2 * many * width * units
    one = jax.ShapeDtypeStruct((many, units), BF)

    def gate_up(parts):
        return run(
            lambda w, *parts: row_tiles(
                gate_up_kernel, parts, w, [], [one] * 3, 2 * flops, "gate_up"
            ),
            q.w_ffn_in,
            *parts,
        )

    normed_far = far_rows(q.normed1)
    normed_near = to_core([q.normed1])
    whole_two = [q.normed0] + q.normed0_far + q.normed0_near + to_core(q.normed0_far)
    out0 = gate_up(whole_two)
    q.close(out0=out0, normed1_far=normed_far, normed1_near=normed_near, cot_own1=cot_own[1])
    cot_far = far_rows(q.cot_own1)
    parts1 = [q.normed1] + q.normed1_far + q.normed1_near + to_core(q.normed1_far)
    out1 = gate_up(parts1)
    whole_two = whole_two + parts1
    q.close(out1=out1, cot1=cot_far)
    hidden = [q.out0[0], q.out1[0]]
    cot1 = [q.cot_own1] + q.cot1
    cot_parts.append(cot1 + to_core(cot1))

    def grad(lefts, rights, *settings, **more):
        def call(*values):
            return grad_kernel(values[: len(lefts)], values[len(lefts) :], *settings, **more)

        return run(call, *lefts, *rights)

    wide = min(256, depth)

    def gate_up_back(i):
        out = (q.out0, q.out1)[i]
        (d,) = run(
            lambda w, v, a, *parts: row_tiles(
                gate_up_back_kernel,
                parts,
                w,
                [v, a],
                [jax.ShapeDtypeStruct((many, 2 * units), BF)],
                flops,
                "gate_up_back",
            ),
            w_ffn_out,
            out[1],
            out[2],
            *cot_parts[i],
        )
        return d

    grad_fo = grad(hidden, cot_parts[0] + cot_parts[1], "right", wide, "grad_out")
    q.close(grad_fo=grad_fo)

    sum_fo = lax.psum_scatter(q.grad_fo, "dp", scatter_dimension=1, tiled=True)
    d0 = gate_up_back(0)
    q.close(up0=upper(d0, q.w_ffn_in), d0=d0)

    (near0,) = to_core([q.up0])
    d1 = gate_up_back(1)
    up1 = upper(d1, q.w_ffn_in)
    far0, kept0 = lower(q.d0, q.w_ffn_in, near0)
    q.close(far0=far0, kept0=kept0, up1=up1, d1=d1, w_ffn_out=w_ffn_out)

    coming0 = to_far(q.far0)
    (near1,) = to_core([q.up1])
    down0 = upper(hidden[0], q.w_ffn_out)
    down1 = upper(hidden[1], q.w_ffn_out)
    far1, kept1 = lower(q.d1, q.w_ffn_in, near1)
    q.close(far1=far1, kept1=kept1, coming0=coming0, down0=down0, down1=down1)

    def middle_back(kept, coming, mid, scaling, cot):
        unit_rows = mid * scaling
        d_norm, gain = norm_backward(kept + coming.astype(F32), unit_rows, scaling, gains[1])
        d_mid = cot.astype(F32) + d_norm
        return d_mid.astype(BF), d_mid, gain

    def grad_in(part):
        return grad(whole_two, [q.d0, q.d1], "left", wide, "grad_in", fixed=(part, 2))

    def sum_in(value):
        return lax.psum_scatter(value, "dp", scatter_dimension=0, tiled=True)

    coming1 = to_far(q.far1)
    down_near = to_core([q.down0, q.down1])
    back0 = run(
        middle_back, *landed(q.kept0, q.coming0), middle[0], scale_two[0], cotangent[cut(0)]
    )
    grad_fg = grad_in(0)
    q.close(
        coming1=coming1, back0=back0, grad_fg=grad_fg, down_near=down_near, sum_fo=sum_fo
    )

    low_far = far_rows(q.back0[0])
    sum_fg = sum_in(q.grad_fg)
    back1 = run(
        middle_back, *landed(q.kept1, q.coming1), middle[1], scale_two[1], cotangent[cut(1)]
    )
    grad_fu = grad_in(1)
    q.close(back1=back1, grad_fu=grad_fu, low0_far=low_far)

    def d_gated_of(parts):
        (d,) = run(
            lambda w, *parts: row_tiles(
                d_gated_kernel,
                parts,
                w,
                [],
                [jax.ShapeDtypeStruct((many, channels), BF)],
                2 * many * width * channels,
                "d_gated",
            ),
            q.w_mo,
            *parts,
        )
        return d.reshape(n_tensor, piece, channels)

    low_far = far_rows(q.back1[0])
    low0 = [q.back0[0]] + q.low0_far
    whole_d0 = low0 + to_core(low0)
    low1_near = to_core([q.back1[0]])
    down_far0, down_kept0 = lower(hidden[0], q.w_ffn_out, q.down_near[0])
    down_far1, down_kept1 = lower(hidden[1], q.w_ffn_out, q.down_near[1])
    d_gated0 = d_gated_of(whole_d0)
    q.close(
        d_gated0=d_gated0,
        low1_far=low_far,
        low1_near=low1_near,
        whole_d0=whole_d0,
        down_far=[down_far0, down_far1],
        down_kept=[down_kept0, down_kept1],
    )

    down_coming = [to_far(q.down_far[0]), to_far(q.down_far[1])]

    whole_d1 = [q.back1[0]] + q.low1_far + q.low1_near + to_core(q.low1_far)
    d_gated1 = d_gated_of(whole_d1)
    scanned = recurrence_call(
        backward_kernel,
        order[::-1],
        offsets,
        q.pre + [q.before, q.d_gated0, d_gated1],
        [jax.ShapeDtypeStruct((n_tensor, piece, 3 * channels), BF)] * CHUNKS,
        channels,
        "recurrence_backward",
    )
    q.last = scanned[-1]
    q.close(scanned=scanned, whole_d1=whole_d1, sum_fg=sum_fg, grad_fu=q.grad_fu)
    d_pieces = [v.reshape(-1, 3 * channels) for v in q.scanned]
    whole_one = far_a + near_a + far_b + near_b

    def grad_mix_in(k):
        return grad(
            whole_one, d_pieces, "left", depth, "grad_mix_in", fixed=(k, 3), owner=owner
        )

    def over_y(halves):
        return exchange(halves[0], "dp", n_dp, 1)

    def over_z(halves, offset):
        return exchange(halves[0], "dp", n_dp, offset)

    def finished(kept, coming, offset):
        while kept.shape[0] > 1:
            sent, kept = halves_added(kept, coming)
            offset *= 2
            coming = exchange(sent, "dp", n_dp, offset)
        return kept, coming

    sum_fu = sum_in(q.grad_fu)
    grad0 = grad_mix_in(0)
    q.close(grad0=grad0)

    y0 = over_y(q.grad0)
    up0 = upper(d_pieces[0], w_mix_in)
    grad1 = grad_mix_in(1)
    up1 = upper(d_pieces[1], w_mix_in)
    q.close(grad1=grad1, up0=up0, up1=up1, y0=y0, down_coming=down_coming)

    half0 = add_halves(q.grad0[1], q.y0)
    y1 = over_y(q.grad1)
    z0 = over_z(half0, 2)
    near0, near1 = to_core([q.up0, q.up1])
    grad2 = grad_mix_in(2)
    far0, kept0 = lower(d_pieces[0], w_mix_in, near0)
    q.close(
        grad2=grad2,
        near1=near1,
        y1=y1,
        z0=z0,
        kept_y0=half0[1],
        far0=far0,
        kept0=kept0,
    )

    y2 = over_y(q.grad2)
    half1 = add_halves(q.grad1[1], q.y1)
    z1 = over_z(half1, 2)
    half0 = add_halves(q.kept_y0, q.z0)
    w0 = over_z(half0, 4)
    coming0 = to_far(q.far0)
    grad3 = grad(
        q.gated, q.whole_d0 + q.whole_d1, "right", depth, "grad_mix_out", owner=owner
    )
    far1, kept1 = lower(d_pieces[1], w_mix_in, q.near1)
    q.close(
        far1=far1,
        kept1=kept1,
        sum_fu=sum_fu,
        coming0=coming0,
        grad3=grad3,
        y2=y2,
        z1=z1,
        w0=w0,
        kept_y1=half1[1],
        kept_z0=half0[1],
    )

    firsts = [mix_in_m[0], mix_in_m[1], mix_in_m[2], mix_out_m, ffn_in_m[0], ffn_in_m[1], ffn_out_m]
    seconds = [mix_in_v[0], mix_in_v[1], mix_in_v[2], mix_out_v, ffn_in_v[0], ffn_in_v[1], ffn_out_v]
    moments = [None] * 7

    def lamb(at, kept, coming=None):
        tall, wide = weights[at].shape
        if coming is not None:
            kept, coming = finished(kept, coming, 4)

        def call(kept, *coming):
            if coming:
                total = kept[0].astype(F32) + coming[0][0].astype(F32)
            else:
                total = kept.astype(F32)
            first, second, update = adam_moments(
                total[:tall, :wide], weights[at], firsts[at], seconds[at], WEIGHT_DECAY
            )
            return update, first, second, jnp.sum(update * update)

        update, first, second, square = run(call, kept, *([] if coming is None else [coming]))
        moments[at] = (first, second, update, square)

    def input_back(kept, coming, own, scaling, d_mid):
        unit_rows = own.astype(F32) * scaling
        d_norm, gain = norm_backward(kept + coming.astype(F32), unit_rows, scaling, gains[0])
        return d_mid + d_norm, gain

    coming1 = to_far(q.far1)
    half2 = add_halves(q.grad2[1], q.y2)
    y3 = over_y(q.grad3)
    z2 = over_z(half2, 2)
    half1 = add_halves(q.kept_y1, q.z1)
    w1 = over_z(half1, 4)
    input_grad0, gain_one0 = run(
        input_back,
        *landed(q.kept0, q.coming0),
        tokens[cut(0)],
        scale_one[cut(0)],
        q.back0[1],
    )
    lamb(0, q.kept_z0, q.w0)
    lamb(6, q.sum_fo)
    mixed = run(
        lambda *parts: jnp.concatenate(
            [
                m + k + c.astype(F32)
                for m, k, c in zip(parts[:CHUNKS], parts[CHUNKS : 2 * CHUNKS], parts[2 * CHUNKS :])
            ],
            axis=0,
        ).astype(BF),
        *middle,
        *[
            v
            for pair in zip(
                *[
                    landed(k, c)
                    for k, c in zip(q.down_kept, q.down_coming)
                ]
            )
            for v in pair
        ],
    )
    q.close(
        coming1=coming1,
        y3=y3,
        z2=z2,
        kept_y2=half2[1],
        w1=w1,
        kept_z1=half1[1],
    )

    half3 = add_halves(q.grad3[1], q.y3)
    z3 = over_z(half3, 2)
    half2 = add_halves(q.kept_y2, q.z2)
    w2 = over_z(half2, 4)
    input_grad1, gain_one1 = run(
        input_back,
        *landed(q.kept1, q.coming1),
        tokens[cut(1)],
        scale_one[cut(1)],
        q.back1[1],
    )
    lamb(1, q.kept_z1, q.w1)
    q.close(z3=z3, kept_y3=half3[1], w2=w2, kept_z2=half2[1])

    half3 = add_halves(q.kept_y3, q.z3)
    w3 = over_z(half3, 4)
    lamb(4, q.sum_fg)
    lamb(5, q.sum_fu)
    lamb(2, q.kept_z2, q.w2)
    squares = [weight_sq[i] for i in range(7)] + [m[3] if m else jnp.zeros((), F32) for m in moments]
    packed = run(
        lambda one, *others: jnp.stack(
            [one + others[0], others[1] + others[2], jnp.pad(jnp.stack(others[3:]), (0, width - 14))]
        ),
        gain_one0,
        gain_one1,
        q.back0[2],
        q.back1[2],
        *squares,
    )
    q.close(packed=packed, w3=w3, kept_z3=half3[1])
    lamb(3, q.kept_z3, q.w3)
    input_grad = jnp.concatenate([input_grad0, input_grad1], axis=0)
    place = lax.broadcasted_iota(jnp.int32, (3, width), 1)
    last_row = lax.broadcasted_iota(jnp.int32, (3, width), 0) == 2
    packed = q.packed + jnp.where(last_row & (place == 10), moments[3][3], 0.0)
    packed = total_over_mesh(packed, n_dp, n_tensor)
    gain_grads = packed[:2]
    squares = packed[2, :14].reshape(2, 7)
    gn_first, gn_second, gn_update = adam_moments(gain_grads, gains, gains_m, gains_v, 0.0)
    weight_sq = jnp.concatenate([squares[0], jnp.sum(gains * gains, axis=1)])
    update_sq = jnp.concatenate([squares[1], jnp.sum(gn_update * gn_update, axis=1)])
    trust = jnp.sqrt(weight_sq) / jnp.sqrt(update_sq + NORM_EPSILON)
    nexts, copies = new_weights(
        LEARN_RATE * trust[0:7], (mix_in, mix_out, ffn_in, ffn_out), [m[2] for m in moments]
    )
    gains_next = gains - LEARN_RATE * trust[7:9][:, None] * gn_update
    layer_norms = jnp.stack([jnp.sqrt(weight_sq), jnp.sqrt(update_sq)])

    def grouped(values):
        return (jnp.stack(values[0:3]), values[3], jnp.stack(values[4:6]), values[6])

    return (
        (mixed, input_grad)
        + tuple(nexts)
        + (gains_next,)
        + grouped([m[0] for m in moments])
        + (gn_first,)
        + grouped([m[1] for m in moments])
        + (gn_second,)
        + tuple(copies)
        + (layer_norms,)
    )


def solution(mesh):
    rows = P(("dp", "tensor"), None)
    inner = P(None, "dp", "tensor")
    outer = P("tensor", "dp")
    matrices = (inner, outer, inner, outer)
    in_specs = (rows, rows, P("dp", None)) + (matrices + (P(),)) * 3
    out_specs = (rows, rows) + (matrices + (P(),)) * 3 + matrices + (P(),)
    body = functools.partial(per_device, mesh.shape["dp"], mesh.shape["tensor"])
    return jax.shard_map(
        body, mesh=mesh, in_specs=in_specs, out_specs=out_specs, check_vma=False
    )
```

```python
import functools

import jax
import jax.numpy as jnp
from jax import lax
from jax.experimental import pallas as pl
from jax.experimental.pallas import tpu as pltpu
from jax.sharding import PartitionSpec as P

STEP = 10
LOWER_BOUND = 0.8
RMS_EPSILON = 1e-06
BETA_ONE = 0.9
BETA_TWO = 0.999
ADAM_EPSILON = 1e-06
WEIGHT_DECAY = 0.01
LEARN_RATE = 0.5
NORM_EPSILON = 1e-12
CHUNKS = 2
BF = jnp.bfloat16
F32 = jnp.float32
LANES = 128
SUB = 8


def likely_flops(flops):
    return int(1.6 * flops) + 4_000_000_000


def exchange(value, axis, size, offset):
    return lax.ppermute(value, axis, [(i, i ^ offset) for i in range(size)])


def after(value, *others):
    return lax.optimization_barrier((value,) + others)[0]


def mm(a, b):
    return jnp.dot(a, b, preferred_element_type=F32)


def mm_nt(a, b):
    return lax.dot_general(a, b, (((1,), (1,)), ((), ())), preferred_element_type=F32)


def mm_tn(a, b):
    return lax.dot_general(a, b, (((0,), (0,)), ((), ())), preferred_element_type=F32)


class Sequence:
    def __init__(self):
        self.last = None
        self.held = {}

    def run(self, call, *operands):
        if self.last is not None:
            operands = (after(operands[0], self.last),) + operands[1:]
        result = call(*operands)
        self.last = jax.tree.leaves(result)[0]
        return result

    def close(self, **named):
        names = list(named)
        out = lax.optimization_barrier(tuple(named[n] for n in names) + (self.last,))
        self.last = jax.tree.leaves(out[0])[0]
        self.held.update(zip(names, out[:-1]))

    def __getattr__(self, name):
        return self.__dict__["held"][name]


def halving(n):
    offsets, offset = [], 1
    while offset < n:
        offsets.append(offset)
        offset *= 2
    return offsets


def offsets_by_place(exchanges):
    offsets = [0]
    for offset in reversed(exchanges):
        offsets = offsets + [o ^ offset for o in offsets]
    return offsets


def owners(index, exchanges):
    return jnp.stack([index ^ o for o in offsets_by_place(exchanges)]).astype(jnp.int32)


def spread(blocks, owner):
    rows, columns = blocks[0].shape
    whole = jnp.zeros((rows * len(blocks), columns), blocks[0].dtype)
    for p, block in enumerate(blocks):
        whole = lax.dynamic_update_slice(whole, block, (owner[p] * rows, 0))
    return whole


def halves_added(kept, coming):
    total = (kept.astype(F32) + coming.astype(F32)).astype(BF)
    half = total.shape[0] // 2
    return total[half:], total[:half]


def near_added(operand, weight, near):
    rows, depth = operand.shape[0] // 2, operand.shape[1]
    width = weight.shape[0]
    tile = rows // 2
    outs = [jax.ShapeDtypeStruct((tile, width), BF), jax.ShapeDtypeStruct((tile, width), F32)]
    settings = dict(
        out_shape=outs,
        compiler_params=pltpu.CompilerParams(vmem_limit_bytes=56 * 2**20),
        cost_estimate=pl.CostEstimate(
            flops=likely_flops(2 * rows * weight.size), bytes_accessed=2 * weight.size, transcendentals=0
        ),
        name="near_added",
    )
    if depth >= width:
        wide = min(256, width)

        def by_columns(v, w, added, far, kept):
            total = mm_nt(v[...], w[...])
            far[...] = (total[tile:] + added[tile:, :].astype(F32)).astype(BF)
            kept[...] = total[:tile] + added[:tile, :].astype(F32)

        def columns(height):
            return pl.BlockSpec((height, wide), lambda j: (0, j))

        return pl.pallas_call(
            by_columns,
            grid=(width // wide,),
            in_specs=[
                pl.BlockSpec((rows, depth), lambda j: (0, 0), pipeline_mode=pl.Buffered(1)),
                pl.BlockSpec((wide, depth), lambda j: (j, 0)),
                columns(rows),
            ],
            out_specs=[columns(tile)] * 2,
            **settings,
        )(operand, weight, near)

    def by_rows(v, w, n, far, kept):
        step = pl.program_id(0)
        total = mm_nt(v[...], w[...]) + n[...].astype(F32)

        @pl.when(step == 0)
        def _():
            far[...] = total.astype(BF)

        @pl.when(step == 1)
        def _():
            kept[...] = total

    def rowed(v):
        return pl.BlockSpec((tile, v.shape[1]), lambda i: (1 - i, 0))

    fixed = pl.BlockSpec((tile, width), lambda i: (0, 0))
    return pl.pallas_call(
        by_rows,
        grid=(2,),
        in_specs=[
            rowed(operand),
            pl.BlockSpec(weight.shape, lambda i: (0, 0), pipeline_mode=pl.Buffered(1)),
            rowed(near),
        ],
        out_specs=[fixed, fixed],
        **settings,
    )(operand, weight, near)


def sigmoid(v):
    return 0.5 * jnp.tanh(0.5 * v) + 0.5


def gate_up_kernel(x, w, hidden, slope, act):
    units = hidden.shape[1]
    for n in range(0, units, 256):
        at = slice(n, min(n + 256, units))
        up_at = slice(units + n, units + min(n + 256, units))
        gate = jnp.dot(x[...], w[:, at], preferred_element_type=F32)
        up = jnp.dot(x[...], w[:, up_at], preferred_element_type=F32)
        s = sigmoid(gate)
        a = gate * s
        hidden[:, at] = (a * up).astype(BF)
        act[:, at] = a.astype(BF)
        slope[:, at] = (up * (s * (1.0 + gate * (1.0 - s)))).astype(BF)


def gate_up_back_kernel(c, w, slope, act, out):
    units = slope.shape[1]
    for n in range(0, units, 256):
        at = slice(n, min(n + 256, units))
        up_at = slice(units + n, units + min(n + 256, units))
        d = jnp.dot(c[...], w[:, at], preferred_element_type=F32)
        out[:, at] = (d * slope[:, at].astype(F32)).astype(BF)
        out[:, up_at] = (d * act[:, at].astype(F32)).astype(BF)


def d_gated_kernel(x, w, out):
    out[...] = jnp.dot(x[...], w[...], preferred_element_type=F32).astype(BF)


def pre_kernel(x, w, rate, act_in, act_gate, slope_in, slope_gate):
    channels = rate.shape[1]

    def silu(v):
        s = sigmoid(v)
        a = v * s
        return a, s + a * (1.0 - s)

    def product(k):
        return jnp.dot(
            x[...], w[:, k * channels : (k + 1) * channels], preferred_element_type=F32
        )

    act, slope = silu(product(0))
    act_in[...] = act
    slope_in[...] = slope.astype(BF)
    rate[...] = LOWER_BOUND + (1.0 - LOWER_BOUND) * sigmoid(product(1))
    act, slope = silu(product(2))
    act_gate[...] = act.astype(BF)
    slope_gate[...] = slope.astype(BF)


def row_tiles(kernel, parts, weight, others, outs, flops, name):
    count = len(parts)
    tile, depth = parts[0].shape

    def body(*refs):
        sources, w, rest = refs[:count], refs[count], refs[count + 1 : -2]
        buffer, arrived = refs[-2:]
        step = pl.program_id(0)

        def copy(p):
            return pltpu.make_async_copy(sources[p], buffer.at[p % 2], arrived.at[p % 2])

        @pl.when(step == 0)
        def _():
            copy(0).start()

        for p in range(count):

            @pl.when(step == p)
            def _(p=p):
                if p + 1 < count:
                    copy(p + 1).start()
                copy(p).wait()

        kernel(buffer.at[lax.rem(step, 2)], w, *rest)

    def spec(v):
        return pl.BlockSpec((tile, v.shape[1]), lambda i: (i, 0))

    return pl.pallas_call(
        body,
        grid=(count,),
        in_specs=[pl.BlockSpec(memory_space=pl.ANY)] * count
        + [pl.BlockSpec(weight.shape, lambda i: (0, 0), pipeline_mode=pl.Buffered(1))]
        + [spec(v) for v in others],
        out_specs=[spec(v) for v in outs],
        out_shape=outs,
        scratch_shapes=[pltpu.VMEM((2, tile, depth), BF), pltpu.SemaphoreType.DMA((2,))],
        compiler_params=pltpu.CompilerParams(vmem_limit_bytes=56 * 2**20),
        cost_estimate=pl.CostEstimate(
            flops=likely_flops(flops), bytes_accessed=weight.size * 4, transcendentals=0
        ),
        name=name,
    )(*parts, weight, *others)


def grad_kernel(lefts, rights, moving, wide, name, fixed=(0, 1), owner=None):
    part, parts = fixed
    part, span = part if isinstance(part, tuple) else (part, 1)
    mover, other = (lefts, rights) if moving == "left" else (rights, lefts)
    rows = sum(v.shape[0] for v in mover)
    steps = mover[0].shape[1] // wide
    held = other[0].shape[1] // parts * span
    begin = other[0].shape[1] // parts * part
    shape = (wide, held) if moving == "left" else (held, wide)
    half = steps // 2
    count, others = len(mover), len(other)

    def body(owners_ref, sources, write):
        movers, fixers = sources[:count], sources[count : count + others]
        moved, kept, arrived, ready = sources[-4:]
        step = pl.program_id(0)

        def copies(at, slot):
            column = at if owners_ref is None else owners_ref[lax.rem(at + half, steps)]
            columns = pl.ds(pl.multiple_of(column * wide, wide), wide)
            made, row = [], 0
            for p, source in enumerate(movers):
                size = source.shape[0]
                made.append(
                    pltpu.make_async_copy(
                        source.at[:, columns],
                        moved.at[slot, pl.ds(row, size), :],
                        arrived.at[slot, p],
                    )
                )
                row += size
            return made

        def fixed_copies():
            made, row = [], 0
            for p, source in enumerate(fixers):
                size = source.shape[0]
                made.append(
                    pltpu.make_async_copy(
                        source.at[:, pl.ds(begin, held)],
                        kept.at[pl.ds(row, size), :],
                        ready.at[p],
                    )
                )
                row += size
            return made

        @pl.when(step == 0)
        def _():
            for copy in copies(0, 0) + fixed_copies():
                copy.start()

        slot = lax.rem(step, 2)

        @pl.when(step + 1 < steps)
        def _():
            for copy in copies(step + 1, 1 - slot):
                copy.start()

        for copy in copies(step, slot):
            copy.wait()

        @pl.when(step == 0)
        def _():
            for copy in fixed_copies():
                copy.wait()

        pair = (moved[slot], kept[...]) if moving == "left" else (kept[...], moved[slot])
        total = lax.dot_general(
            *pair, (((0,), (0,)), ((), ())), preferred_element_type=F32
        ).astype(BF)
        write(step, total)

    settings = dict(
        compiler_params=pltpu.CompilerParams(vmem_limit_bytes=56 * 2**20),
        cost_estimate=pl.CostEstimate(
            flops=likely_flops(2 * steps * shape[0] * shape[1] * rows),
            bytes_accessed=2 * steps * shape[0] * shape[1],
            transcendentals=0,
        ),
        name=name,
    )
    in_specs = [pl.BlockSpec(memory_space=pl.ANY)] * (count + others)
    scratch = [
        pltpu.VMEM((2, rows, wide), BF),
        pltpu.VMEM((rows, held), BF),
        pltpu.SemaphoreType.DMA((2, count)),
        pltpu.SemaphoreType.DMA((others,)),
    ]
    if owner is None:

        def kernel(*refs):
            out = refs[count + others]

            def write(step, total):
                out[...] = total

            body(None, refs[: count + others] + refs[-4:], write)

        whole = (shape[0] * steps, shape[1]) if moving == "left" else (shape[0], shape[1] * steps)
        place = (lambda p: (p, 0)) if moving == "left" else (lambda p: (0, p))
        return pl.pallas_call(
            kernel,
            grid=(steps,),
            in_specs=in_specs,
            out_specs=pl.BlockSpec(shape, place),
            out_shape=jax.ShapeDtypeStruct(whole, BF),
            scratch_shapes=scratch,
            **settings,
        )(*mover, *other)

    def kernel_by_place(owners_ref, *refs):
        sent, kept = refs[count + others : count + others + 2]

        def write(step, total):
            @pl.when(step < half)
            def _():
                sent[0] = total

            @pl.when(step >= half)
            def _():
                kept[0] = total

        body(owners_ref, refs[: count + others] + refs[-4:], write)

    return pl.pallas_call(
        kernel_by_place,
        grid_spec=pltpu.PrefetchScalarGridSpec(
            num_scalar_prefetch=1,
            grid=(steps,),
            in_specs=in_specs,
            out_specs=[
                pl.BlockSpec((1,) + shape, lambda p, o: (jnp.minimum(p, half - 1), 0, 0)),
                pl.BlockSpec((1,) + shape, lambda p, o: (jnp.maximum(p - half, 0), 0, 0)),
            ],
            scratch_shapes=scratch,
        ),
        out_shape=[jax.ShapeDtypeStruct((half,) + shape, BF)] * 2,
        **settings,
    )(owner, *mover, *other)


def keep_of(row0, offsets):
    places = row0 + lax.broadcasted_iota(jnp.int32, (SUB, LANES), 0)
    start = places == offsets[0]
    for d in range(1, offsets.shape[0]):
        start = start | (places == offsets[d])
    return jnp.where(start, 0.0, 1.0).astype(F32)


def forward_kernel(order, offsets, free, act_in, act_gate, before, *rest):
    gated, carry = rest[:-1], rest[-1]
    block = pl.program_id(0)
    rows, channels = free.shape[1:]
    piece = rows // len(gated)

    @pl.when(block == 0)
    def _():
        carry[...] = jnp.zeros_like(carry)

    row_id = lax.broadcasted_iota(jnp.int32, (SUB, LANES), 0)

    def step(i, _, p):
        local = pl.multiple_of(i * 2 * SUB, 2 * SUB)
        base = pl.multiple_of(p * piece + i * 2 * SUB, 2 * SUB)
        keeps = [keep_of(block * rows + base + g * SUB, offsets) for g in range(2)]
        for c in range(channels // LANES):
            lanes = pl.ds(c * LANES, LANES)
            state = carry[:, lanes]
            gates = act_gate[0, pl.ds(base, 2 * SUB), lanes].astype(F32)
            outs = []
            for g in range(2):
                here = pl.ds(base + g * SUB, SUB)
                rate = keeps[g] * free[0, here, lanes]
                a, b = rate, (1.0 - rate) * act_in[0, here, lanes]
                for s in (1, 2, 4):
                    inside = row_id >= s
                    a_up = jnp.where(inside, pltpu.roll(a, s, 0), 1.0)
                    b_up = jnp.where(inside, pltpu.roll(b, s, 0), 0.0)
                    b = a * b_up + b
                    a = a * a_up
                whole = b + a * state
                before[0, here, lanes] = jnp.where(row_id == 0, state, pltpu.roll(whole, 1, 0))
                last_a = jnp.broadcast_to(a[SUB - 1 : SUB], (SUB, LANES))
                last_b = jnp.broadcast_to(b[SUB - 1 : SUB], (SUB, LANES))
                state = last_b + last_a * state
                outs.append(whole * gates[g * SUB : (g + 1) * SUB])
            carry[:, lanes] = state
            gated[p][0, pl.ds(local, 2 * SUB), lanes] = jnp.concatenate(outs, axis=0).astype(BF)
        return 0

    for p in range(len(gated)):
        lax.fori_loop(0, piece // (2 * SUB), functools.partial(step, p=p), 0)


def backward_kernel(
    order, offsets, free, act_in, act_gate, slope_in, slope_gate, before, *rest
):
    pieces = (len(rest) - 1) // 2
    dgated, dpieces, carry = rest[:pieces], rest[pieces : 2 * pieces], rest[-1]
    step_id = pl.program_id(0)
    block = pl.num_programs(0) - 1 - step_id
    rows, channels = free.shape[1:]
    piece = rows // pieces
    groups = piece // (2 * SUB)

    @pl.when(step_id == 0)
    def _():
        carry[...] = jnp.zeros_like(carry)

    row_id = lax.broadcasted_iota(jnp.int32, (SUB, LANES), 0)

    def step(i, _, p):
        local = pl.multiple_of((groups - 1 - i) * 2 * SUB, 2 * SUB)
        base = pl.multiple_of(p * piece + (groups - 1 - i) * 2 * SUB, 2 * SUB)
        keeps = [keep_of(block * rows + base + g * SUB, offsets) for g in range(2)]
        for c in range(channels // LANES):
            lanes = pl.ds(c * LANES, LANES)
            both = pl.ds(base, 2 * SUB)
            flow = carry[:, lanes]
            halves = [
                v.astype(F32)
                for v in (
                    act_gate[0, both, lanes],
                    slope_in[0, both, lanes],
                    slope_gate[0, both, lanes],
                    dgated[p][0, pl.ds(local, 2 * SUB), lanes],
                )
            ]
            outs = [None, None]
            for g in (1, 0):
                here = pl.ds(base + g * SUB, SUB)
                gate, in_slope, gate_slope, dg = [v[g * SUB : (g + 1) * SUB] for v in halves]
                open_rate, act, prev = free[0, here, lanes], act_in[0, here, lanes], before[0, here, lanes]
                keep = keeps[g]
                rate = keep * open_rate
                rest_in = 1.0 - rate
                state = rate * prev + rest_in * act
                x = dg * gate
                a, b = rate, rate * x
                for s in (1, 2, 4):
                    inside = row_id < SUB - s
                    a_down = jnp.where(inside, pltpu.roll(a, SUB - s, 0), 1.0)
                    b_down = jnp.where(inside, pltpu.roll(b, SUB - s, 0), 0.0)
                    b = a * b_down + b
                    a = a * a_down
                q = b + a * flow
                carried = x + jnp.where(row_id == SUB - 1, flow, pltpu.roll(q, SUB - 1, 0))
                first_a = jnp.broadcast_to(a[0:1], (SUB, LANES))
                first_b = jnp.broadcast_to(b[0:1], (SUB, LANES))
                flow = first_b + first_a * flow
                d_in = carried * rest_in * in_slope
                d_forget = (
                    carried
                    * (prev - act)
                    * keep
                    * ((open_rate - LOWER_BOUND) * (1.0 - open_rate) * (1.0 / (1.0 - LOWER_BOUND)))
                )
                d_gate = dg * state * gate_slope
                outs[g] = (d_in, d_forget, d_gate)
            carry[:, lanes] = flow
            for k in range(3):
                value = jnp.concatenate([outs[0][k], outs[1][k]], axis=0).astype(BF)
                at = pl.ds(k * channels + c * LANES, LANES)
                dpieces[p][0, pl.ds(local, 2 * SUB), at] = value
        return 0

    for p in reversed(range(pieces)):
        lax.fori_loop(0, groups, functools.partial(step, p=p), 0)


def recurrence_call(kernel, order, offsets, operands, outs, channels, name):
    blocks, rows = operands[0].shape[:2]

    def spec(v):
        return pl.BlockSpec((1,) + v.shape[1:], lambda a, o, f: (o[a], 0, 0))

    return pl.pallas_call(
        kernel,
        grid_spec=pltpu.PrefetchScalarGridSpec(
            num_scalar_prefetch=2,
            grid=(blocks,),
            in_specs=[spec(v) for v in operands],
            out_specs=[spec(v) for v in outs],
            scratch_shapes=[pltpu.VMEM((SUB, channels), F32)],
        ),
        out_shape=outs,
        compiler_params=pltpu.CompilerParams(vmem_limit_bytes=48 * 2**20),
        cost_estimate=pl.CostEstimate(
            flops=blocks * rows * channels * 15000,
            bytes_accessed=blocks * rows * channels * 4 * 6,
            transcendentals=blocks * rows * channels * 3,
        ),
        name=name,
    )(order, offsets, *operands)


def unit(values):
    scaling = lax.rsqrt(jnp.mean(values * values, axis=-1, keepdims=True) + RMS_EPSILON)
    return values * scaling, scaling


def norm_backward(d_normed, unit_rows, scaling, gain):
    d_unit = d_normed * gain
    d_values = scaling * (d_unit - unit_rows * jnp.mean(d_unit * unit_rows, axis=-1, keepdims=True))
    return d_values, jnp.sum(d_normed * unit_rows, axis=0)


def adam_moments(grad, weight, first, second, decay_rate):
    first_next = BETA_ONE * first + (1.0 - BETA_ONE) * grad
    second_next = BETA_TWO * second + (1.0 - BETA_TWO) * grad * grad
    update = (
        first_next
        / (1.0 - BETA_ONE**STEP)
        / (jnp.sqrt(second_next / (1.0 - BETA_TWO**STEP)) + ADAM_EPSILON)
        + decay_rate * weight
    )
    return (first_next, second_next, update)


def total_over_mesh(values, n_dp, n_tensor):
    for axis, size, offsets in (
        ("tensor", n_tensor, (1, 2)),
        ("tensor", n_tensor, (4, 8)),
        ("dp", n_dp, (1,)),
        ("dp", n_dp, (2, 4)),
        ("dp", n_dp, (8,)),
    ):
        offsets = [o for o in offsets if o < size]
        if len(offsets) == 2:
            one, two = offsets
            parts = [exchange(values, axis, size, o) for o in (one, two, one + two)]
            values = (values + parts[0]) + (parts[1] + parts[2])
        elif offsets:
            values = values + exchange(values, axis, size, offsets[0])
    return values


def new_weights(steps, weights, updates):
    tiles = weights[3].shape[0] // 352
    counts = [v.shape[0] if v.ndim == 3 else 0 for v in weights]

    def kernel(factor, *refs):
        olds, changes, news, copies = refs[:4], refs[4:11], refs[11:15], refs[15:]
        n = 0
        for old, new, copy, count in zip(olds, news, copies, counts):
            for k in range(max(count, 1)):
                at = (k,) if count else Ellipsis
                value = old[at] - factor[n] * changes[n][...]
                new[at] = value
                copy[at] = value.astype(BF)
                n += 1

    def spec(v):
        if v.ndim == 3:
            return pl.BlockSpec((v.shape[0], v.shape[1] // tiles, v.shape[2]), lambda i, f: (0, i, 0))
        return pl.BlockSpec((v.shape[0] // tiles, v.shape[1]), lambda i, f: (i, 0))

    outs = pl.pallas_call(
        kernel,
        grid_spec=pltpu.PrefetchScalarGridSpec(
            num_scalar_prefetch=1,
            grid=(tiles,),
            in_specs=[spec(v) for v in weights] + [spec(v) for v in updates],
            out_specs=[spec(v) for v in weights] * 2,
        ),
        out_shape=[jax.ShapeDtypeStruct(v.shape, F32) for v in weights]
        + [jax.ShapeDtypeStruct(v.shape, BF) for v in weights],
        compiler_params=pltpu.CompilerParams(vmem_limit_bytes=60 * 2**20),
        name="new_weights",
    )(steps, *weights, *updates)
    return outs[:4], outs[4:]


def per_device(
    n_dp,
    n_tensor,
    tokens,
    cotangent,
    doc_lengths,
    mix_in,
    mix_out,
    ffn_in,
    ffn_out,
    gains,
    mix_in_m,
    mix_out_m,
    ffn_in_m,
    ffn_out_m,
    gains_m,
    mix_in_v,
    mix_out_v,
    ffn_in_v,
    ffn_out_v,
    gains_v,
):
    rows, width = tokens.shape
    depth = mix_in.shape[1]
    channels = mix_in.shape[2]
    hidden_units = ffn_in.shape[2]
    units = -(-hidden_units // LANES) * LANES
    piece = rows // CHUNKS
    pieces = range(CHUNKS)
    dp_id = lax.axis_index("dp")
    tensor_id = lax.axis_index("tensor")
    near_first = halving(n_dp)
    owner = owners(dp_id, near_first)
    row_places = offsets_by_place(halving(n_tensor))
    place_of = jnp.array([row_places.index(o) for o in range(n_tensor)], jnp.int32)
    order = place_of[jnp.arange(n_tensor) ^ tensor_id]
    offsets = (jnp.cumsum(doc_lengths[0]) - doc_lengths[0]).astype(jnp.int32)
    q = Sequence()
    run = q.run

    def cut(i):
        return slice(i * piece, (i + 1) * piece)

    def padded(v):
        return jnp.pad(v, ((0, 0), (0, units - hidden_units)))

    weights = [mix_in[0], mix_in[1], mix_in[2], mix_out, ffn_in[0], ffn_in[1], ffn_out]

    own_mix_in = jnp.concatenate([mix_in[k] for k in range(3)], axis=1).astype(BF)
    own_mix_in, own_tokens = lax.optimization_barrier((own_mix_in, tokens))
    halves, scales_one = [], []
    for i in range(2):
        half = own_tokens[i * (rows // 2) : (i + 1) * (rows // 2)]
        unit_i, scale_i = unit(half.astype(F32))
        halves.append((unit_i * gains[0]).astype(BF))
        scales_one.append(scale_i)
    scale_one = jnp.concatenate(scales_one, axis=0)
    far_offsets = offsets_by_place(near_first)[1 : n_dp // 2]
    early = sorted(far_offsets, key=lambda o: (o & near_first[1] == 0, o))
    early, late = early[: len(early) // 2 + 1], early[len(early) // 2 + 1 :]
    all_offsets = [0] + far_offsets
    owner_far = [dp_id ^ j for j in all_offsets]
    owner_near = [dp_id ^ j ^ 1 for j in all_offsets]

    def distant(half):
        held, offset = [half], n_tensor // 2
        while offset > 1:
            held = held + [exchange(part, "tensor", n_tensor, offset) for part in held]
            offset //= 2
        return held

    far = {j: exchange(own_mix_in, "dp", n_dp, j) for j in early}
    near = {0: exchange(own_mix_in, "dp", n_dp, 1)}
    far_a = distant(halves[0])
    first = lax.optimization_barrier((far_a, near, far, own_mix_in, halves[1]))
    far_a, near, far, own_mix_in, own_b = first
    own_ffn_in = jnp.concatenate([padded(ffn_in[k].astype(BF)) for k in range(2)], axis=1)
    far.update({j: exchange(own_mix_in, "dp", n_dp, j) for j in late})
    near.update({j: exchange(far[j], "dp", n_dp, 1) for j in early})
    far_b = distant(own_b)
    near_a = [exchange(far_a[0], "tensor", n_tensor, 1)]
    near_b = [exchange(after(own_b, near_a[0]), "tensor", n_tensor, 1)]
    second = lax.optimization_barrier(
        (far_a, far_b, near, far, own_ffn_in, near_a, near_b, mix_out.astype(BF).T, own_mix_in)
    )
    far_a, far_b, near, far, own_ffn_in, near_a, near_b, own_mix_out, own_mix_in = second
    near.update({j: exchange(far[j], "dp", n_dp, 1) for j in late})
    near_a += [exchange(part, "tensor", n_tensor, 1) for part in far_a[1:]]
    near_b += [exchange(after(part, near_a[-1]), "tensor", n_tensor, 1) for part in far_b[1:]]
    known = [(dp_id, own_mix_in)] + [(dp_id ^ j, far[j]) for j in far_offsets]
    known += [(dp_id ^ j ^ 1, near[j]) for j in [0] + early]
    w_mix_in = jnp.zeros((width, 3 * channels), BF)
    for place, block in known:
        w_mix_in = lax.dynamic_update_slice(w_mix_in, block, (place * depth, 0))
    far_mo = [own_mix_out] + [exchange(own_mix_out, "dp", n_dp, j) for j in far_offsets]
    third = lax.optimization_barrier(
        (near_a, near_b, w_mix_in, own_ffn_in, [near[j] for j in late], far_mo, cotangent)
    )
    near_a, near_b, w_mix_in, own_ffn_in, last, far_mo, cot_all = third
    q.last = near_b[0]

    def far_rows(own):
        return distant(own)[1:]

    def to_core(parts):
        return [exchange(part, "tensor", n_tensor, 1) for part in parts]

    def to_far(rows_sent):
        return exchange(rows_sent, "tensor", n_tensor, 2)

    def landed(kept, coming):
        places, offset = n_tensor // 4, 2
        while places > 1:
            total = kept + coming.astype(F32)
            offset, places = 2 * offset, places // 2
            kept = total[: places * piece]
            coming = exchange(total[places * piece :].astype(BF), "tensor", n_tensor, offset)
        return kept, coming

    def upper(operand, weight):
        half = operand.shape[0] // 2
        return run(lambda v, w: mm_nt(v[half:], w).astype(BF), operand, weight)

    def lower(operand, weight, near):
        return run(near_added, operand, weight, near)

    def add_halves(kept, coming):
        return run(halves_added, kept, coming)

    w_ffn_in = lax.all_gather(own_ffn_in, "dp", axis=0, tiled=True)
    cot_own = [cot_all[cut(i)] for i in pieces]
    cot_far = far_rows(cot_own[0])
    near_mo = exchange(jnp.concatenate(far_mo, axis=0), "dp", n_dp, 1)
    for j, block in zip(late, last):
        w_mix_in = lax.dynamic_update_slice(w_mix_in, block, ((dp_id ^ j ^ 1) * depth, 0))
    whole_one = [v for pair in zip(far_a + near_a, far_b + near_b) for v in pair]
    tall = n_tensor * rows
    pre = run(
        lambda w, *parts: row_tiles(
            pre_kernel,
            parts,
            w,
            [],
            [jax.ShapeDtypeStruct((tall, channels), t) for t in (F32, F32, BF, BF, BF)],
            2 * tall * width * 3 * channels,
            "pre",
        ),
        w_mix_in,
        *whole_one,
    )
    q.close(pre=[v.reshape(n_tensor, rows, channels) for v in pre], cot0=cot_far)

    cot0_near = to_core([cot_own[0]] + q.cot0)
    scanned = recurrence_call(
        forward_kernel,
        order,
        offsets,
        q.pre[:3],
        [jax.ShapeDtypeStruct((n_tensor, rows, channels), F32)]
        + [jax.ShapeDtypeStruct((n_tensor, piece, channels), BF)] * CHUNKS,
        channels,
        "recurrence_forward",
    )
    q.last = scanned[0]
    mo_blocks = far_mo + [near_mo[p * depth : (p + 1) * depth] for p in range(len(far_mo))]
    w_mix_out = run(lambda *blocks: spread(blocks, owner_far + owner_near), *mo_blocks)
    gated = [v.reshape(-1, channels) for v in scanned[1:]]
    q.close(
        up0=upper(gated[0], w_mix_out),
        w_mo=w_mix_out,
        gated=gated,
        before=scanned[0],
        cot0_near=cot0_near,
    )
    cot_parts = [[cot_own[0]] + q.cot0 + q.cot0_near]

    (near0,) = to_core([q.up0])
    q.close(up1=upper(q.gated[1], q.w_mo), near0=near0)

    (near1,) = to_core([q.up1])
    far0, kept0 = lower(q.gated[0], q.w_mo, q.near0)
    q.close(far0=far0, kept0=kept0, near1=near1)

    coming0 = to_far(q.far0)
    far1, kept1 = lower(q.gated[1], q.w_mo, q.near1)
    q.close(far1=far1, kept1=kept1, coming0=coming0)

    coming1 = to_far(q.far1)

    def middle_of(kept, coming, own):
        middle = own.astype(F32) + kept + coming.astype(F32)
        unit_rows, scaling = unit(middle)
        return (unit_rows * gains[1]).astype(BF), middle, scaling

    normed0, middle0, scale0 = run(middle_of, *landed(q.kept0, q.coming0), tokens[cut(0)])
    q.close(coming1=coming1, normed0=normed0, middle0=middle0, scale0=scale0)
    normed_far = far_rows(q.normed0)
    normed_near = to_core([q.normed0])
    normed1, middle1, scale1 = run(middle_of, *landed(q.kept1, q.coming1), tokens[cut(1)])
    weight_sq = run(lambda *ws: jnp.stack([jnp.sum(w * w) for w in ws]), *weights)
    q.close(w_ffn_in=w_ffn_in, weight_sq=weight_sq)
    w_ffn_out = lax.all_gather(
        after(padded(ffn_out.astype(BF).T), q.w_ffn_in), "dp", axis=0, tiled=True
    )
    q.close(
        normed1=normed1, middle1=middle1, scale1=scale1, normed0_far=normed_far, normed0_near=normed_near
    )
    weight_sq = q.weight_sq
    middle, scale_two = [q.middle0, q.middle1], [q.scale0, q.scale1]

    many = n_tensor * piece
    flops = 2 * many * width * units
    one = jax.ShapeDtypeStruct((many, units), BF)

    def gate_up(parts):
        return run(
            lambda w, *parts: row_tiles(
                gate_up_kernel, parts, w, [], [one] * 3, 2 * flops, "gate_up"
            ),
            q.w_ffn_in,
            *parts,
        )

    normed_far = far_rows(q.normed1)
    normed_near = to_core([q.normed1])
    whole_two = [q.normed0] + q.normed0_far + q.normed0_near + to_core(q.normed0_far)
    out0 = gate_up(whole_two)
    q.close(out0=out0, normed1_far=normed_far, normed1_near=normed_near, cot_own1=cot_own[1])
    cot_far = far_rows(q.cot_own1)
    parts1 = [q.normed1] + q.normed1_far + q.normed1_near + to_core(q.normed1_far)
    out1 = gate_up(parts1)
    whole_two = whole_two + parts1
    q.close(out1=out1, cot1=cot_far)
    hidden = [q.out0[0], q.out1[0]]
    cot1 = [q.cot_own1] + q.cot1
    cot_parts.append(cot1 + to_core(cot1))

    def grad(lefts, rights, *settings, **more):
        def call(*values):
            return grad_kernel(values[: len(lefts)], values[len(lefts) :], *settings, **more)

        return run(call, *lefts, *rights)

    wide = min(256, depth)

    def gate_up_back(i):
        out = (q.out0, q.out1)[i]
        (d,) = run(
            lambda w, v, a, *parts: row_tiles(
                gate_up_back_kernel,
                parts,
                w,
                [v, a],
                [jax.ShapeDtypeStruct((many, 2 * units), BF)],
                flops,
                "gate_up_back",
            ),
            w_ffn_out,
            out[1],
            out[2],
            *cot_parts[i],
        )
        return d

    grad_fo = grad(hidden, cot_parts[0] + cot_parts[1], "right", wide, "grad_out")
    q.close(grad_fo=grad_fo)

    sum_fo = lax.psum_scatter(q.grad_fo, "dp", scatter_dimension=1, tiled=True)
    d0 = gate_up_back(0)
    q.close(up0=upper(d0, q.w_ffn_in), d0=d0)

    (near0,) = to_core([q.up0])
    d1 = gate_up_back(1)
    up1 = upper(d1, q.w_ffn_in)
    far0, kept0 = lower(q.d0, q.w_ffn_in, near0)
    q.close(far0=far0, kept0=kept0, up1=up1, d1=d1, w_ffn_out=w_ffn_out)

    coming0 = to_far(q.far0)
    (near1,) = to_core([q.up1])
    down0 = upper(hidden[0], q.w_ffn_out)
    down1 = upper(hidden[1], q.w_ffn_out)
    far1, kept1 = lower(q.d1, q.w_ffn_in, near1)
    q.close(far1=far1, kept1=kept1, coming0=coming0, down0=down0, down1=down1)

    def middle_back(kept, coming, mid, scaling, cot):
        unit_rows = mid * scaling
        d_norm, gain = norm_backward(kept + coming.astype(F32), unit_rows, scaling, gains[1])
        d_mid = cot.astype(F32) + d_norm
        return d_mid.astype(BF), d_mid, gain

    def grad_in(part):
        return grad(whole_two, [q.d0, q.d1], "left", wide, "grad_in", fixed=(part, 2))

    def sum_in(value):
        return lax.psum_scatter(value, "dp", scatter_dimension=0, tiled=True)

    coming1 = to_far(q.far1)
    down_near = to_core([q.down0, q.down1])
    back0 = run(
        middle_back, *landed(q.kept0, q.coming0), middle[0], scale_two[0], cotangent[cut(0)]
    )
    grad_fg = grad_in(0)
    q.close(
        coming1=coming1, back0=back0, grad_fg=grad_fg, down_near=down_near, sum_fo=sum_fo
    )

    low_far = far_rows(q.back0[0])
    sum_fg = sum_in(q.grad_fg)
    back1 = run(
        middle_back, *landed(q.kept1, q.coming1), middle[1], scale_two[1], cotangent[cut(1)]
    )
    grad_fu = grad_in(1)
    q.close(back1=back1, grad_fu=grad_fu, low0_far=low_far)

    def d_gated_of(parts):
        (d,) = run(
            lambda w, *parts: row_tiles(
                d_gated_kernel,
                parts,
                w,
                [],
                [jax.ShapeDtypeStruct((many, channels), BF)],
                2 * many * width * channels,
                "d_gated",
            ),
            q.w_mo,
            *parts,
        )
        return d.reshape(n_tensor, piece, channels)

    low_far = far_rows(q.back1[0])
    low0 = [q.back0[0]] + q.low0_far
    whole_d0 = low0 + to_core(low0)
    low1_near = to_core([q.back1[0]])
    down_far0, down_kept0 = lower(hidden[0], q.w_ffn_out, q.down_near[0])
    down_far1, down_kept1 = lower(hidden[1], q.w_ffn_out, q.down_near[1])
    d_gated0 = d_gated_of(whole_d0)
    q.close(
        d_gated0=d_gated0,
        low1_far=low_far,
        low1_near=low1_near,
        whole_d0=whole_d0,
        down_far=[down_far0, down_far1],
        down_kept=[down_kept0, down_kept1],
    )

    down_coming = [to_far(q.down_far[0]), to_far(q.down_far[1])]

    whole_d1 = [q.back1[0]] + q.low1_far + q.low1_near + to_core(q.low1_far)
    d_gated1 = d_gated_of(whole_d1)
    scanned = recurrence_call(
        backward_kernel,
        order[::-1],
        offsets,
        q.pre + [q.before, q.d_gated0, d_gated1],
        [jax.ShapeDtypeStruct((n_tensor, piece, 3 * channels), BF)] * CHUNKS,
        channels,
        "recurrence_backward",
    )
    q.last = scanned[-1]
    q.close(scanned=scanned, whole_d1=whole_d1, sum_fg=sum_fg, grad_fu=q.grad_fu)
    d_pieces = [v.reshape(-1, 3 * channels) for v in q.scanned]
    whole_one = far_a + near_a + far_b + near_b

    def grad_mix_in(k):
        return grad(
            whole_one, d_pieces, "left", depth, "grad_mix_in", fixed=(k, 3), owner=owner
        )

    def over_y(halves):
        return exchange(halves[0], "dp", n_dp, 1)

    def over_z(halves, offset):
        return exchange(halves[0], "dp", n_dp, offset)

    def finished(kept, coming, offset):
        while kept.shape[0] > 1:
            sent, kept = halves_added(kept, coming)
            offset *= 2
            coming = exchange(sent, "dp", n_dp, offset)
        return kept, coming

    sum_fu = sum_in(q.grad_fu)
    grad0 = grad_mix_in(0)
    q.close(grad0=grad0)

    y0 = over_y(q.grad0)
    up0 = upper(d_pieces[0], w_mix_in)
    grad1 = grad_mix_in(1)
    up1 = upper(d_pieces[1], w_mix_in)
    q.close(grad1=grad1, up0=up0, up1=up1, y0=y0, down_coming=down_coming)

    half0 = add_halves(q.grad0[1], q.y0)
    y1 = over_y(q.grad1)
    z0 = over_z(half0, 2)
    near0, near1 = to_core([q.up0, q.up1])
    grad2 = grad_mix_in(2)
    far0, kept0 = lower(d_pieces[0], w_mix_in, near0)
    q.close(
        grad2=grad2,
        near1=near1,
        y1=y1,
        z0=z0,
        kept_y0=half0[1],
        far0=far0,
        kept0=kept0,
    )

    y2 = over_y(q.grad2)
    half1 = add_halves(q.grad1[1], q.y1)
    z1 = over_z(half1, 2)
    half0 = add_halves(q.kept_y0, q.z0)
    w0 = over_z(half0, 4)
    coming0 = to_far(q.far0)
    grad3 = grad(
        q.gated, q.whole_d0 + q.whole_d1, "right", depth, "grad_mix_out", owner=owner
    )
    far1, kept1 = lower(d_pieces[1], w_mix_in, q.near1)
    q.close(
        far1=far1,
        kept1=kept1,
        sum_fu=sum_fu,
        coming0=coming0,
        grad3=grad3,
        y2=y2,
        z1=z1,
        w0=w0,
        kept_y1=half1[1],
        kept_z0=half0[1],
    )

    firsts = [mix_in_m[0], mix_in_m[1], mix_in_m[2], mix_out_m, ffn_in_m[0], ffn_in_m[1], ffn_out_m]
    seconds = [mix_in_v[0], mix_in_v[1], mix_in_v[2], mix_out_v, ffn_in_v[0], ffn_in_v[1], ffn_out_v]
    moments = [None] * 7

    def lamb(at, kept, coming=None):
        tall, wide = weights[at].shape
        if coming is not None:
            kept, coming = finished(kept, coming, 4)

        def call(kept, *coming):
            if coming:
                total = kept[0].astype(F32) + coming[0][0].astype(F32)
            else:
                total = kept.astype(F32)
            first, second, update = adam_moments(
                total[:tall, :wide], weights[at], firsts[at], seconds[at], WEIGHT_DECAY
            )
            return update, first, second, jnp.sum(update * update)

        update, first, second, square = run(call, kept, *([] if coming is None else [coming]))
        moments[at] = (first, second, update, square)

    def input_back(kept, coming, own, scaling, d_mid):
        unit_rows = own.astype(F32) * scaling
        d_norm, gain = norm_backward(kept + coming.astype(F32), unit_rows, scaling, gains[0])
        return d_mid + d_norm, gain

    coming1 = to_far(q.far1)
    half2 = add_halves(q.grad2[1], q.y2)
    y3 = over_y(q.grad3)
    z2 = over_z(half2, 2)
    half1 = add_halves(q.kept_y1, q.z1)
    w1 = over_z(half1, 4)
    input_grad0, gain_one0 = run(
        input_back,
        *landed(q.kept0, q.coming0),
        tokens[cut(0)],
        scale_one[cut(0)],
        q.back0[1],
    )
    lamb(0, q.kept_z0, q.w0)
    lamb(6, q.sum_fo)
    mixed = run(
        lambda *parts: jnp.concatenate(
            [
                m + k + c.astype(F32)
                for m, k, c in zip(parts[:CHUNKS], parts[CHUNKS : 2 * CHUNKS], parts[2 * CHUNKS :])
            ],
            axis=0,
        ).astype(BF),
        *middle,
        *[
            v
            for pair in zip(
                *[
                    landed(k, c)
                    for k, c in zip(q.down_kept, q.down_coming)
                ]
            )
            for v in pair
        ],
    )
    q.close(
        coming1=coming1,
        y3=y3,
        z2=z2,
        kept_y2=half2[1],
        w1=w1,
        kept_z1=half1[1],
    )

    half3 = add_halves(q.grad3[1], q.y3)
    z3 = over_z(half3, 2)
    half2 = add_halves(q.kept_y2, q.z2)
    w2 = over_z(half2, 4)
    input_grad1, gain_one1 = run(
        input_back,
        *landed(q.kept1, q.coming1),
        tokens[cut(1)],
        scale_one[cut(1)],
        q.back1[1],
    )
    lamb(1, q.kept_z1, q.w1)
    q.close(z3=z3, kept_y3=half3[1], w2=w2, kept_z2=half2[1])

    half3 = add_halves(q.kept_y3, q.z3)
    w3 = over_z(half3, 4)
    lamb(4, q.sum_fg)
    lamb(5, q.sum_fu)
    lamb(2, q.kept_z2, q.w2)
    squares = [weight_sq[i] for i in range(7)] + [m[3] if m else jnp.zeros((), F32) for m in moments]
    packed = run(
        lambda one, *others: jnp.stack(
            [one + others[0], others[1] + others[2], jnp.pad(jnp.stack(others[3:]), (0, width - 14))]
        ),
        gain_one0,
        gain_one1,
        q.back0[2],
        q.back1[2],
        *squares,
    )
    q.close(packed=packed, w3=w3, kept_z3=half3[1])
    lamb(3, q.kept_z3, q.w3)
    input_grad = jnp.concatenate([input_grad0, input_grad1], axis=0)
    place = lax.broadcasted_iota(jnp.int32, (3, width), 1)
    last_row = lax.broadcasted_iota(jnp.int32, (3, width), 0) == 2
    packed = q.packed + jnp.where(last_row & (place == 10), moments[3][3], 0.0)
    packed = total_over_mesh(packed, n_dp, n_tensor)
    gain_grads = packed[:2]
    squares = packed[2, :14].reshape(2, 7)
    gn_first, gn_second, gn_update = adam_moments(gain_grads, gains, gains_m, gains_v, 0.0)
    weight_sq = jnp.concatenate([squares[0], jnp.sum(gains * gains, axis=1)])
    update_sq = jnp.concatenate([squares[1], jnp.sum(gn_update * gn_update, axis=1)])
    trust = jnp.sqrt(weight_sq) / jnp.sqrt(update_sq + NORM_EPSILON)
    nexts, copies = new_weights(
        LEARN_RATE * trust[0:7], (mix_in, mix_out, ffn_in, ffn_out), [m[2] for m in moments]
    )
    gains_next = gains - LEARN_RATE * trust[7:9][:, None] * gn_update
    layer_norms = jnp.stack([jnp.sqrt(weight_sq), jnp.sqrt(update_sq)])

    def grouped(values):
        return (jnp.stack(values[0:3]), values[3], jnp.stack(values[4:6]), values[6])

    return (
        (mixed, input_grad)
        + tuple(nexts)
        + (gains_next,)
        + grouped([m[0] for m in moments])
        + (gn_first,)
        + grouped([m[1] for m in moments])
        + (gn_second,)
        + tuple(copies)
        + (layer_norms,)
    )


def solution(mesh):
    rows = P(("dp", "tensor"), None)
    inner = P(None, "dp", "tensor")
    outer = P("tensor", "dp")
    matrices = (inner, outer, inner, outer)
    in_specs = (rows, rows, P("dp", None)) + (matrices + (P(),)) * 3
    out_specs = (rows, rows) + (matrices + (P(),)) * 3 + matrices + (P(),)
    body = functools.partial(per_device, mesh.shape["dp"], mesh.shape["tensor"])
    return jax.shard_map(
        body, mesh=mesh, in_specs=in_specs, out_specs=out_specs, check_vma=False
    )
```
